32 devices in a mesh: seq: 2 (over x), dp: 16 (over z, y, core).
Axes of the slice: x: 2, y: 2, z: 4, core: 2. Of those that a mesh axis runs over, the one named last changes fastest.
Arguments:
- queries: bfloat16 [16, 256, 2048], P('dp', 'seq'), may hold values from -6 to 6
- key_rows: bfloat16 [16, 256, 256], P('dp', 'seq'), may hold values from -6 to 6
- value_matrix: bfloat16 [16, 256, 256], P('dp', 'seq'), may hold values from -6 to 6
- head_sink_logits: float32 [32], replicated, may hold values from 2 to 6
- residual: bfloat16 [16, 256, 2880], P('dp', 'seq'), may hold values from -6 to 6
- out_weight: bfloat16 [2048, 2880], P('dp'), may hold values from -0.125 to 0.125
- norm_gain: float32 [2880], replicated, may hold values from 0.25 to 1.75
- router: bfloat16 [2880, 128], replicated, may hold values from -0.109375 to 0.109375
- expert_gate: bfloat16 [2880, 4096], P('dp', 'seq'), may hold values from -0.109375 to 0.109375
- expert_up: bfloat16 [2880, 4096], P('dp', 'seq'), may hold values from -0.109375 to 0.109375
- expert_down: bfloat16 [2880, 4096], P('dp', 'seq'), may hold values from -0.125 to 0.125
- routes: int32 [16, 256, 4], P('dp', 'seq'), may hold values from 0 to 127, as said below
- group_ids: int32 [16], P('dp'), may hold values from 0 to 3, never falling along the last dimension, each value on 1 to 8 neighbouring positions
- rewards: int32 [16], P('dp'), may hold values from 0 to 3
- response_mask: int32 [16, 256], P('dp', 'seq'), may hold values from 0 to 1, as said below
- upstream: bfloat16 [16, 256, 2880], P('dp', 'seq'), may hold values from -6 to 6
Outputs:
- grad_queries: bfloat16 [16, 256, 2048], P('dp', 'seq')
- grad_keys: bfloat16 [16, 256, 256], P('dp', 'seq')
- grad_values: bfloat16 [16, 256, 256], P('dp', 'seq')
- grad_residual: bfloat16 [16, 256, 2880], P('dp', 'seq')
- grad_sinks: float32 [32], replicated
The draws below stay inside these ranges and needn't reach their ends.
Inputs may be any that keep to these rules, and one draw needn't show every extreme that they name: `routes`: each token names 4 different experts. Among the 128 positions of every aligned block of a rollout at most 4 tokens name a given expert below 2; the first block of the first rollout has exactly 4 for each of them. `group_ids`: the rollouts of one group are adjacent and every group has 1 to 8 rollouts. `response_mask`: in each rollout the ones form one run that starts within the first quarter of the positions and ends within the last quarter.
All inputs are finite; a program needn't handle non-finite values.
Results may differ from the reference program's by a relative error of at most 0.0095.
Values may be sent and summed in bfloat16 or wider, within the bound.
A program may use at most 128 MiB of HBM per device.

```python
import math
from functools import partial
import jax
import jax.numpy as jnp
import numpy as np
from jax import lax

D = 2880
HEAD_SIZE = 64
WINDOW = 128
EXPERTS = 128
TOPK = 4
QUERY_HEADS = 32
KEY_VALUE_HEADS = 4
HID = 2048
EW = 2
CAP = 4
TOK_DEV = 128
ROLLOUT_LENGTH = 256
ROLLOUT_COUNT = 16
NTOK = 4096
PIECES = 1
HID_DEV = 2048
GROUPS = 4
GROUP_MOST = 8


def paired_fields(key):
    base = jax.random.fold_in(key, 5)
    query_random_seed, keys_random_seed = jax.random.split(base, 2)
    sampled_query = jnp.clip(jax.random.normal(query_random_seed, (ROLLOUT_COUNT, ROLLOUT_LENGTH, KEY_VALUE_HEADS, QUERY_HEADS // KEY_VALUE_HEADS, HEAD_SIZE), jnp.float32), -6.0, 6.0)
    sampled_keys = jnp.clip(jax.random.normal(keys_random_seed, (ROLLOUT_COUNT, ROLLOUT_LENGTH, KEY_VALUE_HEADS, HEAD_SIZE), jnp.float32), -6.0, 6.0)
    return (sampled_query.reshape(ROLLOUT_COUNT, ROLLOUT_LENGTH, QUERY_HEADS * HEAD_SIZE), sampled_keys.reshape(ROLLOUT_COUNT, ROLLOUT_LENGTH, KEY_VALUE_HEADS * HEAD_SIZE))


def draw_queries(key, part):
    return paired_fields(key)[0].astype(jnp.bfloat16)


def draw_key_rows(key, part):
    return paired_fields(key)[1].astype(jnp.bfloat16)


def draw_routes(key, part):
    base = jax.random.fold_in(key, 11)
    full_key, light_key, order_key, other_key = jax.random.split(base, 4)
    blocks = ROLLOUT_COUNT * (ROLLOUT_LENGTH // TOK_DEV)
    filled = jax.random.randint(full_key, (blocks, EW), 0, 4) == 0
    lighter = jax.random.randint(light_key, (blocks, EW), 0, 2)
    counts = jnp.where(filled, CAP, lighter)
    counts = jnp.where(jnp.arange(blocks)[:, None] == 0, CAP, counts)
    order_scores = jax.random.randint(order_key, (blocks, EW, TOK_DEV), 0, 1 << 20) * TOK_DEV + jnp.arange(TOK_DEV)
    order_rank = jnp.argsort(jnp.argsort(order_scores, axis=-1), axis=-1)
    chosen = order_rank < counts[:, :, None]
    other_scores = jax.random.randint(other_key, (blocks, TOK_DEV, EXPERTS - EW), 0, 1 << 20) * (EXPERTS - EW) + jnp.arange(EXPERTS - EW)
    others = lax.top_k(other_scores, TOPK)[1] + EW
    columns = []
    for place in range(TOPK):
        column = others[:, :, place]
        if place < EW:
            column = jnp.where(chosen[:, place, :], place, column)
        columns.append(column)
    return jnp.stack(columns, axis=-1).reshape(ROLLOUT_COUNT, ROLLOUT_LENGTH, TOPK).astype(jnp.int32)


def draw_response_mask(key, part):
    start_key, finish_key = jax.random.split(jax.random.fold_in(key, 13))
    opening = jax.random.randint(start_key, (ROLLOUT_COUNT, 1), 0, ROLLOUT_LENGTH // 4)
    closing = jax.random.randint(finish_key, (ROLLOUT_COUNT, 1), 3 * ROLLOUT_LENGTH // 4, ROLLOUT_LENGTH)
    position = jnp.arange(ROLLOUT_LENGTH)[None, :]
    return ((position >= opening) & (position <= closing)).astype(jnp.int32)


def set_ends(entries, key, low, high):
    spot = [jax.random.randint(jax.random.fold_in(key, axis), (), 0, length) for axis, length in enumerate(entries.shape)]
    main_axis = entries.shape.index(max(entries.shape))
    neighbour = spot[:main_axis] + [(spot[main_axis] + 1) % entries.shape[main_axis]] + spot[main_axis + 1:]
    return entries.at[tuple(spot)].set(low).at[tuple(neighbour)].set(high)


def steps_of(own_key, shape, cuts, low, high):
    factor_of, own = 1.0, jax.random.fold_in(own_key, 6)
    for axis_at, shards_of in cuts:
        draws = jnp.exp(jax.random.uniform(jax.random.fold_in(own, axis_at), (shards_of,), jnp.float32, low / len(cuts), high / len(cuts)))
        factor_of = factor_of * jnp.repeat(draws, shape[axis_at] // shards_of).reshape([-1 if axis == axis_at else 1 for axis in range(len(shape))])
    return factor_of


def length_profile(count, total, reach, skew):
    weights = [(1 << 20) // math.isqrt(rank ** skew) + 1 for rank in range(2, count + 1)]
    surplus, holding = total - reach - (count - 1), [1] * (count - 1)
    while surplus > 0:
        candidates = [i for i in range(count - 1) if holding[i] < reach]
        whole, remaining = sum([weights[i] for i in candidates]), surplus
        for i in candidates:
            more = min(reach - holding[i], max(1, remaining * weights[i] // whole), surplus)
            holding[i] = holding[i] + more
            surplus = surplus - more
    return np.array([reach] + holding)


def uneven(key, amount, total, most, lean):
    if amount == 2:
        one = jax.random.randint(key, (), max(1, total - most), min(most, total - 1) + 1)
        return jnp.stack([one, total - one])
    sizes = jnp.asarray(length_profile(amount, total, most, lean), jnp.int32)
    twos = (amount - 1) // 2
    donor, receiver = sizes[1:1 + 2 * twos:2], sizes[2:2 + 2 * twos:2]
    room = jnp.minimum(donor - 1, most - receiver)
    moved = jax.random.randint(jax.random.fold_in(key, 1), (twos,), 0, 1 << 20) % (room + 1)
    sizes = sizes.at[1:1 + 2 * twos:2].set(donor - moved).at[2:2 + 2 * twos:2].set(receiver + moved)
    return sizes[jax.random.permutation(jax.random.fold_in(key, 2), amount)]


def noise(rng, extent, deviation, bound, cuts=(), kind=jnp.bfloat16):
    drawn = jax.random.normal(rng, extent, jnp.float32) * deviation
    if len(cuts) > 0:
        drawn = steps_of(rng, extent, cuts, -0.22, 0.18) * drawn
    return jnp.clip(drawn, min=-bound, max=bound).astype(kind)


def setup_inputs(seed: int = 0) -> dict:
    streams_of = jax.random.split(jax.random.key(seed), 17)
    queries = draw_queries(jax.random.fold_in(streams_of[16], 71), 0)
    key_rows = draw_key_rows(jax.random.fold_in(streams_of[16], 71), 0)
    value_matrix = noise(streams_of[2], (ROLLOUT_COUNT, ROLLOUT_LENGTH, KEY_VALUE_HEADS * HEAD_SIZE), 1.0, 6.0, ((0, 16), (1, 2)))
    head_sink_logits = jnp.clip(jax.random.uniform(streams_of[3], (QUERY_HEADS,), jnp.float32, 2.0, 6.0), 2.0, 6.0)
    residual = noise(streams_of[4], (ROLLOUT_COUNT, ROLLOUT_LENGTH, D), 1.0, 6.0, ((0, 16), (1, 2)))
    out_weight = noise(streams_of[5], (QUERY_HEADS * HEAD_SIZE, D), (QUERY_HEADS * HEAD_SIZE) ** -0.5, 0.125, ((0, 16),))
    norm_gain = jnp.clip(1.0 + 0.15 * jax.random.normal(streams_of[6], (D,), jnp.float32), 0.25, 1.75)
    router = noise(streams_of[7], (D, EXPERTS), D ** -0.5, 0.109375)
    expert_gate = noise(streams_of[8], (D, EW * HID), D ** -0.5, 0.109375, ((0, 16), (1, 2)))
    expert_up = noise(streams_of[9], (D, EW * HID), D ** -0.5, 0.109375, ((0, 16), (1, 2)))
    expert_down = noise(streams_of[10], (D, EW * HID), HID ** -0.5, 0.125, ((0, 16), (1, 2)))
    routes = draw_routes(jax.random.fold_in(streams_of[16], 71), 0)
    group_ids = jnp.searchsorted(jnp.cumsum(uneven(streams_of[12], GROUPS, ROLLOUT_COUNT, GROUP_MOST, 0)), jnp.arange(ROLLOUT_COUNT), side="right").astype(jnp.int32)
    rewards = set_ends(jax.random.randint(streams_of[13], (ROLLOUT_COUNT,), 0, 4), jax.random.fold_in(streams_of[13], 1), 0, 3).astype(jnp.int32)
    response_mask = draw_response_mask(jax.random.fold_in(streams_of[16], 71), 0)
    upstream = noise(streams_of[15], (ROLLOUT_COUNT, ROLLOUT_LENGTH, D), 1.0, 6.0, ((0, 16), (1, 2)))
    return {"queries": queries, "key_rows": key_rows, "value_matrix": value_matrix, "head_sink_logits": head_sink_logits, "residual": residual, "out_weight": out_weight, "norm_gain": norm_gain, "router": router, "expert_gate": expert_gate, "expert_up": expert_up, "expert_down": expert_down, "routes": routes, "group_ids": group_ids, "rewards": rewards, "response_mask": response_mask, "upstream": upstream}


NORM_EPS = 1e-05
GLU_SLOPE = 1.702
HIGHEST = lax.Precision.HIGHEST

def rounded(values):
    return lax.optimization_barrier(values.astype(jnp.bfloat16))

def glu_forward(gate_pre, up_pre):
    return rounded((up_pre + 1.0) * gate_pre * jax.nn.sigmoid(GLU_SLOPE * gate_pre))

def glu_grads(grad_act, gate_pre, up_pre):
    sigmoid_gate = jax.nn.sigmoid(GLU_SLOPE * gate_pre)
    grad_up = grad_act * (gate_pre * sigmoid_gate)
    grad_gate = grad_act * (up_pre + 1.0) * (sigmoid_gate + GLU_SLOPE * gate_pre * sigmoid_gate * (1.0 - sigmoid_gate))
    return (grad_gate, grad_up)

def head_scores(query_tile_block, key_tile_block, head_sink_logits, allowed):
    query_total_count = query_tile_block.shape[0]
    key_total_count = key_tile_block.shape[0]
    query_head_rows = query_tile_block.reshape(query_total_count, KEY_VALUE_HEADS, QUERY_HEADS // KEY_VALUE_HEADS, HEAD_SIZE).astype(jnp.float32)
    key_head_rows = key_tile_block.reshape(key_total_count, KEY_VALUE_HEADS, HEAD_SIZE).astype(jnp.float32)
    attention_scores = jnp.einsum('baqj,eaj->aqbe', query_head_rows, key_head_rows) * HEAD_SIZE ** (-0.5)
    attention_scores = jnp.where(allowed[None, None], attention_scores, -1e+30)
    sink_logit_column = head_sink_logits.reshape(KEY_VALUE_HEADS, QUERY_HEADS // KEY_VALUE_HEADS)[:, :, None]
    largest = jnp.maximum(lax.optimization_barrier(jnp.max(attention_scores, axis=3)), sink_logit_column)
    raised = jnp.where(allowed[None, None], jnp.exp(attention_scores - largest[..., None]), 0.0)
    sink_raised = jnp.exp(sink_logit_column - largest)
    denominator = lax.optimization_barrier(jnp.sum(raised, axis=3)) + sink_raised
    return (raised / denominator[..., None], sink_raised / denominator)

def head_mix(reduced_probabilities, value_tile_block):
    key_total_count = value_tile_block.shape[0]
    value_head_rows = value_tile_block.reshape(key_total_count, KEY_VALUE_HEADS, HEAD_SIZE).astype(jnp.float32)
    mixed_output = jnp.einsum('amlh,hai->lami', reduced_probabilities.astype(jnp.float32), value_head_rows)
    return rounded(mixed_output.reshape(mixed_output.shape[0], QUERY_HEADS * HEAD_SIZE))

def head_grads(probs, reduced_probabilities, sink_probs, query_tile_block, key_tile_block, value_tile_block, mixed_gradient):
    query_total_count = query_tile_block.shape[0]
    key_total_count = key_tile_block.shape[0]
    query_head_rows = query_tile_block.reshape(query_total_count, KEY_VALUE_HEADS, QUERY_HEADS // KEY_VALUE_HEADS, HEAD_SIZE).astype(jnp.float32)
    key_head_rows = key_tile_block.reshape(key_total_count, KEY_VALUE_HEADS, HEAD_SIZE).astype(jnp.float32)
    value_head_rows = value_tile_block.reshape(key_total_count, KEY_VALUE_HEADS, HEAD_SIZE).astype(jnp.float32)
    heads_gradient = mixed_gradient.reshape(query_total_count, KEY_VALUE_HEADS, QUERY_HEADS // KEY_VALUE_HEADS, HEAD_SIZE).astype(jnp.float32)
    probability_gradient = jnp.einsum('baqj,eaj->aqbe', heads_gradient, value_head_rows)
    spread = lax.optimization_barrier(jnp.sum(probs * probability_gradient, axis=3))
    score_gradient = rounded(probs * (probability_gradient - spread[..., None])).astype(jnp.float32)
    head_scaling = HEAD_SIZE ** (-0.5)
    query_gradient = jnp.einsum('amlh,hai->lami', score_gradient, key_head_rows) * head_scaling
    key_gradient = jnp.einsum('ujko,kujm->oum', score_gradient, query_head_rows) * head_scaling
    value_gradient = jnp.einsum('ujko,kujm->oum', reduced_probabilities.astype(jnp.float32), heads_gradient)
    sink_gradient = -lax.optimization_barrier(jnp.sum(sink_probs * spread, axis=2)).reshape(QUERY_HEADS)
    return (query_gradient.reshape(query_total_count, QUERY_HEADS * HEAD_SIZE).astype(jnp.bfloat16), key_gradient.reshape(key_total_count, KEY_VALUE_HEADS * HEAD_SIZE), value_gradient.reshape(key_total_count, KEY_VALUE_HEADS * HEAD_SIZE), sink_gradient)

def fold_keys(parts):
    own_part = parts[:, WINDOW:]
    halo_part = parts[:, :WINDOW]
    from_next = jnp.concatenate([halo_part[1:], jnp.zeros_like(halo_part[:1])], axis=0)
    tail_rows = own_part[:, TOK_DEV - WINDOW:] + from_next
    merged = jnp.concatenate([own_part[:, :TOK_DEV - WINDOW], tail_rows], axis=1)
    return merged.reshape(ROLLOUT_LENGTH, parts.shape[2])

def one_rollout(head_sink_logits, out_weight, norm_gain, router, expert_gate, expert_up, expert_down, packed):
    queries, key_rows, value_matrix, residual, mask_row, route_rows, upstream, token_scale = packed
    blocks = ROLLOUT_LENGTH // TOK_DEV
    block_ids = jnp.arange(blocks, dtype=jnp.int32)
    key_padded = jnp.concatenate([jnp.zeros((WINDOW, key_rows.shape[1]), key_rows.dtype), key_rows], axis=0)
    value_padded = jnp.concatenate([jnp.zeros((WINDOW, value_matrix.shape[1]), value_matrix.dtype), value_matrix], axis=0)
    row_index = jnp.arange(TOK_DEV, dtype=jnp.int32)[:, None]
    col_index = jnp.arange(WINDOW + TOK_DEV, dtype=jnp.int32)[None, :]
    in_window = (col_index >= row_index + 1) & (col_index <= row_index + WINDOW)

    def block_probs(block_id):
        offset = block_id * TOK_DEV
        query_tile_block = lax.dynamic_slice_in_dim(queries, offset, TOK_DEV, 0)
        key_tile_block = lax.dynamic_slice_in_dim(key_padded, offset, WINDOW + TOK_DEV, 0)
        value_tile_block = lax.dynamic_slice_in_dim(value_padded, offset, WINDOW + TOK_DEV, 0)
        allowed = in_window & ((col_index >= WINDOW) | (block_id > 0))
        probs, sink_probs = head_scores(query_tile_block, key_tile_block, head_sink_logits, allowed)
        return (probs, sink_probs, query_tile_block, key_tile_block, value_tile_block)

    def block_forward(block_id):
        probs, sink_probs, query_tile_block, key_tile_block, value_tile_block = block_probs(block_id)
        return head_mix(rounded(probs), value_tile_block)
    attended = lax.map(block_forward, block_ids).reshape(ROLLOUT_LENGTH, QUERY_HEADS * HEAD_SIZE)
    projected = jnp.dot(attended, out_weight, preferred_element_type=jnp.float32)
    mid_rows = rounded(residual.astype(jnp.float32) + projected)
    mid_wide = mid_rows.astype(jnp.float32)
    inv_rms = lax.rsqrt(lax.optimization_barrier(jnp.mean(mid_wide * mid_wide, axis=1, keepdims=True)) + NORM_EPS)
    unit_rows = mid_wide * inv_rms
    normed = rounded(unit_rows * norm_gain[None, :])
    logits = jnp.dot(normed, router, preferred_element_type=jnp.float32)
    route_logits = jnp.take_along_axis(logits, route_rows, axis=1)
    raised = jnp.exp(route_logits)
    route_weights = raised / lax.optimization_barrier(jnp.sum(raised, axis=1, keepdims=True))
    route_hot = route_rows[:, :, None] == jnp.arange(EXPERTS, dtype=jnp.int32)[None, None, :]
    member = route_hot[:, :, :EW]
    expert_share = lax.optimization_barrier(jnp.sum(jnp.where(member, route_weights[:, :, None], 0.0), axis=1))
    chosen = jnp.any(member, axis=1).reshape(blocks, TOK_DEV, EW)
    slot_rank = jnp.cumsum(chosen.astype(jnp.int32), axis=1) - 1
    slot_wide = (chosen[..., None] & (slot_rank[..., None] == jnp.arange(CAP, dtype=jnp.int32))).astype(jnp.float32)
    slot_rows = rounded(jnp.einsum('btec,btd->becd', slot_wide, normed.reshape(blocks, TOK_DEV, D).astype(jnp.float32), precision=HIGHEST))
    loss_weight = token_scale * mask_row.astype(jnp.float32)
    upstream_slots = jnp.einsum('btec,btd->becd', slot_wide, upstream.reshape(blocks, TOK_DEV, D).astype(jnp.float32), precision=HIGHEST)
    weight_slots = jnp.einsum('btec,bt->bec', slot_wide, loss_weight.reshape(blocks, TOK_DEV), precision=HIGHEST)
    share_slots = jnp.einsum('btec,bte->bec', slot_wide, expert_share.reshape(blocks, TOK_DEV, EW), precision=HIGHEST)
    cot_slots = weight_slots[..., None] * upstream_slots
    grad_share_parts = []
    grad_normed_moe = jnp.zeros((ROLLOUT_LENGTH, D), jnp.float32)
    for expert in range(EW):
        gate_cols = expert_gate[:, expert * HID:(expert + 1) * HID]
        up_cols = expert_up[:, expert * HID:(expert + 1) * HID]
        down_cols = expert_down[:, expert * HID:(expert + 1) * HID]
        flat_rows = slot_rows[:, expert].reshape(blocks * CAP, D)
        gate_pre = jnp.dot(flat_rows, gate_cols, preferred_element_type=jnp.float32)
        up_pre = jnp.dot(flat_rows, up_cols, preferred_element_type=jnp.float32)
        activation = glu_forward(gate_pre, up_pre)
        down_pieces = down_cols.reshape(D, PIECES, HID_DEV).astype(jnp.float32)
        partial_out = rounded(jnp.einsum('nph,dph->npd', activation.reshape(-1, PIECES, HID_DEV).astype(jnp.float32), down_pieces))
        expert_out = lax.optimization_barrier(jnp.sum(partial_out.astype(jnp.float32), axis=1)).reshape(blocks, CAP, D)
        expert_cot = cot_slots[:, expert]
        grad_share_parts.append(lax.optimization_barrier(jnp.sum(expert_cot * expert_out, axis=2)))
        grad_out = rounded(share_slots[:, expert, :, None] * expert_cot).reshape(blocks * CAP, D)
        grad_act = jnp.dot(grad_out, down_cols, preferred_element_type=jnp.float32)
        grad_gate, grad_up = glu_grads(grad_act, gate_pre, up_pre)
        gate_pieces = gate_cols.reshape(D, PIECES, HID_DEV).astype(jnp.float32)
        up_pieces = up_cols.reshape(D, PIECES, HID_DEV).astype(jnp.float32)
        gate_low = rounded(grad_gate).reshape(-1, PIECES, HID_DEV).astype(jnp.float32)
        up_low = rounded(grad_up).reshape(-1, PIECES, HID_DEV).astype(jnp.float32)
        grad_piece = rounded(jnp.einsum('nph,dph->npd', gate_low, gate_pieces) + jnp.einsum('nph,dph->npd', up_low, up_pieces))
        grad_rows = lax.optimization_barrier(jnp.sum(grad_piece.astype(jnp.float32), axis=1)).reshape(blocks, CAP, D)
        grad_normed_moe = grad_normed_moe + jnp.einsum('btc,bcd->btd', slot_wide[:, :, expert], grad_rows, precision=HIGHEST).reshape(ROLLOUT_LENGTH, D)
    grad_share_slots = jnp.stack(grad_share_parts, axis=1)
    grad_share = jnp.einsum('btec,bec->bte', slot_wide, grad_share_slots, precision=HIGHEST).reshape(ROLLOUT_LENGTH, EW)
    grad_weights = lax.optimization_barrier(jnp.sum(jnp.where(member, grad_share[:, None, :], 0.0), axis=2))
    grad_route = route_weights * (grad_weights - lax.optimization_barrier(jnp.sum(route_weights * grad_weights, axis=1, keepdims=True)))
    grad_logits = rounded(lax.optimization_barrier(jnp.sum(jnp.where(route_hot, grad_route[:, :, None], 0.0), axis=1)))
    grad_normed = jnp.dot(grad_logits, router.T, preferred_element_type=jnp.float32) + grad_normed_moe
    grad_unit = grad_normed * norm_gain[None, :]
    grad_mid = loss_weight[:, None] * upstream.astype(jnp.float32) + inv_rms * (grad_unit - unit_rows * lax.optimization_barrier(jnp.mean(grad_unit * unit_rows, axis=1, keepdims=True)))
    grad_residual = grad_mid.astype(jnp.bfloat16)
    grad_attended = jnp.dot(grad_residual, out_weight.T, preferred_element_type=jnp.float32).astype(jnp.bfloat16)

    def block_backward(block_id):
        probs, sink_probs, query_tile_block, key_tile_block, value_tile_block = block_probs(block_id)
        grad_block = lax.dynamic_slice_in_dim(grad_attended, block_id * TOK_DEV, TOK_DEV, 0)
        return head_grads(probs, rounded(probs), sink_probs, query_tile_block, key_tile_block, value_tile_block, grad_block)
    query_gradient, key_gradient, value_gradient, sink_gradient = lax.map(block_backward, block_ids)
    return (query_gradient.reshape(ROLLOUT_LENGTH, QUERY_HEADS * HEAD_SIZE), fold_keys(key_gradient).astype(jnp.bfloat16), fold_keys(value_gradient).astype(jnp.bfloat16), grad_residual, lax.optimization_barrier(jnp.sum(sink_gradient, axis=0)))

def reference(queries, key_rows, value_matrix, head_sink_logits, residual, out_weight, norm_gain, router, expert_gate, expert_up, expert_down, routes, group_ids, rewards, response_mask, upstream):
    group_hot = (group_ids[:, None] == jnp.arange(GROUPS, dtype=jnp.int32)[None, :]).astype(jnp.float32)
    reward = rewards.astype(jnp.float32)
    reward_terms = jnp.stack([jnp.ones_like(reward), reward, reward * reward], axis=1)
    group_totals = lax.optimization_barrier(jnp.sum(group_hot[:, :, None] * reward_terms[:, None, :], axis=0))
    group_sizes = group_totals[:, 0]
    group_means = group_totals[:, 1] / group_sizes
    group_spread = group_totals[:, 2] / group_sizes - group_means * group_means
    own_mean = lax.optimization_barrier(jnp.sum(group_hot * group_means[None, :], axis=1))
    own_spread = lax.optimization_barrier(jnp.sum(group_hot * group_spread[None, :], axis=1))
    advantage = (reward - own_mean) / jnp.sqrt(jnp.maximum(own_spread, 1.0))
    token_total = jnp.sum(response_mask.astype(jnp.float32))
    token_scale = -advantage * NTOK / token_total
    stepper = partial(one_rollout, head_sink_logits, out_weight, norm_gain, router, expert_gate, expert_up, expert_down)
    grads = lax.map(stepper, (queries, key_rows, value_matrix, residual, response_mask, routes, upstream, token_scale))
    return (grads[0], grads[1], grads[2], grads[3], lax.optimization_barrier(jnp.sum(grads[4], axis=0)))
```

```python
import functools

import jax
import jax.numpy as jnp
from jax import lax
from jax.experimental import pallas as pl
from jax.experimental.pallas import tpu as pltpu
from jax.sharding import PartitionSpec as P

D = 2880
HEAD_SIZE = 64
WINDOW = 128
EXPERTS = 128
QUERY_HEADS = 32
KEY_VALUE_HEADS = 4
EW = 2
CAP = 4


NORM_EPS = 1e-05
GLU_SLOPE = 1.702
HIGHEST = lax.Precision.HIGHEST
CONTRACT_LAST = (((1,), (1,)), ((), ()))


def passed_along(value, axis, steps):
    count = lax.axis_size(axis)
    initial, last = (max(0, -steps), min(count, count - steps))
    return lax.ppermute(value, axis, [(source, source + steps) for source in range(initial, last)])


def glu_forward(gate_pre, up_pre):
    return ((up_pre + 1.0) * gate_pre * jax.nn.sigmoid(GLU_SLOPE * gate_pre)).astype(jnp.bfloat16)


def glu_grads(grad_act, gate_pre, up_pre):
    sigmoid_gate = jax.nn.sigmoid(GLU_SLOPE * gate_pre)
    grad_up = grad_act * (gate_pre * sigmoid_gate)
    grad_gate = (
        grad_act
        * (up_pre + 1.0)
        * (sigmoid_gate + GLU_SLOPE * gate_pre * sigmoid_gate * (1.0 - sigmoid_gate))
    )
    return (grad_gate, grad_up)


def head_scores(query_tile_block, key_tile_block, head_sink_logits, allowed):
    query_total_count = query_tile_block.shape[0]
    key_total_count = key_tile_block.shape[0]
    query_head_rows = query_tile_block.reshape(
        query_total_count, KEY_VALUE_HEADS, QUERY_HEADS // KEY_VALUE_HEADS, HEAD_SIZE
    )
    key_head_rows = key_tile_block.reshape(key_total_count, KEY_VALUE_HEADS, HEAD_SIZE)
    attention_scores = jnp.einsum(
        "baqj,eaj->aqbe", query_head_rows, key_head_rows, preferred_element_type=jnp.float32
    ) * HEAD_SIZE ** (-0.5)
    attention_scores = jnp.where(allowed[None, None], attention_scores, -1e30)
    sink_logit_column = head_sink_logits.reshape(KEY_VALUE_HEADS, QUERY_HEADS // KEY_VALUE_HEADS)[
        :, :, None
    ]
    largest = jnp.maximum(jnp.max(attention_scores, axis=3), sink_logit_column)
    raised = jnp.where(allowed[None, None], jnp.exp(attention_scores - largest[..., None]), 0.0)
    sink_raised = jnp.exp(sink_logit_column - largest)
    denominator = jnp.sum(raised, axis=3) + sink_raised
    return (raised / denominator[..., None], sink_raised / denominator)


def head_mix(reduced_probabilities, value_tile_block):
    key_total_count = value_tile_block.shape[0]
    value_head_rows = value_tile_block.reshape(key_total_count, KEY_VALUE_HEADS, HEAD_SIZE)
    mixed_output = jnp.einsum(
        "amlh,hai->lami", reduced_probabilities, value_head_rows, preferred_element_type=jnp.float32
    )
    return mixed_output.reshape(mixed_output.shape[0], QUERY_HEADS * HEAD_SIZE).astype(jnp.bfloat16)


def head_grads(
    probs,
    reduced_probabilities,
    sink_probs,
    query_tile_block,
    key_tile_block,
    value_tile_block,
    mixed_gradient,
):
    query_total_count = query_tile_block.shape[0]
    key_total_count = key_tile_block.shape[0]
    query_head_rows = query_tile_block.reshape(
        query_total_count, KEY_VALUE_HEADS, QUERY_HEADS // KEY_VALUE_HEADS, HEAD_SIZE
    )
    key_head_rows = key_tile_block.reshape(key_total_count, KEY_VALUE_HEADS, HEAD_SIZE)
    value_head_rows = value_tile_block.reshape(key_total_count, KEY_VALUE_HEADS, HEAD_SIZE)
    heads_gradient = mixed_gradient.reshape(
        query_total_count, KEY_VALUE_HEADS, QUERY_HEADS // KEY_VALUE_HEADS, HEAD_SIZE
    )
    probability_gradient = jnp.einsum(
        "baqj,eaj->aqbe", heads_gradient, value_head_rows, preferred_element_type=jnp.float32
    )
    spread = jnp.sum(probs * probability_gradient, axis=3)
    score_gradient = (probs * (probability_gradient - spread[..., None])).astype(jnp.bfloat16)
    head_scaling = HEAD_SIZE ** (-0.5)
    query_gradient = (
        jnp.einsum(
            "amlh,hai->lami", score_gradient, key_head_rows, preferred_element_type=jnp.float32
        )
        * head_scaling
    )
    key_gradient = (
        jnp.einsum(
            "ujko,kujm->oum", score_gradient, query_head_rows, preferred_element_type=jnp.float32
        )
        * head_scaling
    )
    value_gradient = jnp.einsum(
        "ujko,kujm->oum", reduced_probabilities, heads_gradient, preferred_element_type=jnp.float32
    )
    sink_gradient = -jnp.sum(sink_probs * spread, axis=2).reshape(QUERY_HEADS)
    return (
        query_gradient.reshape(query_total_count, QUERY_HEADS * HEAD_SIZE).astype(jnp.bfloat16),
        key_gradient.reshape(key_total_count, KEY_VALUE_HEADS * HEAD_SIZE),
        value_gradient.reshape(key_total_count, KEY_VALUE_HEADS * HEAD_SIZE),
        sink_gradient,
    )


def block_backward(grad_flat, gate_pre, up_pre, gate_full, up_full, down_full):
    grad_act = jnp.dot(grad_flat, down_full, preferred_element_type=jnp.float32)
    grad_gate, grad_up = glu_grads(grad_act, gate_pre, up_pre)
    grad_pair = jnp.concatenate([grad_gate, grad_up], axis=1).astype(jnp.bfloat16)
    weight_pair = jnp.concatenate([gate_full, up_full], axis=1)
    return lax.dot_general(
        grad_pair, weight_pair, CONTRACT_LAST, preferred_element_type=jnp.float32
    ).astype(jnp.bfloat16)


def general_shards(
    queries,
    key_rows,
    value_matrix,
    head_sink_logits,
    residual,
    out_weight,
    norm_gain,
    router,
    expert_gate,
    expert_up,
    expert_down,
    routes,
    group_ids,
    rewards,
    response_mask,
    upstream,
):
    seq_count = lax.axis_size("seq")
    dp_count = lax.axis_size("dp")
    seq_index = lax.axis_index("seq")
    query_rows = queries[0]
    own_keys = key_rows[0]
    own_values = value_matrix[0]
    tokens_here = query_rows.shape[0]
    pieces = seq_count // EW
    group_count = max(dp_count // 4, 1)
    all_tokens = dp_count * seq_count * tokens_here
    group_hot = (group_ids[0] == jnp.arange(group_count, dtype=jnp.int32)).astype(jnp.float32)
    reward = rewards[0].astype(jnp.float32)
    group_terms = (
        group_hot[:, None] * jnp.stack([jnp.ones_like(reward), reward, reward * reward])[None, :]
    )
    mask_wide = response_mask[0].astype(jnp.float32)
    local_count = jnp.sum(mask_wide)
    first_device = (seq_index == 0).astype(jnp.float32)
    group_totals, token_total = lax.psum((group_terms * first_device, local_count), ("seq", "dp"))
    group_sizes = group_totals[:, 0]
    group_means = group_totals[:, 1] / group_sizes
    group_spread = group_totals[:, 2] / group_sizes - group_means * group_means
    own_mean = jnp.sum(group_hot * group_means)
    own_spread = jnp.sum(group_hot * group_spread)
    advantage = (reward - own_mean) / jnp.sqrt(jnp.maximum(own_spread, 1.0))
    token_scale = -advantage * all_tokens / token_total
    loss_weight = token_scale * mask_wide
    halo_keys, halo_values = passed_along((own_keys, own_values), "seq", 1)
    key_tile_block = jnp.concatenate([halo_keys, own_keys], axis=0)
    value_tile_block = jnp.concatenate([halo_values, own_values], axis=0)
    row_index = jnp.arange(tokens_here, dtype=jnp.int32)[:, None]
    col_index = jnp.arange(WINDOW + tokens_here, dtype=jnp.int32)[None, :]
    allowed = (
        (col_index >= row_index + 1)
        & (col_index <= row_index + WINDOW)
        & ((col_index >= WINDOW) | (seq_index > 0))
    )
    probs, sink_probs = head_scores(query_rows, key_tile_block, head_sink_logits, allowed)
    reduced_probabilities = probs.astype(jnp.bfloat16)
    attended = head_mix(reduced_probabilities, value_tile_block)
    out_full = lax.all_gather(out_weight, "dp", axis=0, tiled=True)
    projected = jnp.dot(attended, out_full, preferred_element_type=jnp.float32)
    mid_rows = lax.optimization_barrier(
        (residual[0].astype(jnp.float32) + projected).astype(jnp.bfloat16)
    )
    mid_wide = mid_rows.astype(jnp.float32)
    inv_rms = lax.rsqrt(jnp.mean(mid_wide * mid_wide, axis=1, keepdims=True) + NORM_EPS)
    unit_rows = mid_wide * inv_rms
    normed = (unit_rows * norm_gain[None, :]).astype(jnp.bfloat16)
    logits = jnp.dot(normed, router, preferred_element_type=jnp.float32)
    route_hot = routes[0][:, :, None] == jnp.arange(EXPERTS, dtype=jnp.int32)[None, None, :]
    route_logits = jnp.sum(jnp.where(route_hot, logits[:, None, :], 0.0), axis=2)
    raised = jnp.exp(route_logits)
    route_weights = raised / jnp.sum(raised, axis=1, keepdims=True)
    member = route_hot[:, :, :EW]
    expert_share = jnp.sum(jnp.where(member, route_weights[:, :, None], 0.0), axis=1)
    chosen = jnp.any(member, axis=1)
    slot_rank = jnp.cumsum(chosen.astype(jnp.int32), axis=0) - 1
    slot_hot = chosen[:, :, None] & (
        slot_rank[:, :, None] == jnp.arange(CAP, dtype=jnp.int32)[None, None, :]
    )
    slot_low = slot_hot.astype(jnp.bfloat16)
    slot_wide = slot_hot.astype(jnp.float32)
    slot_rows = jnp.einsum(
        "tec,td->ecd", slot_low, normed, preferred_element_type=jnp.float32
    ).astype(jnp.bfloat16)
    outgoing = jnp.broadcast_to(slot_rows[:, None], (EW, pieces, CAP, D)).reshape(seq_count, CAP, D)
    upstream_slots = jnp.einsum(
        "tec,td->ecd", slot_low, upstream[0], preferred_element_type=jnp.float32
    )
    weight_slots = jnp.einsum("tec,t->ec", slot_wide, loss_weight, precision=HIGHEST)
    share_slots = jnp.einsum("tec,te->ec", slot_wide, expert_share, precision=HIGHEST)
    cot_slots = weight_slots[:, :, None] * upstream_slots
    grad_out = (share_slots[:, :, None] * cot_slots).astype(jnp.bfloat16)
    grad_outgoing = jnp.broadcast_to(grad_out[:, None], (EW, pieces, CAP, D)).reshape(
        seq_count, CAP, D
    )
    gate_full, up_full, down_full = (
        lax.all_gather(expert_gate, "dp", axis=0, tiled=True),
        lax.all_gather(expert_up, "dp", axis=0, tiled=True),
        lax.all_gather(expert_down, "dp", axis=0, tiled=True),
    )
    arrived = lax.all_to_all(outgoing, "seq", split_axis=0, concat_axis=0, tiled=True)
    senders = arrived.shape[0]
    items = arrived.shape[1]
    block_senders = arrived.shape[0]
    block_items = arrived.shape[1]
    flat_rows = arrived.reshape(block_senders * block_items, D)
    gate_pre = jnp.dot(flat_rows, gate_full, preferred_element_type=jnp.float32)
    up_pre = jnp.dot(flat_rows, up_full, preferred_element_type=jnp.float32)
    activation = glu_forward(gate_pre, up_pre)
    partial_out = lax.dot_general(
        activation, down_full, CONTRACT_LAST, preferred_element_type=jnp.float32
    ).astype(jnp.bfloat16)
    partial_out, gate_pre, up_pre = (
        partial_out.reshape(block_senders, block_items, D),
        gate_pre,
        up_pre,
    )
    back_out = lax.all_to_all(partial_out, "seq", split_axis=0, concat_axis=0, tiled=True)
    gate_held = gate_pre.reshape(senders, items, -1)
    up_held = up_pre.reshape(senders, items, -1)
    grad_arrived = lax.all_to_all(grad_outgoing, "seq", split_axis=0, concat_axis=0, tiled=True)
    grad_piece = block_backward(
        grad_arrived.reshape(seq_count * CAP, D),
        gate_held.reshape(seq_count * CAP, -1),
        up_held.reshape(seq_count * CAP, -1),
        gate_full,
        up_full,
        down_full,
    )
    grad_back = lax.all_to_all(
        grad_piece.reshape(seq_count, CAP, D), "seq", split_axis=0, concat_axis=0, tiled=True
    )
    expert_out = jnp.sum(back_out.reshape(EW, pieces, CAP, D).astype(jnp.float32), axis=1)
    grad_share_slots = jnp.sum(cot_slots * expert_out, axis=2)
    grad_rows = jnp.sum(grad_back.reshape(EW, pieces, CAP, D).astype(jnp.float32), axis=1)
    grad_normed_moe = jnp.einsum("tec,ecd->td", slot_wide, grad_rows, precision=HIGHEST)
    grad_share = jnp.einsum("tec,ec->te", slot_wide, grad_share_slots, precision=HIGHEST)
    grad_weights = jnp.sum(jnp.where(member, grad_share[:, None, :], 0.0), axis=2)
    grad_route = route_weights * (
        grad_weights - jnp.sum(route_weights * grad_weights, axis=1, keepdims=True)
    )
    grad_logits = jnp.sum(jnp.where(route_hot, grad_route[:, :, None], 0.0), axis=1).astype(
        jnp.bfloat16
    )
    grad_normed = (
        lax.dot_general(grad_logits, router, CONTRACT_LAST, preferred_element_type=jnp.float32)
        + grad_normed_moe
    )
    grad_unit = grad_normed * norm_gain[None, :]
    grad_mid = loss_weight[:, None] * upstream[0].astype(jnp.float32) + inv_rms * (
        grad_unit - unit_rows * jnp.mean(grad_unit * unit_rows, axis=1, keepdims=True)
    )
    grad_residual = grad_mid.astype(jnp.bfloat16)
    grad_attended = lax.dot_general(
        grad_residual, out_full, CONTRACT_LAST, preferred_element_type=jnp.float32
    ).astype(jnp.bfloat16)
    query_gradient, key_gradient, value_gradient, sink_gradient = head_grads(
        probs,
        reduced_probabilities,
        sink_probs,
        query_rows,
        key_tile_block,
        value_tile_block,
        grad_attended,
    )
    next_keys, next_values = (
        passed_along(key_gradient[:WINDOW].astype(jnp.bfloat16), "seq", -1).astype(jnp.float32),
        passed_along(value_gradient[:WINDOW].astype(jnp.bfloat16), "seq", -1).astype(jnp.float32),
    )
    own_key_grad = key_gradient[WINDOW:]
    own_value_grad = value_gradient[WINDOW:]
    split_at = tokens_here - WINDOW
    grad_key_rows = jnp.concatenate(
        [own_key_grad[:split_at], own_key_grad + next_keys], axis=0
    ).astype(jnp.bfloat16)
    grad_value_rows = jnp.concatenate(
        [own_value_grad[:split_at], own_value_grad + next_values], axis=0
    ).astype(jnp.bfloat16)
    grad_sinks = lax.psum(sink_gradient, ("seq", "dp"))
    return (
        query_gradient[None],
        grad_key_rows[None],
        grad_value_rows[None],
        grad_residual[None],
        grad_sinks,
    )


MESH = pl.DeviceIdType.MESH
MIB = 1 << 20


def halving_place(index, count):
    place, weight, rest = 0, count // 2, index
    while weight:
        place = place + lax.rem(rest, 2) * weight
        rest = lax.div(rest, 2)
        weight //= 2
    return place


def flipped(index, bit):
    return index + bit - 2 * bit * lax.rem(lax.div(index, bit), 2)


def expert_kernel(
    count,
    slots_ref,
    gate_ref,
    up_ref,
    down_ref,
    own_ref,
    other_ref,
    theirs,
    outgoing,
    arrived,
    sent,
    total,
    received,
    grads,
    back,
    seq_send,
    seq_recv,
    to_send,
    to_recv,
    halve_send,
    halve_recv,
    double_send,
    double_recv,
    back_send,
    back_recv,
):
    bits = count.bit_length() - 1
    me = lax.axis_index("dp")
    side = lax.axis_index("seq")
    far = 1 - side
    place = halving_place(me, count)
    depth = gate_ref.shape[0]
    hidden = gate_ref.shape[1]
    wide = 3 * hidden // 2

    barrier = pltpu.get_barrier_semaphore()
    pl.semaphore_signal(barrier, inc=1, device_id={"seq": far}, device_id_type=MESH)

    def greet(step, carry):
        pl.semaphore_signal(
            barrier, inc=1, device_id={"dp": lax.rem(me + step, count)}, device_id_type=MESH
        )
        return carry

    lax.fori_loop(1, count, greet, 0)
    pl.semaphore_wait(barrier, count)

    swap = pltpu.make_async_remote_copy(
        src_ref=slots_ref.at[far],
        dst_ref=theirs,
        send_sem=seq_send.at[0],
        recv_sem=seq_recv.at[0],
        device_id={"seq": far},
        device_id_type=MESH,
    )
    swap.start()
    back[...] = jnp.zeros_like(back)
    swap.wait()
    mine = slots_ref[side]
    came = theirs[...]
    first = jnp.where(side == 0, mine, came)
    second = jnp.where(side == 0, came, mine)
    outgoing[...] = jnp.concatenate(
        [first[:, :CAP], second[:, :CAP], first[:, CAP:], second[:, CAP:]], axis=1
    ).astype(jnp.bfloat16)

    def slice_copy(step):
        to = lax.rem(me + step, count)
        return pltpu.make_async_remote_copy(
            src_ref=outgoing.at[to],
            dst_ref=arrived.at[place],
            send_sem=to_send.at[step],
            recv_sem=to_recv.at[step],
            device_id={"dp": to},
            device_id_type=MESH,
        )

    def start_slice(step, carry):
        slice_copy(step).start()
        return carry

    def wait_slice(step, carry):
        slice_copy(step).wait()
        return carry

    lax.fori_loop(1, count, start_slice, 0)
    arrived[place] = outgoing[me]
    lax.fori_loop(1, count, wait_slice, 0)

    half = count // 2
    rows = EW * CAP
    tile = 512

    def products(start):
        block = arrived[pl.ds(start, half)].astype(jnp.float32)
        normed = block[:, :rows].reshape(half * rows, -1)[:, :depth].astype(jnp.bfloat16)
        upstream = block[:, rows:].reshape(half * rows, -1)[:, :depth].astype(jnp.bfloat16)

        def product(column):
            which, at = divmod(column, hidden)
            weight = (gate_ref, up_ref, down_ref)[which]
            return jnp.dot(
                upstream if which == 2 else normed,
                weight[:, at : at + tile],
                preferred_element_type=jnp.float32,
            ).reshape(half, rows, tile)

        for column in range(0, wide, tile):
            yield column, jnp.concatenate([product(column), product(wide + column)], axis=1)

    def halve_copy(stage):
        blocks = half >> stage
        return pltpu.make_async_remote_copy(
            src_ref=sent[stage],
            dst_ref=received[stage],
            send_sem=halve_send.at[stage],
            recv_sem=halve_recv.at[stage],
            device_id={"dp": flipped(me, 1 << stage)},
            device_id_type=MESH,
        )

    bit_of = [lax.rem(lax.div(me, 1 << stage), 2) for stage in range(bits)]
    for column, value in products((1 - bit_of[0]) * half):
        sent[0][:, :, column : column + tile] = value.astype(jnp.bfloat16)
    halve_copy(0).start()
    for column, value in products(bit_of[0] * half):
        total[:, :, column : column + tile] = value
    base = 0
    for stage in range(1, bits):
        blocks = half >> stage
        halve_copy(stage - 1).wait()
        away = (1 - bit_of[stage]) * blocks
        keep = bit_of[stage] * blocks
        sent[stage][...] = (
            total[pl.ds(base + away, blocks)]
            + received[stage - 1][pl.ds(away, blocks)].astype(jnp.float32)
        ).astype(jnp.bfloat16)
        halve_copy(stage).start()
        total[pl.ds(base + keep, blocks)] += received[stage - 1][pl.ds(keep, blocks)].astype(
            jnp.float32
        )
        base = base + keep
    halve_copy(bits - 1).wait()
    summed = total[base] + received[bits - 1][0].astype(jnp.float32)

    gate_pre = summed[:rows, :hidden]
    up_pre = jnp.concatenate([summed[:rows, hidden:], summed[rows:, : hidden // 2]], axis=1)
    grad_act = summed[rows:, hidden // 2 :]
    sigmoid_gate = 1.0 / (1.0 + jnp.exp(-GLU_SLOPE * gate_pre))
    gate_sigmoid = gate_pre * sigmoid_gate
    raised_up = up_pre + 1.0
    activation = (raised_up * gate_sigmoid).astype(jnp.bfloat16).astype(jnp.float32)
    share = jnp.sum(activation * grad_act, axis=1, keepdims=True)
    grad_up = grad_act * gate_sigmoid
    grad_gate = (
        grad_act * raised_up * (sigmoid_gate + GLU_SLOPE * gate_sigmoid * (1.0 - sigmoid_gate))
    )
    grads[place] = jnp.concatenate([grad_gate, grad_up], axis=0).astype(jnp.bfloat16)

    for stage in range(bits):
        blocks = 1 << stage
        start = place // blocks * blocks
        copy = pltpu.make_async_remote_copy(
            src_ref=grads.at[pl.ds(start, blocks)],
            dst_ref=grads.at[pl.ds(start, blocks)],
            send_sem=double_send.at[stage],
            recv_sem=double_recv.at[stage],
            device_id={"dp": flipped(me, half >> stage)},
            device_id_type=MESH,
        )
        copy.start()
        copy.wait()

    flat = grads[...].reshape(count * 2 * rows, hidden)
    contract = (((1,), (1,)), ((), ()))
    from_gate = lax.dot_general(flat, gate_ref[...], contract, preferred_element_type=jnp.float32)
    from_up = lax.dot_general(flat, up_ref[...], contract, preferred_element_type=jnp.float32)
    from_gate = from_gate.reshape(count, 2 * rows, depth)
    from_up = from_up.reshape(count, 2 * rows, depth)
    back[:, :, :depth] = from_gate[:, :rows] + from_up[:, rows:]

    def back_copy(step):
        to = lax.rem(me + step, count)
        return pltpu.make_async_remote_copy(
            src_ref=back.at[halving_place(to, count)],
            dst_ref=own_ref.at[me],
            send_sem=back_send.at[step],
            recv_sem=back_recv.at[step],
            device_id={"dp": to},
            device_id_type=MESH,
        )

    def start_back(step, carry):
        back_copy(step).start()
        return carry

    def wait_back(step, carry):
        back_copy(step).wait()
        return carry

    lax.fori_loop(1, count, start_back, 0)
    own_ref[me] = back[place]
    own_ref[count] = jnp.broadcast_to(share, own_ref.shape[1:])
    lax.fori_loop(1, count, wait_back, 0)
    last = pltpu.make_async_remote_copy(
        src_ref=own_ref,
        dst_ref=other_ref,
        send_sem=seq_send.at[1],
        recv_sem=seq_recv.at[1],
        device_id={"seq": far},
        device_id_type=MESH,
    )
    last.start()
    last.wait()


def in_place_experts(slots, gate, up, down):
    count, lanes = slots.shape[1], slots.shape[3]
    bits = count.bit_length() - 1
    rows = EW * CAP
    hidden = gate.shape[1]
    wide = 3 * hidden // 2
    stages = [pltpu.VMEM((count >> (stage + 1), 2 * rows, wide), jnp.bfloat16) for stage in range(bits)]
    vmem = pl.BlockSpec(memory_space=pltpu.VMEM)
    dma = pltpu.SemaphoreType.DMA
    result = jax.ShapeDtypeStruct((count + 1, rows, lanes), jnp.float32)
    return pl.pallas_call(
        functools.partial(expert_kernel, count),
        out_shape=(result, result),
        in_specs=[vmem] * 4,
        out_specs=(vmem, vmem),
        scratch_shapes=[
            pltpu.VMEM((count, rows, lanes), jnp.float32),
            pltpu.VMEM((count, 2 * rows, lanes), jnp.bfloat16),
            pltpu.VMEM((count, 2 * rows, lanes), jnp.bfloat16),
            stages,
            pltpu.VMEM((count // 2, 2 * rows, wide), jnp.float32),
            stages,
            pltpu.VMEM((count, 2 * rows, hidden), jnp.bfloat16),
            pltpu.VMEM((count, rows, lanes), jnp.float32),
            dma((2,)),
            dma((2,)),
            dma((count,)),
            dma((count,)),
            dma((bits,)),
            dma((bits,)),
            dma((bits,)),
            dma((bits,)),
            dma((count,)),
            dma((count,)),
        ],
        compiler_params=pltpu.CompilerParams(
            collective_id=1, has_side_effects=True, vmem_limit_bytes=40 * MIB
        ),
        name="expert_kernel",
    )(slots, gate, up, down)


def shards(
    queries,
    key_rows,
    value_matrix,
    head_sink_logits,
    residual,
    out_weight,
    norm_gain,
    router,
    expert_gate,
    expert_up,
    expert_down,
    routes,
    group_ids,
    rewards,
    response_mask,
    upstream,
):
    seq_count = lax.axis_size("seq")
    dp_count = lax.axis_size("dp")
    seq_index = lax.axis_index("seq")
    query_rows = queries[0]
    own_keys = key_rows[0]
    own_values = value_matrix[0]
    tokens_here = query_rows.shape[0]
    group_count = max(dp_count // 4, 1)
    all_tokens = dp_count * seq_count * tokens_here
    group_hot = (group_ids[0] == jnp.arange(group_count, dtype=jnp.int32)).astype(jnp.float32)
    reward = rewards[0].astype(jnp.float32)
    group_terms = (
        group_hot[:, None] * jnp.stack([jnp.ones_like(reward), reward, reward * reward])[None, :]
    )
    mask_wide = response_mask[0].astype(jnp.float32)
    local_count = jnp.sum(mask_wide)
    first_device = (seq_index == 0).astype(jnp.float32)
    group_totals, token_total = lax.psum((group_terms * first_device, local_count), ("seq", "dp"))
    group_sizes = group_totals[:, 0]
    group_means = group_totals[:, 1] / group_sizes
    group_spread = group_totals[:, 2] / group_sizes - group_means * group_means
    own_mean = jnp.sum(group_hot * group_means)
    own_spread = jnp.sum(group_hot * group_spread)
    advantage = (reward - own_mean) / jnp.sqrt(jnp.maximum(own_spread, 1.0))
    token_scale = -advantage * all_tokens / token_total
    loss_weight = token_scale * mask_wide
    halo_keys, halo_values = passed_along((own_keys, own_values), "seq", 1)
    key_tile_block = jnp.concatenate([halo_keys, own_keys], axis=0)
    value_tile_block = jnp.concatenate([halo_values, own_values], axis=0)
    row_index = jnp.arange(tokens_here, dtype=jnp.int32)[:, None]
    col_index = jnp.arange(WINDOW + tokens_here, dtype=jnp.int32)[None, :]
    allowed = (
        (col_index >= row_index + 1)
        & (col_index <= row_index + WINDOW)
        & ((col_index >= WINDOW) | (seq_index > 0))
    )
    probs, sink_probs = head_scores(query_rows, key_tile_block, head_sink_logits, allowed)
    reduced_probabilities = probs.astype(jnp.bfloat16)
    attended = head_mix(reduced_probabilities, value_tile_block)
    out_full = lax.all_gather(out_weight, "dp", axis=0, tiled=True)
    projected = jnp.dot(attended, out_full, preferred_element_type=jnp.float32)
    mid_rows = lax.optimization_barrier(
        (residual[0].astype(jnp.float32) + projected).astype(jnp.bfloat16)
    )
    mid_wide = mid_rows.astype(jnp.float32)
    inv_rms = lax.rsqrt(jnp.mean(mid_wide * mid_wide, axis=1, keepdims=True) + NORM_EPS)
    unit_rows = mid_wide * inv_rms
    normed = (unit_rows * norm_gain[None, :]).astype(jnp.bfloat16)
    logits = jnp.dot(normed, router, preferred_element_type=jnp.float32)
    route_hot = routes[0][:, :, None] == jnp.arange(EXPERTS, dtype=jnp.int32)[None, None, :]
    route_logits = jnp.sum(jnp.where(route_hot, logits[:, None, :], 0.0), axis=2)
    raised = jnp.exp(route_logits)
    route_weights = raised / jnp.sum(raised, axis=1, keepdims=True)
    member = route_hot[:, :, :EW]
    expert_share = jnp.sum(jnp.where(member, route_weights[:, :, None], 0.0), axis=1)
    chosen = jnp.any(member, axis=1)
    slot_rank = jnp.cumsum(chosen.astype(jnp.int32), axis=0) - 1
    slot_hot = chosen[:, :, None] & (
        slot_rank[:, :, None] == jnp.arange(CAP, dtype=jnp.int32)[None, None, :]
    )
    slot_low = slot_hot.astype(jnp.bfloat16)
    slot_wide = slot_hot.astype(jnp.float32)
    slot_rows = jnp.einsum(
        "tec,td->ecd", slot_low, normed, preferred_element_type=jnp.float32
    )
    weight_slots = jnp.einsum("tec,t->ec", slot_wide, loss_weight, precision=HIGHEST)
    share_slots = jnp.einsum("tec,te->ec", slot_wide, expert_share, precision=HIGHEST)
    upstream_slots = jnp.einsum(
        "tec,td->ecd", slot_low, upstream[0], preferred_element_type=jnp.float32
    )
    depth = expert_gate.shape[0]
    lanes = -(-depth // 128) * 128
    slots = jnp.concatenate([slot_rows, upstream_slots], axis=1)
    slots = slots.reshape(EW, 2 * CAP, dp_count, depth).transpose(0, 2, 1, 3)
    slots = jnp.pad(slots, ((0, 0), (0, 0), (0, 0), (0, lanes - depth)))
    own_part, other_part = in_place_experts(slots, expert_gate, expert_up, expert_down)
    both_parts = jnp.where(
        seq_index == 0, jnp.stack([own_part, other_part]), jnp.stack([other_part, own_part])
    )
    both_parts = lax.dynamic_slice_in_dim(both_parts, seq_index * CAP, CAP, 2)
    grad_share_slots = weight_slots * both_parts[:, dp_count, :, 0]
    grad_rows = (
        both_parts[:, :dp_count, :, :depth].transpose(0, 2, 1, 3).reshape(EW, CAP, D)
        * (weight_slots * share_slots)[:, :, None]
    )
    grad_normed_moe = jnp.einsum("tec,ecd->td", slot_wide, grad_rows, precision=HIGHEST)
    grad_share = jnp.einsum("tec,ec->te", slot_wide, grad_share_slots, precision=HIGHEST)
    grad_weights = jnp.sum(jnp.where(member, grad_share[:, None, :], 0.0), axis=2)
    grad_route = route_weights * (
        grad_weights - jnp.sum(route_weights * grad_weights, axis=1, keepdims=True)
    )
    grad_logits = jnp.sum(jnp.where(route_hot, grad_route[:, :, None], 0.0), axis=1).astype(
        jnp.bfloat16
    )
    grad_normed = (
        lax.dot_general(grad_logits, router, CONTRACT_LAST, preferred_element_type=jnp.float32)
        + grad_normed_moe
    )
    grad_unit = grad_normed * norm_gain[None, :]
    grad_mid = loss_weight[:, None] * upstream[0].astype(jnp.float32) + inv_rms * (
        grad_unit - unit_rows * jnp.mean(grad_unit * unit_rows, axis=1, keepdims=True)
    )
    grad_residual = grad_mid.astype(jnp.bfloat16)
    grad_attended = lax.dot_general(
        grad_residual, out_full, CONTRACT_LAST, preferred_element_type=jnp.float32
    ).astype(jnp.bfloat16)
    query_gradient, key_gradient, value_gradient, sink_gradient = head_grads(
        probs,
        reduced_probabilities,
        sink_probs,
        query_rows,
        key_tile_block,
        value_tile_block,
        grad_attended,
    )
    next_keys, next_values = (
        passed_along(key_gradient[:WINDOW].astype(jnp.bfloat16), "seq", -1).astype(jnp.float32),
        passed_along(value_gradient[:WINDOW].astype(jnp.bfloat16), "seq", -1).astype(jnp.float32),
    )
    own_key_grad = key_gradient[WINDOW:]
    own_value_grad = value_gradient[WINDOW:]
    split_at = tokens_here - WINDOW
    grad_key_rows = jnp.concatenate(
        [own_key_grad[:split_at], own_key_grad + next_keys], axis=0
    ).astype(jnp.bfloat16)
    grad_value_rows = jnp.concatenate(
        [own_value_grad[:split_at], own_value_grad + next_values], axis=0
    ).astype(jnp.bfloat16)
    grad_sinks = lax.psum(sink_gradient, ("seq", "dp"))
    return (
        query_gradient[None],
        grad_key_rows[None],
        grad_value_rows[None],
        grad_residual[None],
        grad_sinks,
    )


def solution(mesh):
    seq_count, dp_count = mesh.shape["seq"], mesh.shape["dp"]
    in_place = seq_count == EW and dp_count & (dp_count - 1) == 0
    return jax.shard_map(
        shards if in_place else general_shards,
        mesh=mesh,
        in_specs=(
            P("dp", "seq", None),
            P("dp", "seq", None),
            P("dp", "seq", None),
            P(),
            P("dp", "seq", None),
            P("dp", None),
            P(),
            P(),
            P("dp", "seq"),
            P("dp", "seq"),
            P("dp", "seq"),
            P("dp", "seq", None),
            P("dp"),
            P("dp"),
            P("dp", "seq"),
            P("dp", "seq", None),
        ),
        out_specs=(
            P("dp", "seq", None),
            P("dp", "seq", None),
            P("dp", "seq", None),
            P("dp", "seq", None),
            P(),
        ),
        check_vma=False,
    )
```

```python
import functools

import jax
import jax.numpy as jnp
from jax import lax
from jax.experimental import pallas as pl
from jax.experimental.pallas import tpu as pltpu
from jax.sharding import PartitionSpec as P

D = 2880
HEAD_SIZE = 64
WINDOW = 128
EXPERTS = 128
QUERY_HEADS = 32
KEY_VALUE_HEADS = 4
EW = 2
CAP = 4


NORM_EPS = 1e-05
GLU_SLOPE = 1.702
HIGHEST = lax.Precision.HIGHEST
CONTRACT_LAST = (((1,), (1,)), ((), ()))


def passed_along(value, axis, steps):
    count = lax.axis_size(axis)
    initial, last = (max(0, -steps), min(count, count - steps))
    return lax.ppermute(value, axis, [(source, source + steps) for source in range(initial, last)])


def glu_forward(gate_pre, up_pre):
    return ((up_pre + 1.0) * gate_pre * jax.nn.sigmoid(GLU_SLOPE * gate_pre)).astype(jnp.bfloat16)


def glu_grads(grad_act, gate_pre, up_pre):
    sigmoid_gate = jax.nn.sigmoid(GLU_SLOPE * gate_pre)
    grad_up = grad_act * (gate_pre * sigmoid_gate)
    grad_gate = (
        grad_act
        * (up_pre + 1.0)
        * (sigmoid_gate + GLU_SLOPE * gate_pre * sigmoid_gate * (1.0 - sigmoid_gate))
    )
    return (grad_gate, grad_up)


def head_scores(query_tile_block, key_tile_block, head_sink_logits, allowed):
    query_total_count = query_tile_block.shape[0]
    key_total_count = key_tile_block.shape[0]
    query_head_rows = query_tile_block.reshape(
        query_total_count, KEY_VALUE_HEADS, QUERY_HEADS // KEY_VALUE_HEADS, HEAD_SIZE
    )
    key_head_rows = key_tile_block.reshape(key_total_count, KEY_VALUE_HEADS, HEAD_SIZE)
    attention_scores = jnp.einsum(
        "baqj,eaj->aqbe", query_head_rows, key_head_rows, preferred_element_type=jnp.float32
    ) * HEAD_SIZE ** (-0.5)
    attention_scores = jnp.where(allowed[None, None], attention_scores, -1e30)
    sink_logit_column = head_sink_logits.reshape(KEY_VALUE_HEADS, QUERY_HEADS // KEY_VALUE_HEADS)[
        :, :, None
    ]
    largest = jnp.maximum(jnp.max(attention_scores, axis=3), sink_logit_column)
    raised = jnp.where(allowed[None, None], jnp.exp(attention_scores - largest[..., None]), 0.0)
    sink_raised = jnp.exp(sink_logit_column - largest)
    denominator = jnp.sum(raised, axis=3) + sink_raised
    return (raised / denominator[..., None], sink_raised / denominator)


def head_mix(reduced_probabilities, value_tile_block):
    key_total_count = value_tile_block.shape[0]
    value_head_rows = value_tile_block.reshape(key_total_count, KEY_VALUE_HEADS, HEAD_SIZE)
    mixed_output = jnp.einsum(
        "amlh,hai->lami", reduced_probabilities, value_head_rows, preferred_element_type=jnp.float32
    )
    return mixed_output.reshape(mixed_output.shape[0], QUERY_HEADS * HEAD_SIZE).astype(jnp.bfloat16)


def head_grads(
    probs,
    reduced_probabilities,
    sink_probs,
    query_tile_block,
    key_tile_block,
    value_tile_block,
    mixed_gradient,
):
    query_total_count = query_tile_block.shape[0]
    key_total_count = key_tile_block.shape[0]
    query_head_rows = query_tile_block.reshape(
        query_total_count, KEY_VALUE_HEADS, QUERY_HEADS // KEY_VALUE_HEADS, HEAD_SIZE
    )
    key_head_rows = key_tile_block.reshape(key_total_count, KEY_VALUE_HEADS, HEAD_SIZE)
    value_head_rows = value_tile_block.reshape(key_total_count, KEY_VALUE_HEADS, HEAD_SIZE)
    heads_gradient = mixed_gradient.reshape(
        query_total_count, KEY_VALUE_HEADS, QUERY_HEADS // KEY_VALUE_HEADS, HEAD_SIZE
    )
    probability_gradient = jnp.einsum(
        "baqj,eaj->aqbe", heads_gradient, value_head_rows, preferred_element_type=jnp.float32
    )
    spread = jnp.sum(probs * probability_gradient, axis=3)
    score_gradient = (probs * (probability_gradient - spread[..., None])).astype(jnp.bfloat16)
    head_scaling = HEAD_SIZE ** (-0.5)
    query_gradient = (
        jnp.einsum(
            "amlh,hai->lami", score_gradient, key_head_rows, preferred_element_type=jnp.float32
        )
        * head_scaling
    )
    key_gradient = (
        jnp.einsum(
            "ujko,kujm->oum", score_gradient, query_head_rows, preferred_element_type=jnp.float32
        )
        * head_scaling
    )
    value_gradient = jnp.einsum(
        "ujko,kujm->oum", reduced_probabilities, heads_gradient, preferred_element_type=jnp.float32
    )
    sink_gradient = -jnp.sum(sink_probs * spread, axis=2).reshape(QUERY_HEADS)
    return (
        query_gradient.reshape(query_total_count, QUERY_HEADS * HEAD_SIZE).astype(jnp.bfloat16),
        key_gradient.reshape(key_total_count, KEY_VALUE_HEADS * HEAD_SIZE),
        value_gradient.reshape(key_total_count, KEY_VALUE_HEADS * HEAD_SIZE),
        sink_gradient,
    )


def block_backward(grad_flat, gate_pre, up_pre, gate_full, up_full, down_full):
    grad_act = jnp.dot(grad_flat, down_full, preferred_element_type=jnp.float32)
    grad_gate, grad_up = glu_grads(grad_act, gate_pre, up_pre)
    grad_pair = jnp.concatenate([grad_gate, grad_up], axis=1).astype(jnp.bfloat16)
    weight_pair = jnp.concatenate([gate_full, up_full], axis=1)
    return lax.dot_general(
        grad_pair, weight_pair, CONTRACT_LAST, preferred_element_type=jnp.float32
    ).astype(jnp.bfloat16)


def general_shards(
    queries,
    key_rows,
    value_matrix,
    head_sink_logits,
    residual,
    out_weight,
    norm_gain,
    router,
    expert_gate,
    expert_up,
    expert_down,
    routes,
    group_ids,
    rewards,
    response_mask,
    upstream,
):
    seq_count = lax.axis_size("seq")
    dp_count = lax.axis_size("dp")
    seq_index = lax.axis_index("seq")
    query_rows = queries[0]
    own_keys = key_rows[0]
    own_values = value_matrix[0]
    tokens_here = query_rows.shape[0]
    pieces = seq_count // EW
    group_count = max(dp_count // 4, 1)
    all_tokens = dp_count * seq_count * tokens_here
    group_hot = (group_ids[0] == jnp.arange(group_count, dtype=jnp.int32)).astype(jnp.float32)
    reward = rewards[0].astype(jnp.float32)
    group_terms = (
        group_hot[:, None] * jnp.stack([jnp.ones_like(reward), reward, reward * reward])[None, :]
    )
    mask_wide = response_mask[0].astype(jnp.float32)
    local_count = jnp.sum(mask_wide)
    first_device = (seq_index == 0).astype(jnp.float32)
    group_totals, token_total = lax.psum((group_terms * first_device, local_count), ("seq", "dp"))
    group_sizes = group_totals[:, 0]
    group_means = group_totals[:, 1] / group_sizes
    group_spread = group_totals[:, 2] / group_sizes - group_means * group_means
    own_mean = jnp.sum(group_hot * group_means)
    own_spread = jnp.sum(group_hot * group_spread)
    advantage = (reward - own_mean) / jnp.sqrt(jnp.maximum(own_spread, 1.0))
    token_scale = -advantage * all_tokens / token_total
    loss_weight = token_scale * mask_wide
    halo_keys, halo_values = passed_along((own_keys, own_values), "seq", 1)
    key_tile_block = jnp.concatenate([halo_keys, own_keys], axis=0)
    value_tile_block = jnp.concatenate([halo_values, own_values], axis=0)
    row_index = jnp.arange(tokens_here, dtype=jnp.int32)[:, None]
    col_index = jnp.arange(WINDOW + tokens_here, dtype=jnp.int32)[None, :]
    allowed = (
        (col_index >= row_index + 1)
        & (col_index <= row_index + WINDOW)
        & ((col_index >= WINDOW) | (seq_index > 0))
    )
    probs, sink_probs = head_scores(query_rows, key_tile_block, head_sink_logits, allowed)
    reduced_probabilities = probs.astype(jnp.bfloat16)
    attended = head_mix(reduced_probabilities, value_tile_block)
    out_full = lax.all_gather(out_weight, "dp", axis=0, tiled=True)
    projected = jnp.dot(attended, out_full, preferred_element_type=jnp.float32)
    mid_rows = lax.optimization_barrier(
        (residual[0].astype(jnp.float32) + projected).astype(jnp.bfloat16)
    )
    mid_wide = mid_rows.astype(jnp.float32)
    inv_rms = lax.rsqrt(jnp.mean(mid_wide * mid_wide, axis=1, keepdims=True) + NORM_EPS)
    unit_rows = mid_wide * inv_rms
    normed = (unit_rows * norm_gain[None, :]).astype(jnp.bfloat16)
    logits = jnp.dot(normed, router, preferred_element_type=jnp.float32)
    route_hot = routes[0][:, :, None] == jnp.arange(EXPERTS, dtype=jnp.int32)[None, None, :]
    route_logits = jnp.sum(jnp.where(route_hot, logits[:, None, :], 0.0), axis=2)
    raised = jnp.exp(route_logits)
    route_weights = raised / jnp.sum(raised, axis=1, keepdims=True)
    member = route_hot[:, :, :EW]
    expert_share = jnp.sum(jnp.where(member, route_weights[:, :, None], 0.0), axis=1)
    chosen = jnp.any(member, axis=1)
    slot_rank = jnp.cumsum(chosen.astype(jnp.int32), axis=0) - 1
    slot_hot = chosen[:, :, None] & (
        slot_rank[:, :, None] == jnp.arange(CAP, dtype=jnp.int32)[None, None, :]
    )
    slot_low = slot_hot.astype(jnp.bfloat16)
    slot_wide = slot_hot.astype(jnp.float32)
    slot_rows = jnp.einsum(
        "tec,td->ecd", slot_low, normed, preferred_element_type=jnp.float32
    ).astype(jnp.bfloat16)
    outgoing = jnp.broadcast_to(slot_rows[:, None], (EW, pieces, CAP, D)).reshape(seq_count, CAP, D)
    upstream_slots = jnp.einsum(
        "tec,td->ecd", slot_low, upstream[0], preferred_element_type=jnp.float32
    )
    weight_slots = jnp.einsum("tec,t->ec", slot_wide, loss_weight, precision=HIGHEST)
    share_slots = jnp.einsum("tec,te->ec", slot_wide, expert_share, precision=HIGHEST)
    cot_slots = weight_slots[:, :, None] * upstream_slots
    grad_out = (share_slots[:, :, None] * cot_slots).astype(jnp.bfloat16)
    grad_outgoing = jnp.broadcast_to(grad_out[:, None], (EW, pieces, CAP, D)).reshape(
        seq_count, CAP, D
    )
    gate_full, up_full, down_full = (
        lax.all_gather(expert_gate, "dp", axis=0, tiled=True),
        lax.all_gather(expert_up, "dp", axis=0, tiled=True),
        lax.all_gather(expert_down, "dp", axis=0, tiled=True),
    )
    arrived = lax.all_to_all(outgoing, "seq", split_axis=0, concat_axis=0, tiled=True)
    senders = arrived.shape[0]
    items = arrived.shape[1]
    block_senders = arrived.shape[0]
    block_items = arrived.shape[1]
    flat_rows = arrived.reshape(block_senders * block_items, D)
    gate_pre = jnp.dot(flat_rows, gate_full, preferred_element_type=jnp.float32)
    up_pre = jnp.dot(flat_rows, up_full, preferred_element_type=jnp.float32)
    activation = glu_forward(gate_pre, up_pre)
    partial_out = lax.dot_general(
        activation, down_full, CONTRACT_LAST, preferred_element_type=jnp.float32
    ).astype(jnp.bfloat16)
    partial_out, gate_pre, up_pre = (
        partial_out.reshape(block_senders, block_items, D),
        gate_pre,
        up_pre,
    )
    back_out = lax.all_to_all(partial_out, "seq", split_axis=0, concat_axis=0, tiled=True)
    gate_held = gate_pre.reshape(senders, items, -1)
    up_held = up_pre.reshape(senders, items, -1)
    grad_arrived = lax.all_to_all(grad_outgoing, "seq", split_axis=0, concat_axis=0, tiled=True)
    grad_piece = block_backward(
        grad_arrived.reshape(seq_count * CAP, D),
        gate_held.reshape(seq_count * CAP, -1),
        up_held.reshape(seq_count * CAP, -1),
        gate_full,
        up_full,
        down_full,
    )
    grad_back = lax.all_to_all(
        grad_piece.reshape(seq_count, CAP, D), "seq", split_axis=0, concat_axis=0, tiled=True
    )
    expert_out = jnp.sum(back_out.reshape(EW, pieces, CAP, D).astype(jnp.float32), axis=1)
    grad_share_slots = jnp.sum(cot_slots * expert_out, axis=2)
    grad_rows = jnp.sum(grad_back.reshape(EW, pieces, CAP, D).astype(jnp.float32), axis=1)
    grad_normed_moe = jnp.einsum("tec,ecd->td", slot_wide, grad_rows, precision=HIGHEST)
    grad_share = jnp.einsum("tec,ec->te", slot_wide, grad_share_slots, precision=HIGHEST)
    grad_weights = jnp.sum(jnp.where(member, grad_share[:, None, :], 0.0), axis=2)
    grad_route = route_weights * (
        grad_weights - jnp.sum(route_weights * grad_weights, axis=1, keepdims=True)
    )
    grad_logits = jnp.sum(jnp.where(route_hot, grad_route[:, :, None], 0.0), axis=1).astype(
        jnp.bfloat16
    )
    grad_normed = (
        lax.dot_general(grad_logits, router, CONTRACT_LAST, preferred_element_type=jnp.float32)
        + grad_normed_moe
    )
    grad_unit = grad_normed * norm_gain[None, :]
    grad_mid = loss_weight[:, None] * upstream[0].astype(jnp.float32) + inv_rms * (
        grad_unit - unit_rows * jnp.mean(grad_unit * unit_rows, axis=1, keepdims=True)
    )
    grad_residual = grad_mid.astype(jnp.bfloat16)
    grad_attended = lax.dot_general(
        grad_residual, out_full, CONTRACT_LAST, preferred_element_type=jnp.float32
    ).astype(jnp.bfloat16)
    query_gradient, key_gradient, value_gradient, sink_gradient = head_grads(
        probs,
        reduced_probabilities,
        sink_probs,
        query_rows,
        key_tile_block,
        value_tile_block,
        grad_attended,
    )
    next_keys, next_values = (
        passed_along(key_gradient[:WINDOW].astype(jnp.bfloat16), "seq", -1).astype(jnp.float32),
        passed_along(value_gradient[:WINDOW].astype(jnp.bfloat16), "seq", -1).astype(jnp.float32),
    )
    own_key_grad = key_gradient[WINDOW:]
    own_value_grad = value_gradient[WINDOW:]
    split_at = tokens_here - WINDOW
    grad_key_rows = jnp.concatenate(
        [own_key_grad[:split_at], own_key_grad + next_keys], axis=0
    ).astype(jnp.bfloat16)
    grad_value_rows = jnp.concatenate(
        [own_value_grad[:split_at], own_value_grad + next_values], axis=0
    ).astype(jnp.bfloat16)
    grad_sinks = lax.psum(sink_gradient, ("seq", "dp"))
    return (
        query_gradient[None],
        grad_key_rows[None],
        grad_value_rows[None],
        grad_residual[None],
        grad_sinks,
    )


MESH = pl.DeviceIdType.MESH
MIB = 1 << 20


def halving_place(index, count):
    place, weight, rest = 0, count // 2, index
    while weight:
        place = place + lax.rem(rest, 2) * weight
        rest = lax.div(rest, 2)
        weight //= 2
    return place


def flipped(index, bit):
    return index + bit - 2 * bit * lax.rem(lax.div(index, bit), 2)


def expert_kernel(
    count,
    slots_ref,
    facts_ref,
    gate_ref,
    up_ref,
    down_ref,
    own_ref,
    other_ref,
    theirs,
    outgoing,
    arrived,
    sent,
    total,
    received,
    grads,
    back,
    seq_send,
    seq_recv,
    to_send,
    to_recv,
    halve_send,
    halve_recv,
    double_send,
    double_recv,
    back_send,
    back_recv,
):
    bits = count.bit_length() - 1
    me = lax.axis_index("dp")
    side = lax.axis_index("seq")
    far = 1 - side
    place = halving_place(me, count)
    depth = gate_ref.shape[0]
    hidden = gate_ref.shape[1]
    wide = 3 * hidden // 2

    barrier = pltpu.get_barrier_semaphore()
    pl.semaphore_signal(barrier, inc=1, device_id={"seq": far}, device_id_type=MESH)

    def greet(step, carry):
        pl.semaphore_signal(
            barrier, inc=1, device_id={"dp": lax.rem(me + step, count)}, device_id_type=MESH
        )
        return carry

    lax.fori_loop(1, count, greet, 0)
    pl.semaphore_wait(barrier, count)

    swap = pltpu.make_async_remote_copy(
        src_ref=slots_ref.at[far],
        dst_ref=theirs,
        send_sem=seq_send.at[0],
        recv_sem=seq_recv.at[0],
        device_id={"seq": far},
        device_id_type=MESH,
    )
    swap.start()
    back[...] = jnp.broadcast_to(facts_ref[...], back.shape)
    swap.wait()
    mine = slots_ref[side]
    came = theirs[...]
    first = jnp.where(side == 0, mine, came)
    second = jnp.where(side == 0, came, mine)
    outgoing[...] = jnp.concatenate(
        [first[:, :CAP], second[:, :CAP], first[:, CAP:], second[:, CAP:]], axis=1
    ).astype(jnp.bfloat16)

    def slice_copy(step):
        to = lax.rem(me + step, count)
        return pltpu.make_async_remote_copy(
            src_ref=outgoing.at[to],
            dst_ref=arrived.at[place],
            send_sem=to_send.at[step],
            recv_sem=to_recv.at[step],
            device_id={"dp": to},
            device_id_type=MESH,
        )

    def start_slice(step, carry):
        slice_copy(step).start()
        return carry

    def wait_slice(step, carry):
        slice_copy(step).wait()
        return carry

    lax.fori_loop(1, count, start_slice, 0)
    arrived[place] = outgoing[me]
    lax.fori_loop(1, count, wait_slice, 0)

    half = count // 2
    rows = EW * CAP
    tile = 512

    def products(start):
        block = arrived[pl.ds(start, half)].astype(jnp.float32)
        normed = block[:, :rows].reshape(half * rows, -1)[:, :depth].astype(jnp.bfloat16)
        upstream = block[:, rows:].reshape(half * rows, -1)[:, :depth].astype(jnp.bfloat16)

        def product(column):
            which, at = divmod(column, hidden)
            weight = (gate_ref, up_ref, down_ref)[which]
            return jnp.dot(
                upstream if which == 2 else normed,
                weight[:, at : at + tile],
                preferred_element_type=jnp.float32,
            ).reshape(half, rows, tile)

        for column in range(0, wide, tile):
            yield column, jnp.concatenate([product(column), product(wide + column)], axis=1)

    def halve_copy(stage):
        blocks = half >> stage
        return pltpu.make_async_remote_copy(
            src_ref=sent[stage],
            dst_ref=received[stage],
            send_sem=halve_send.at[stage],
            recv_sem=halve_recv.at[stage],
            device_id={"dp": flipped(me, 1 << stage)},
            device_id_type=MESH,
        )

    bit_of = [lax.rem(lax.div(me, 1 << stage), 2) for stage in range(bits)]
    for column, value in products((1 - bit_of[0]) * half):
        sent[0][:, :, column : column + tile] = value.astype(jnp.bfloat16)
    halve_copy(0).start()
    for column, value in products(bit_of[0] * half):
        total[:, :, column : column + tile] = value
    base = 0
    for stage in range(1, bits):
        blocks = half >> stage
        halve_copy(stage - 1).wait()
        away = (1 - bit_of[stage]) * blocks
        keep = bit_of[stage] * blocks
        sent[stage][...] = (
            total[pl.ds(base + away, blocks)]
            + received[stage - 1][pl.ds(away, blocks)].astype(jnp.float32)
        ).astype(jnp.bfloat16)
        halve_copy(stage).start()
        total[pl.ds(base + keep, blocks)] += received[stage - 1][pl.ds(keep, blocks)].astype(
            jnp.float32
        )
        base = base + keep
    halve_copy(bits - 1).wait()
    summed = total[base] + received[bits - 1][0].astype(jnp.float32)

    gate_pre = summed[:rows, :hidden]
    up_pre = jnp.concatenate([summed[:rows, hidden:], summed[rows:, : hidden // 2]], axis=1)
    grad_act = summed[rows:, hidden // 2 :]
    sigmoid_gate = 1.0 / (1.0 + jnp.exp(-GLU_SLOPE * gate_pre))
    gate_sigmoid = gate_pre * sigmoid_gate
    raised_up = up_pre + 1.0
    activation = (raised_up * gate_sigmoid).astype(jnp.bfloat16).astype(jnp.float32)
    share = jnp.sum(activation * grad_act, axis=1, keepdims=True)
    grad_up = grad_act * gate_sigmoid
    grad_gate = (
        grad_act * raised_up * (sigmoid_gate + GLU_SLOPE * gate_sigmoid * (1.0 - sigmoid_gate))
    )
    grads[place] = jnp.concatenate([grad_gate, grad_up], axis=0).astype(jnp.bfloat16)

    for stage in range(bits):
        blocks = 1 << stage
        start = place // blocks * blocks
        copy = pltpu.make_async_remote_copy(
            src_ref=grads.at[pl.ds(start, blocks)],
            dst_ref=grads.at[pl.ds(start, blocks)],
            send_sem=double_send.at[stage],
            recv_sem=double_recv.at[stage],
            device_id={"dp": flipped(me, half >> stage)},
            device_id_type=MESH,
        )
        copy.start()
        copy.wait()

    flat = grads[...].reshape(count * 2 * rows, hidden)
    contract = (((1,), (1,)), ((), ()))
    from_gate = lax.dot_general(flat, gate_ref[...], contract, preferred_element_type=jnp.float32)
    from_up = lax.dot_general(flat, up_ref[...], contract, preferred_element_type=jnp.float32)
    from_gate = from_gate.reshape(count, 2 * rows, depth)
    from_up = from_up.reshape(count, 2 * rows, depth)
    back[:, :, :depth] = from_gate[:, :rows] + from_up[:, rows:]

    def back_copy(step):
        to = lax.rem(me + step, count)
        return pltpu.make_async_remote_copy(
            src_ref=back.at[halving_place(to, count)],
            dst_ref=own_ref.at[me],
            send_sem=back_send.at[step],
            recv_sem=back_recv.at[step],
            device_id={"dp": to},
            device_id_type=MESH,
        )

    def start_back(step, carry):
        back_copy(step).start()
        return carry

    def wait_back(step, carry):
        back_copy(step).wait()
        return carry

    lax.fori_loop(1, count, start_back, 0)
    own_ref[me] = back[place]
    own_ref[count] = jnp.broadcast_to(share, own_ref.shape[1:])
    lax.fori_loop(1, count, wait_back, 0)
    last = pltpu.make_async_remote_copy(
        src_ref=own_ref,
        dst_ref=other_ref,
        send_sem=seq_send.at[1],
        recv_sem=seq_recv.at[1],
        device_id={"seq": far},
        device_id_type=MESH,
    )
    last.start()
    last.wait()


def in_place_experts(slots, facts, gate, up, down):
    count, lanes = slots.shape[1], slots.shape[3]
    bits = count.bit_length() - 1
    rows = EW * CAP
    hidden = gate.shape[1]
    wide = 3 * hidden // 2
    stages = [pltpu.VMEM((count >> (stage + 1), 2 * rows, wide), jnp.bfloat16) for stage in range(bits)]
    vmem = pl.BlockSpec(memory_space=pltpu.VMEM)
    dma = pltpu.SemaphoreType.DMA
    result = jax.ShapeDtypeStruct((count + 1, rows, lanes), jnp.float32)
    return pl.pallas_call(
        functools.partial(expert_kernel, count),
        out_shape=(result, result),
        in_specs=[vmem] * 5,
        out_specs=(vmem, vmem),
        scratch_shapes=[
            pltpu.VMEM((count, rows, lanes), jnp.float32),
            pltpu.VMEM((count, 2 * rows, lanes), jnp.bfloat16),
            pltpu.VMEM((count, 2 * rows, lanes), jnp.bfloat16),
            stages,
            pltpu.VMEM((count // 2, 2 * rows, wide), jnp.float32),
            stages,
            pltpu.VMEM((count, 2 * rows, hidden), jnp.bfloat16),
            pltpu.VMEM((count, rows, lanes), jnp.float32),
            dma((2,)),
            dma((2,)),
            dma((count,)),
            dma((count,)),
            dma((bits,)),
            dma((bits,)),
            dma((bits,)),
            dma((bits,)),
            dma((count,)),
            dma((count,)),
        ],
        compiler_params=pltpu.CompilerParams(
            collective_id=1, has_side_effects=True, vmem_limit_bytes=40 * MIB
        ),
        name="expert_kernel",
    )(slots, facts, gate, up, down)


def gather_kernel(
    count,
    weight_ref,
    full_ref,
    own_sem,
    line_send,
    line_recv,
    pair_send,
    pair_recv,
    side_send,
    side_recv,
    core_send,
    core_recv,
):
    line = count // 4
    waves = line - 1
    me = lax.axis_index("dp")
    side = lax.axis_index("seq")
    core, pair, spot = lax.rem(me, 2), lax.rem(lax.div(me, 2), 2), lax.div(me, 4)
    rows = weight_ref.shape[0]
    lone = rows * 3 // 128 * 16
    shared = rows - 2 * lone
    lone_start = pl.multiple_of(side * (lone + shared), 16)
    plane_start = pl.multiple_of(side * lone, 16)
    far_start = pl.multiple_of((1 - side) * (lone + shared), 16)
    chunks = ((lone_start, lone), (lone, shared))

    def index(spot, pair, core):
        return (spot * 2 + pair) * 2 + core

    def part(owner, start, size, own=False):
        if own:
            return weight_ref.at[pl.ds(start, size)]
        return full_ref.at[owner, pl.ds(start, size)]

    def remote(owner, own, start, size, send, recv, target):
        return pltpu.make_async_remote_copy(
            src_ref=part(owner, start, size, own),
            dst_ref=part(owner, start, size),
            send_sem=send,
            recv_sem=recv,
            device_id=target,
            device_id_type=MESH,
        )

    def shard_spot(way, wave):
        return spot - 1 - wave if way == 0 else spot + 1 + wave

    def arrives(way, wave):
        return spot - 1 - wave >= 0 if way == 0 else spot + 1 + wave < line

    def leaves(way, wave):
        if way == 0:
            return (spot + 1 < line) & (spot - wave >= 0)
        return (spot >= 1) & (spot + wave < line)

    def line_copy(way, wave, chunk):
        step = 1 if way == 0 else -1
        owner = index(spot - step * wave, pair, core)
        return remote(
            owner,
            wave == 0,
            *chunks[chunk],
            line_send.at[way, wave, chunk],
            line_recv.at[way, wave, chunk],
            {"dp": index(spot + step, pair, core)},
        )

    def slot(piece):
        return 0 if piece is None else 1 + 2 * piece[1] + piece[0]

    def owner_of(piece, other_pair):
        at = spot if piece is None else shard_spot(*piece)
        return index(at, 1 - pair if other_pair else pair, core)

    def pair_copy(piece, chunk):
        at = slot(piece)
        return remote(
            owner_of(piece, False),
            piece is None,
            *chunks[chunk],
            pair_send.at[at, chunk],
            pair_recv.at[at, chunk],
            {"dp": index(spot, 1 - pair, core)},
        )

    def side_copy(piece, other_pair):
        at = slot(piece)
        return remote(
            owner_of(piece, other_pair),
            False,
            lone_start,
            lone,
            side_send.at[other_pair, at],
            side_recv.at[other_pair, at],
            {"seq": 1 - side},
        )

    def core_copy(piece, other_pair, from_side):
        at = slot(piece)
        if piece is None and other_pair == 0:
            start, size = 0, rows
        elif from_side:
            start, size = far_start, lone
        else:
            start, size = plane_start, lone + shared
        return remote(
            owner_of(piece, other_pair),
            piece is None and other_pair == 0,
            start,
            size,
            core_send.at[from_side, other_pair, at],
            core_recv.at[from_side, other_pair, at],
            {"dp": index(spot, pair, 1 - core)},
        )

    def held(piece, action):
        if piece is None:
            action()
        else:
            pl.when(arrives(*piece))(action)

    barrier = pltpu.get_barrier_semaphore()

    def greet(target):
        pl.semaphore_signal(barrier, inc=1, device_id=target, device_id_type=MESH)

    greet({"seq": 1 - side})
    greet({"dp": index(spot, 1 - pair, core)})
    greet({"dp": index(spot, pair, 1 - core)})
    for way, step in ((0, 1), (1, -1)):

        @pl.when(leaves(way, 0))
        def _(step=step):
            greet({"dp": index(spot + step, pair, core)})

    neighbours = leaves(0, 0).astype(jnp.int32) + leaves(1, 0).astype(jnp.int32)
    pl.semaphore_wait(barrier, 3 + neighbours)

    keep = pltpu.make_async_copy(weight_ref, full_ref.at[me], own_sem)
    for chunk in (0, 1):
        for way in (0, 1):

            @pl.when(leaves(way, 0))
            def _(way=way, chunk=chunk):
                line_copy(way, 0, chunk).start()

        pair_copy(None, chunk).start()
    core_copy(None, 0, 0).start()
    keep.start()

    def line_step(wave):
        for chunk in (0, 1):
            for way in (0, 1):

                @pl.when(arrives(way, wave))
                def _(way=way, chunk=chunk):
                    piece = (way, wave)
                    line_copy(way, wave, chunk).wait_recv()
                    if wave + 1 < waves:

                        @pl.when(leaves(way, wave + 1))
                        def _():
                            line_copy(way, wave + 1, chunk).start()

                    pair_copy(piece, chunk).start()
                    if chunk == 0:
                        side_copy(piece, 0).start()
                    else:
                        core_copy(piece, 0, 0).start()

    def pair_step(pieces):
        for chunk in (0, 1):
            for piece in pieces:

                def arrive(piece=piece, chunk=chunk):
                    pair_copy(piece, chunk).wait_recv()
                    if chunk == 0:
                        side_copy(piece, 1).start()
                    else:
                        core_copy(piece, 1, 0).start()

                held(piece, arrive)

    def side_step(pieces, other_pair):
        for piece in pieces:

            def arrive(piece=piece):
                side_copy(piece, other_pair).wait_recv()
                core_copy(piece, other_pair, 1).start()

            held(piece, arrive)

    waved = [[(0, wave), (1, wave)] for wave in range(waves)]
    ordered = [[None]] + waved
    for wave in range(waves):
        line_step(wave)
        pair_step(ordered[wave])
        if wave:
            side_step(waved[wave - 1], 0)
            side_step(ordered[wave - 1], 1)
    pair_step(ordered[waves])
    side_step(waved[waves - 1], 0)
    side_step(ordered[waves - 1], 1)
    side_step(ordered[waves], 1)

    keep.wait()
    for piece in [None] + sum(waved, []):

        def finish(piece=piece):
            for chunk in (0, 1):
                pair_copy(piece, chunk).wait_send()
            for other_pair in (0, 1):
                core_copy(piece, other_pair, 0).wait()
                if piece is not None or other_pair:
                    side_copy(piece, other_pair).wait_send()
                    core_copy(piece, other_pair, 1).wait()

        held(piece, finish)
    for wave in range(waves):
        for way in (0, 1):

            @pl.when(leaves(way, wave))
            def _(way=way, wave=wave):
                for chunk in (0, 1):
                    line_copy(way, wave, chunk).wait_send()


def gathered(weight, count):
    waves = count // 4 - 1
    slots = 1 + 2 * waves
    dma = pltpu.SemaphoreType.DMA
    full = pl.pallas_call(
        functools.partial(gather_kernel, count),
        out_shape=jax.ShapeDtypeStruct((count,) + weight.shape, weight.dtype),
        in_specs=[pl.BlockSpec(memory_space=pl.ANY)],
        out_specs=pl.BlockSpec(memory_space=pl.ANY),
        scratch_shapes=[
            dma,
            dma((2, waves, 2)),
            dma((2, waves, 2)),
            dma((slots, 2)),
            dma((slots, 2)),
            dma((2, slots)),
            dma((2, slots)),
            dma((2, 2, slots)),
            dma((2, 2, slots)),
        ],
        compiler_params=pltpu.CompilerParams(collective_id=2, has_side_effects=True),
        name="gather_kernel",
    )(weight)
    return full.reshape(count * weight.shape[0], weight.shape[1])


def tail_kernel(
    count, sinks_ref, halo_ref, sums_ref, came_ref, parts, half, far_half, dp_send, dp_recv, seq_send, seq_recv
):
    me = lax.axis_index("dp")
    far = 1 - lax.axis_index("seq")
    barrier = pltpu.get_barrier_semaphore()
    pl.semaphore_signal(barrier, inc=1, device_id={"seq": far}, device_id_type=MESH)

    def greet(step, carry):
        pl.semaphore_signal(
            barrier, inc=1, device_id={"dp": lax.rem(me + step, count)}, device_id_type=MESH
        )
        return carry

    lax.fori_loop(1, count, greet, 0)
    pl.semaphore_wait(barrier, count)

    def across(source, target, at):
        return pltpu.make_async_remote_copy(
            src_ref=source,
            dst_ref=target,
            send_sem=seq_send.at[at],
            recv_sem=seq_recv.at[at],
            device_id={"seq": far},
            device_id_type=MESH,
        )

    def part_copy(step):
        return pltpu.make_async_remote_copy(
            src_ref=sinks_ref,
            dst_ref=parts.at[me],
            send_sem=dp_send.at[step],
            recv_sem=dp_recv.at[step],
            device_id={"dp": lax.rem(me + step, count)},
            device_id_type=MESH,
        )

    def start_part(step, carry):
        part_copy(step).start()
        return carry

    def wait_part(step, carry):
        part_copy(step).wait()
        return carry

    lax.fori_loop(1, count, start_part, 0)
    halo = across(halo_ref, came_ref, 0)
    halo.start()
    parts[me] = sinks_ref[...]
    lax.fori_loop(1, count, wait_part, 0)
    half[...] = jnp.sum(parts[...], axis=0)
    swap = across(half, far_half, 1)
    swap.start()
    swap.wait()
    sums_ref[...] = half[...] + far_half[...]
    halo.wait()


def tail_exchange(sinks, halo, count):
    vmem = pl.BlockSpec(memory_space=pltpu.VMEM)
    dma = pltpu.SemaphoreType.DMA
    tile = (8, 128)
    row = jnp.zeros(tile, jnp.float32).at[0, : sinks.shape[0]].set(sinks)
    sums, came = pl.pallas_call(
        functools.partial(tail_kernel, count),
        out_shape=(
            jax.ShapeDtypeStruct(tile, jnp.float32),
            jax.ShapeDtypeStruct(halo.shape, halo.dtype),
        ),
        in_specs=[vmem] * 2,
        out_specs=(vmem, vmem),
        scratch_shapes=[
            pltpu.VMEM((count,) + tile, jnp.float32),
            pltpu.VMEM(tile, jnp.float32),
            pltpu.VMEM(tile, jnp.float32),
            dma((count,)),
            dma((count,)),
            dma((2,)),
            dma((2,)),
        ],
        compiler_params=pltpu.CompilerParams(collective_id=3, has_side_effects=True),
        name="tail_kernel",
    )(row, halo)
    return sums[0, : sinks.shape[0]], came


def shards(
    queries,
    key_rows,
    value_matrix,
    head_sink_logits,
    residual,
    out_weight,
    norm_gain,
    router,
    expert_gate,
    expert_up,
    expert_down,
    routes,
    group_ids,
    rewards,
    response_mask,
    upstream,
):
    seq_count = lax.axis_size("seq")
    dp_count = lax.axis_size("dp")
    seq_index = lax.axis_index("seq")
    query_rows = queries[0]
    own_keys = key_rows[0]
    own_values = value_matrix[0]
    tokens_here = query_rows.shape[0]
    group_count = max(dp_count // 4, 1)
    all_tokens = dp_count * seq_count * tokens_here
    group_hot = (group_ids[0] == jnp.arange(group_count, dtype=jnp.int32)).astype(jnp.float32)
    reward = rewards[0].astype(jnp.float32)
    group_terms = (
        group_hot[:, None] * jnp.stack([jnp.ones_like(reward), reward, reward * reward])[None, :]
    )
    mask_wide = response_mask[0].astype(jnp.float32)
    local_count = jnp.sum(mask_wide)
    first_device = (seq_index == 0).astype(jnp.float32)
    halo_keys, halo_values = passed_along((own_keys, own_values), "seq", 1)
    key_tile_block = jnp.concatenate([halo_keys, own_keys], axis=0)
    value_tile_block = jnp.concatenate([halo_values, own_values], axis=0)
    row_index = jnp.arange(tokens_here, dtype=jnp.int32)[:, None]
    col_index = jnp.arange(WINDOW + tokens_here, dtype=jnp.int32)[None, :]
    allowed = (
        (col_index >= row_index + 1)
        & (col_index <= row_index + WINDOW)
        & ((col_index >= WINDOW) | (seq_index > 0))
    )
    probs, sink_probs = head_scores(query_rows, key_tile_block, head_sink_logits, allowed)
    reduced_probabilities = probs.astype(jnp.bfloat16)
    attended = head_mix(reduced_probabilities, value_tile_block)
    out_full = gathered(out_weight, dp_count)
    projected = jnp.dot(attended, out_full, preferred_element_type=jnp.float32)
    mid_rows = lax.optimization_barrier(
        (residual[0].astype(jnp.float32) + projected).astype(jnp.bfloat16)
    )
    mid_wide = mid_rows.astype(jnp.float32)
    inv_rms = lax.rsqrt(jnp.mean(mid_wide * mid_wide, axis=1, keepdims=True) + NORM_EPS)
    unit_rows = mid_wide * inv_rms
    normed = (unit_rows * norm_gain[None, :]).astype(jnp.bfloat16)
    logits = jnp.dot(normed, router, preferred_element_type=jnp.float32)
    route_hot = routes[0][:, :, None] == jnp.arange(EXPERTS, dtype=jnp.int32)[None, None, :]
    route_logits = jnp.sum(jnp.where(route_hot, logits[:, None, :], 0.0), axis=2)
    raised = jnp.exp(route_logits)
    route_weights = raised / jnp.sum(raised, axis=1, keepdims=True)
    member = route_hot[:, :, :EW]
    expert_share = jnp.sum(jnp.where(member, route_weights[:, :, None], 0.0), axis=1)
    chosen = jnp.any(member, axis=1)
    slot_rank = jnp.cumsum(chosen.astype(jnp.int32), axis=0) - 1
    slot_hot = chosen[:, :, None] & (
        slot_rank[:, :, None] == jnp.arange(CAP, dtype=jnp.int32)[None, None, :]
    )
    slot_low = slot_hot.astype(jnp.bfloat16)
    slot_wide = slot_hot.astype(jnp.float32)
    slot_rows = jnp.einsum(
        "tec,td->ecd", slot_low, normed, preferred_element_type=jnp.float32
    )
    share_slots = jnp.einsum("tec,te->ec", slot_wide, expert_share, precision=HIGHEST)
    upstream_slots = jnp.einsum(
        "tec,td->ecd", slot_low, upstream[0], preferred_element_type=jnp.float32
    )
    depth = expert_gate.shape[0]
    lanes = -(-depth // 128) * 128
    slots = jnp.concatenate([slot_rows, upstream_slots], axis=1)
    slots = slots.reshape(EW, 2 * CAP, dp_count, depth).transpose(0, 2, 1, 3)
    facts = jnp.concatenate([(group_terms * first_device).reshape(-1), local_count[None]])
    lanes = max(lanes, -(-(depth + facts.shape[0]) // 128) * 128)
    slots = jnp.pad(slots, ((0, 0), (0, 0), (0, 0), (0, lanes - depth)))
    facts = jnp.pad(facts, (depth, lanes - depth - facts.shape[0]))
    facts = jnp.broadcast_to(facts, (EW * CAP, lanes))
    own_part, other_part = in_place_experts(slots, facts, expert_gate, expert_up, expert_down)
    totals = jnp.sum(own_part[:dp_count, 0] + other_part[:dp_count, 0], axis=0)[depth:]
    group_totals = totals[: group_terms.size].reshape(group_terms.shape)
    token_total = totals[group_terms.size]
    group_sizes = group_totals[:, 0]
    group_means = group_totals[:, 1] / group_sizes
    group_spread = group_totals[:, 2] / group_sizes - group_means * group_means
    own_mean = jnp.sum(group_hot * group_means)
    own_spread = jnp.sum(group_hot * group_spread)
    advantage = (reward - own_mean) / jnp.sqrt(jnp.maximum(own_spread, 1.0))
    token_scale = -advantage * all_tokens / token_total
    loss_weight = token_scale * mask_wide
    weight_slots = jnp.einsum("tec,t->ec", slot_wide, loss_weight, precision=HIGHEST)
    both_parts = jnp.where(
        seq_index == 0, jnp.stack([own_part, other_part]), jnp.stack([other_part, own_part])
    )
    both_parts = lax.dynamic_slice_in_dim(both_parts, seq_index * CAP, CAP, 2)
    grad_share_slots = weight_slots * both_parts[:, dp_count, :, 0]
    grad_rows = (
        both_parts[:, :dp_count, :, :depth].transpose(0, 2, 1, 3).reshape(EW, CAP, D)
        * (weight_slots * share_slots)[:, :, None]
    )
    grad_normed_moe = jnp.einsum("tec,ecd->td", slot_wide, grad_rows, precision=HIGHEST)
    grad_share = jnp.einsum("tec,ec->te", slot_wide, grad_share_slots, precision=HIGHEST)
    grad_weights = jnp.sum(jnp.where(member, grad_share[:, None, :], 0.0), axis=2)
    grad_route = route_weights * (
        grad_weights - jnp.sum(route_weights * grad_weights, axis=1, keepdims=True)
    )
    grad_logits = jnp.sum(jnp.where(route_hot, grad_route[:, :, None], 0.0), axis=1).astype(
        jnp.bfloat16
    )
    grad_normed = (
        lax.dot_general(grad_logits, router, CONTRACT_LAST, preferred_element_type=jnp.float32)
        + grad_normed_moe
    )
    grad_unit = grad_normed * norm_gain[None, :]
    grad_mid = loss_weight[:, None] * upstream[0].astype(jnp.float32) + inv_rms * (
        grad_unit - unit_rows * jnp.mean(grad_unit * unit_rows, axis=1, keepdims=True)
    )
    grad_residual = grad_mid.astype(jnp.bfloat16)
    grad_attended = lax.dot_general(
        grad_residual, out_full, CONTRACT_LAST, preferred_element_type=jnp.float32
    ).astype(jnp.bfloat16)
    query_gradient, key_gradient, value_gradient, sink_gradient = head_grads(
        probs,
        reduced_probabilities,
        sink_probs,
        query_rows,
        key_tile_block,
        value_tile_block,
        grad_attended,
    )
    halo = jnp.concatenate([key_gradient[:WINDOW], value_gradient[:WINDOW]], axis=0)
    grad_sinks, came = tail_exchange(sink_gradient, halo.astype(jnp.bfloat16), dp_count)
    came = jnp.where(seq_index + 1 < seq_count, came.astype(jnp.float32), 0.0)
    next_keys, next_values = came[:WINDOW], came[WINDOW:]
    own_key_grad = key_gradient[WINDOW:]
    own_value_grad = value_gradient[WINDOW:]
    split_at = tokens_here - WINDOW
    grad_key_rows = jnp.concatenate(
        [own_key_grad[:split_at], own_key_grad + next_keys], axis=0
    ).astype(jnp.bfloat16)
    grad_value_rows = jnp.concatenate(
        [own_value_grad[:split_at], own_value_grad + next_values], axis=0
    ).astype(jnp.bfloat16)
    return (
        query_gradient[None],
        grad_key_rows[None],
        grad_value_rows[None],
        grad_residual[None],
        grad_sinks,
    )


def solution(mesh):
    seq_count, dp_count = mesh.shape["seq"], mesh.shape["dp"]
    in_place = seq_count == EW and dp_count >= 8 and dp_count & (dp_count - 1) == 0
    return jax.shard_map(
        shards if in_place else general_shards,
        mesh=mesh,
        in_specs=(
            P("dp", "seq", None),
            P("dp", "seq", None),
            P("dp", "seq", None),
            P(),
            P("dp", "seq", None),
            P("dp", None),
            P(),
            P(),
            P("dp", "seq"),
            P("dp", "seq"),
            P("dp", "seq"),
            P("dp", "seq", None),
            P("dp"),
            P("dp"),
            P("dp", "seq"),
            P("dp", "seq", None),
        ),
        out_specs=(
            P("dp", "seq", None),
            P("dp", "seq", None),
            P("dp", "seq", None),
            P("dp", "seq", None),
            P(),
        ),
        check_vma=False,
    )
```

```python
import functools

import jax
import jax.numpy as jnp
from jax import lax
from jax.experimental import pallas as pl
from jax.experimental.pallas import tpu as pltpu
from jax.sharding import PartitionSpec as P

D = 2880
HEAD_SIZE = 64
WINDOW = 128
EXPERTS = 128
QUERY_HEADS = 32
KEY_VALUE_HEADS = 4
EW = 2
CAP = 4


NORM_EPS = 1e-05
GLU_SLOPE = 1.702
HIGHEST = lax.Precision.HIGHEST
CONTRACT_LAST = (((1,), (1,)), ((), ()))


def passed_along(value, axis, steps):
    count = lax.axis_size(axis)
    initial, last = (max(0, -steps), min(count, count - steps))
    return lax.ppermute(value, axis, [(source, source + steps) for source in range(initial, last)])


def glu_forward(gate_pre, up_pre):
    return ((up_pre + 1.0) * gate_pre * jax.nn.sigmoid(GLU_SLOPE * gate_pre)).astype(jnp.bfloat16)


def glu_grads(grad_act, gate_pre, up_pre):
    sigmoid_gate = jax.nn.sigmoid(GLU_SLOPE * gate_pre)
    grad_up = grad_act * (gate_pre * sigmoid_gate)
    grad_gate = (
        grad_act
        * (up_pre + 1.0)
        * (sigmoid_gate + GLU_SLOPE * gate_pre * sigmoid_gate * (1.0 - sigmoid_gate))
    )
    return (grad_gate, grad_up)


def head_scores(query_tile_block, key_tile_block, head_sink_logits, allowed):
    query_total_count = query_tile_block.shape[0]
    key_total_count = key_tile_block.shape[0]
    query_head_rows = query_tile_block.reshape(
        query_total_count, KEY_VALUE_HEADS, QUERY_HEADS // KEY_VALUE_HEADS, HEAD_SIZE
    )
    key_head_rows = key_tile_block.reshape(key_total_count, KEY_VALUE_HEADS, HEAD_SIZE)
    attention_scores = jnp.einsum(
        "baqj,eaj->aqbe", query_head_rows, key_head_rows, preferred_element_type=jnp.float32
    ) * HEAD_SIZE ** (-0.5)
    attention_scores = jnp.where(allowed[None, None], attention_scores, -1e30)
    sink_logit_column = head_sink_logits.reshape(KEY_VALUE_HEADS, QUERY_HEADS // KEY_VALUE_HEADS)[
        :, :, None
    ]
    largest = jnp.maximum(jnp.max(attention_scores, axis=3), sink_logit_column)
    raised = jnp.where(allowed[None, None], jnp.exp(attention_scores - largest[..., None]), 0.0)
    sink_raised = jnp.exp(sink_logit_column - largest)
    denominator = jnp.sum(raised, axis=3) + sink_raised
    return (raised / denominator[..., None], sink_raised / denominator)


def head_mix(reduced_probabilities, value_tile_block):
    key_total_count = value_tile_block.shape[0]
    value_head_rows = value_tile_block.reshape(key_total_count, KEY_VALUE_HEADS, HEAD_SIZE)
    mixed_output = jnp.einsum(
        "amlh,hai->lami", reduced_probabilities, value_head_rows, preferred_element_type=jnp.float32
    )
    return mixed_output.reshape(mixed_output.shape[0], QUERY_HEADS * HEAD_SIZE).astype(jnp.bfloat16)


def head_grads(
    probs,
    reduced_probabilities,
    sink_probs,
    query_tile_block,
    key_tile_block,
    value_tile_block,
    mixed_gradient,
):
    query_total_count = query_tile_block.shape[0]
    key_total_count = key_tile_block.shape[0]
    query_head_rows = query_tile_block.reshape(
        query_total_count, KEY_VALUE_HEADS, QUERY_HEADS // KEY_VALUE_HEADS, HEAD_SIZE
    )
    key_head_rows = key_tile_block.reshape(key_total_count, KEY_VALUE_HEADS, HEAD_SIZE)
    value_head_rows = value_tile_block.reshape(key_total_count, KEY_VALUE_HEADS, HEAD_SIZE)
    heads_gradient = mixed_gradient.reshape(
        query_total_count, KEY_VALUE_HEADS, QUERY_HEADS // KEY_VALUE_HEADS, HEAD_SIZE
    )
    probability_gradient = jnp.einsum(
        "baqj,eaj->aqbe", heads_gradient, value_head_rows, preferred_element_type=jnp.float32
    )
    spread = jnp.sum(probs * probability_gradient, axis=3)
    score_gradient = (probs * (probability_gradient - spread[..., None])).astype(jnp.bfloat16)
    head_scaling = HEAD_SIZE ** (-0.5)
    query_gradient = (
        jnp.einsum(
            "amlh,hai->lami", score_gradient, key_head_rows, preferred_element_type=jnp.float32
        )
        * head_scaling
    )
    key_gradient = (
        jnp.einsum(
            "ujko,kujm->oum", score_gradient, query_head_rows, preferred_element_type=jnp.float32
        )
        * head_scaling
    )
    value_gradient = jnp.einsum(
        "ujko,kujm->oum", reduced_probabilities, heads_gradient, preferred_element_type=jnp.float32
    )
    sink_gradient = -jnp.sum(sink_probs * spread, axis=2).reshape(QUERY_HEADS)
    return (
        query_gradient.reshape(query_total_count, QUERY_HEADS * HEAD_SIZE).astype(jnp.bfloat16),
        key_gradient.reshape(key_total_count, KEY_VALUE_HEADS * HEAD_SIZE),
        value_gradient.reshape(key_total_count, KEY_VALUE_HEADS * HEAD_SIZE),
        sink_gradient,
    )


def block_backward(grad_flat, gate_pre, up_pre, gate_full, up_full, down_full):
    grad_act = jnp.dot(grad_flat, down_full, preferred_element_type=jnp.float32)
    grad_gate, grad_up = glu_grads(grad_act, gate_pre, up_pre)
    grad_pair = jnp.concatenate([grad_gate, grad_up], axis=1).astype(jnp.bfloat16)
    weight_pair = jnp.concatenate([gate_full, up_full], axis=1)
    return lax.dot_general(
        grad_pair, weight_pair, CONTRACT_LAST, preferred_element_type=jnp.float32
    ).astype(jnp.bfloat16)


def general_shards(
    queries,
    key_rows,
    value_matrix,
    head_sink_logits,
    residual,
    out_weight,
    norm_gain,
    router,
    expert_gate,
    expert_up,
    expert_down,
    routes,
    group_ids,
    rewards,
    response_mask,
    upstream,
):
    seq_count = lax.axis_size("seq")
    dp_count = lax.axis_size("dp")
    seq_index = lax.axis_index("seq")
    query_rows = queries[0]
    own_keys = key_rows[0]
    own_values = value_matrix[0]
    tokens_here = query_rows.shape[0]
    pieces = seq_count // EW
    group_count = max(dp_count // 4, 1)
    all_tokens = dp_count * seq_count * tokens_here
    group_hot = (group_ids[0] == jnp.arange(group_count, dtype=jnp.int32)).astype(jnp.float32)
    reward = rewards[0].astype(jnp.float32)
    group_terms = (
        group_hot[:, None] * jnp.stack([jnp.ones_like(reward), reward, reward * reward])[None, :]
    )
    mask_wide = response_mask[0].astype(jnp.float32)
    local_count = jnp.sum(mask_wide)
    first_device = (seq_index == 0).astype(jnp.float32)
    group_totals, token_total = lax.psum((group_terms * first_device, local_count), ("seq", "dp"))
    group_sizes = group_totals[:, 0]
    group_means = group_totals[:, 1] / group_sizes
    group_spread = group_totals[:, 2] / group_sizes - group_means * group_means
    own_mean = jnp.sum(group_hot * group_means)
    own_spread = jnp.sum(group_hot * group_spread)
    advantage = (reward - own_mean) / jnp.sqrt(jnp.maximum(own_spread, 1.0))
    token_scale = -advantage * all_tokens / token_total
    loss_weight = token_scale * mask_wide
    halo_keys, halo_values = passed_along((own_keys, own_values), "seq", 1)
    key_tile_block = jnp.concatenate([halo_keys, own_keys], axis=0)
    value_tile_block = jnp.concatenate([halo_values, own_values], axis=0)
    row_index = jnp.arange(tokens_here, dtype=jnp.int32)[:, None]
    col_index = jnp.arange(WINDOW + tokens_here, dtype=jnp.int32)[None, :]
    allowed = (
        (col_index >= row_index + 1)
        & (col_index <= row_index + WINDOW)
        & ((col_index >= WINDOW) | (seq_index > 0))
    )
    probs, sink_probs = head_scores(query_rows, key_tile_block, head_sink_logits, allowed)
    reduced_probabilities = probs.astype(jnp.bfloat16)
    attended = head_mix(reduced_probabilities, value_tile_block)
    out_full = lax.all_gather(out_weight, "dp", axis=0, tiled=True)
    projected = jnp.dot(attended, out_full, preferred_element_type=jnp.float32)
    mid_rows = lax.optimization_barrier(
        (residual[0].astype(jnp.float32) + projected).astype(jnp.bfloat16)
    )
    mid_wide = mid_rows.astype(jnp.float32)
    inv_rms = lax.rsqrt(jnp.mean(mid_wide * mid_wide, axis=1, keepdims=True) + NORM_EPS)
    unit_rows = mid_wide * inv_rms
    normed = (unit_rows * norm_gain[None, :]).astype(jnp.bfloat16)
    logits = jnp.dot(normed, router, preferred_element_type=jnp.float32)
    route_hot = routes[0][:, :, None] == jnp.arange(EXPERTS, dtype=jnp.int32)[None, None, :]
    route_logits = jnp.sum(jnp.where(route_hot, logits[:, None, :], 0.0), axis=2)
    raised = jnp.exp(route_logits)
    route_weights = raised / jnp.sum(raised, axis=1, keepdims=True)
    member = route_hot[:, :, :EW]
    expert_share = jnp.sum(jnp.where(member, route_weights[:, :, None], 0.0), axis=1)
    chosen = jnp.any(member, axis=1)
    slot_rank = jnp.cumsum(chosen.astype(jnp.int32), axis=0) - 1
    slot_hot = chosen[:, :, None] & (
        slot_rank[:, :, None] == jnp.arange(CAP, dtype=jnp.int32)[None, None, :]
    )
    slot_low = slot_hot.astype(jnp.bfloat16)
    slot_wide = slot_hot.astype(jnp.float32)
    slot_rows = jnp.einsum(
        "tec,td->ecd", slot_low, normed, preferred_element_type=jnp.float32
    ).astype(jnp.bfloat16)
    outgoing = jnp.broadcast_to(slot_rows[:, None], (EW, pieces, CAP, D)).reshape(seq_count, CAP, D)
    upstream_slots = jnp.einsum(
        "tec,td->ecd", slot_low, upstream[0], preferred_element_type=jnp.float32
    )
    weight_slots = jnp.einsum("tec,t->ec", slot_wide, loss_weight, precision=HIGHEST)
    share_slots = jnp.einsum("tec,te->ec", slot_wide, expert_share, precision=HIGHEST)
    cot_slots = weight_slots[:, :, None] * upstream_slots
    grad_out = (share_slots[:, :, None] * cot_slots).astype(jnp.bfloat16)
    grad_outgoing = jnp.broadcast_to(grad_out[:, None], (EW, pieces, CAP, D)).reshape(
        seq_count, CAP, D
    )
    gate_full, up_full, down_full = (
        lax.all_gather(expert_gate, "dp", axis=0, tiled=True),
        lax.all_gather(expert_up, "dp", axis=0, tiled=True),
        lax.all_gather(expert_down, "dp", axis=0, tiled=True),
    )
    arrived = lax.all_to_all(outgoing, "seq", split_axis=0, concat_axis=0, tiled=True)
    senders = arrived.shape[0]
    items = arrived.shape[1]
    block_senders = arrived.shape[0]
    block_items = arrived.shape[1]
    flat_rows = arrived.reshape(block_senders * block_items, D)
    gate_pre = jnp.dot(flat_rows, gate_full, preferred_element_type=jnp.float32)
    up_pre = jnp.dot(flat_rows, up_full, preferred_element_type=jnp.float32)
    activation = glu_forward(gate_pre, up_pre)
    partial_out = lax.dot_general(
        activation, down_full, CONTRACT_LAST, preferred_element_type=jnp.float32
    ).astype(jnp.bfloat16)
    partial_out, gate_pre, up_pre = (
        partial_out.reshape(block_senders, block_items, D),
        gate_pre,
        up_pre,
    )
    back_out = lax.all_to_all(partial_out, "seq", split_axis=0, concat_axis=0, tiled=True)
    gate_held = gate_pre.reshape(senders, items, -1)
    up_held = up_pre.reshape(senders, items, -1)
    grad_arrived = lax.all_to_all(grad_outgoing, "seq", split_axis=0, concat_axis=0, tiled=True)
    grad_piece = block_backward(
        grad_arrived.reshape(seq_count * CAP, D),
        gate_held.reshape(seq_count * CAP, -1),
        up_held.reshape(seq_count * CAP, -1),
        gate_full,
        up_full,
        down_full,
    )
    grad_back = lax.all_to_all(
        grad_piece.reshape(seq_count, CAP, D), "seq", split_axis=0, concat_axis=0, tiled=True
    )
    expert_out = jnp.sum(back_out.reshape(EW, pieces, CAP, D).astype(jnp.float32), axis=1)
    grad_share_slots = jnp.sum(cot_slots * expert_out, axis=2)
    grad_rows = jnp.sum(grad_back.reshape(EW, pieces, CAP, D).astype(jnp.float32), axis=1)
    grad_normed_moe = jnp.einsum("tec,ecd->td", slot_wide, grad_rows, precision=HIGHEST)
    grad_share = jnp.einsum("tec,ec->te", slot_wide, grad_share_slots, precision=HIGHEST)
    grad_weights = jnp.sum(jnp.where(member, grad_share[:, None, :], 0.0), axis=2)
    grad_route = route_weights * (
        grad_weights - jnp.sum(route_weights * grad_weights, axis=1, keepdims=True)
    )
    grad_logits = jnp.sum(jnp.where(route_hot, grad_route[:, :, None], 0.0), axis=1).astype(
        jnp.bfloat16
    )
    grad_normed = (
        lax.dot_general(grad_logits, router, CONTRACT_LAST, preferred_element_type=jnp.float32)
        + grad_normed_moe
    )
    grad_unit = grad_normed * norm_gain[None, :]
    grad_mid = loss_weight[:, None] * upstream[0].astype(jnp.float32) + inv_rms * (
        grad_unit - unit_rows * jnp.mean(grad_unit * unit_rows, axis=1, keepdims=True)
    )
    grad_residual = grad_mid.astype(jnp.bfloat16)
    grad_attended = lax.dot_general(
        grad_residual, out_full, CONTRACT_LAST, preferred_element_type=jnp.float32
    ).astype(jnp.bfloat16)
    query_gradient, key_gradient, value_gradient, sink_gradient = head_grads(
        probs,
        reduced_probabilities,
        sink_probs,
        query_rows,
        key_tile_block,
        value_tile_block,
        grad_attended,
    )
    next_keys, next_values = (
        passed_along(key_gradient[:WINDOW].astype(jnp.bfloat16), "seq", -1).astype(jnp.float32),
        passed_along(value_gradient[:WINDOW].astype(jnp.bfloat16), "seq", -1).astype(jnp.float32),
    )
    own_key_grad = key_gradient[WINDOW:]
    own_value_grad = value_gradient[WINDOW:]
    split_at = tokens_here - WINDOW
    grad_key_rows = jnp.concatenate(
        [own_key_grad[:split_at], own_key_grad + next_keys], axis=0
    ).astype(jnp.bfloat16)
    grad_value_rows = jnp.concatenate(
        [own_value_grad[:split_at], own_value_grad + next_values], axis=0
    ).astype(jnp.bfloat16)
    grad_sinks = lax.psum(sink_gradient, ("seq", "dp"))
    return (
        query_gradient[None],
        grad_key_rows[None],
        grad_value_rows[None],
        grad_residual[None],
        grad_sinks,
    )


MESH = pl.DeviceIdType.MESH
MIB = 1 << 20


def halving_place(index, count):
    place, weight, rest = 0, count // 2, index
    while weight:
        place = place + lax.rem(rest, 2) * weight
        rest = lax.div(rest, 2)
        weight //= 2
    return place


def flipped(index, bit):
    return index + bit - 2 * bit * lax.rem(lax.div(index, bit), 2)


def expert_kernel(
    count,
    slots_ref,
    facts_ref,
    gate_ref,
    up_ref,
    down_ref,
    own_ref,
    other_ref,
    theirs,
    outgoing,
    arrived,
    sent,
    total,
    received,
    grads,
    back,
    seq_send,
    seq_recv,
    to_send,
    to_recv,
    halve_send,
    halve_recv,
    double_send,
    double_recv,
    back_send,
    back_recv,
):
    bits = count.bit_length() - 1
    me = lax.axis_index("dp")
    side = lax.axis_index("seq")
    far = 1 - side
    place = halving_place(me, count)
    depth = gate_ref.shape[0]
    hidden = gate_ref.shape[1]
    wide = 3 * hidden // 2

    barrier = pltpu.get_barrier_semaphore()
    pl.semaphore_signal(barrier, inc=1, device_id={"seq": far}, device_id_type=MESH)

    def greet(step, carry):
        pl.semaphore_signal(
            barrier, inc=1, device_id={"dp": lax.rem(me + step, count)}, device_id_type=MESH
        )
        return carry

    lax.fori_loop(1, count, greet, 0)
    pl.semaphore_wait(barrier, count)

    swap = pltpu.make_async_remote_copy(
        src_ref=slots_ref.at[far],
        dst_ref=theirs,
        send_sem=seq_send.at[0],
        recv_sem=seq_recv.at[0],
        device_id={"seq": far},
        device_id_type=MESH,
    )
    swap.start()
    back[...] = jnp.broadcast_to(facts_ref[...], back.shape)
    swap.wait()
    mine = slots_ref[side]
    came = theirs[...]
    first = jnp.where(side == 0, mine, came)
    second = jnp.where(side == 0, came, mine)
    outgoing[...] = jnp.concatenate(
        [first[:, :CAP], second[:, :CAP], first[:, CAP:], second[:, CAP:]], axis=1
    ).astype(jnp.bfloat16)

    def slice_copy(step):
        to = lax.rem(me + step, count)
        return pltpu.make_async_remote_copy(
            src_ref=outgoing.at[to],
            dst_ref=arrived.at[place],
            send_sem=to_send.at[step],
            recv_sem=to_recv.at[step],
            device_id={"dp": to},
            device_id_type=MESH,
        )

    def start_slice(step, carry):
        slice_copy(step).start()
        return carry

    def wait_slice(step, carry):
        slice_copy(step).wait()
        return carry

    lax.fori_loop(1, count, start_slice, 0)
    arrived[place] = outgoing[me]
    lax.fori_loop(1, count, wait_slice, 0)

    half = count // 2
    rows = EW * CAP
    tile = 512

    def products(start):
        block = arrived[pl.ds(start, half)].astype(jnp.float32)
        normed = block[:, :rows].reshape(half * rows, -1)[:, :depth].astype(jnp.bfloat16)
        upstream = block[:, rows:].reshape(half * rows, -1)[:, :depth].astype(jnp.bfloat16)

        def product(column):
            which, at = divmod(column, hidden)
            weight = (gate_ref, up_ref, down_ref)[which]
            return jnp.dot(
                upstream if which == 2 else normed,
                weight[:, at : at + tile],
                preferred_element_type=jnp.float32,
            ).reshape(half, rows, tile)

        for column in range(0, wide, tile):
            yield column, jnp.concatenate([product(column), product(wide + column)], axis=1)

    def halve_copy(stage):
        blocks = half >> stage
        return pltpu.make_async_remote_copy(
            src_ref=sent[stage],
            dst_ref=received[stage],
            send_sem=halve_send.at[stage],
            recv_sem=halve_recv.at[stage],
            device_id={"dp": flipped(me, 1 << stage)},
            device_id_type=MESH,
        )

    bit_of = [lax.rem(lax.div(me, 1 << stage), 2) for stage in range(bits)]
    for column, value in products((1 - bit_of[0]) * half):
        sent[0][:, :, column : column + tile] = value.astype(jnp.bfloat16)
    halve_copy(0).start()
    for column, value in products(bit_of[0] * half):
        total[:, :, column : column + tile] = value
    base = 0
    for stage in range(1, bits):
        blocks = half >> stage
        halve_copy(stage - 1).wait()
        away = (1 - bit_of[stage]) * blocks
        keep = bit_of[stage] * blocks
        sent[stage][...] = (
            total[pl.ds(base + away, blocks)]
            + received[stage - 1][pl.ds(away, blocks)].astype(jnp.float32)
        ).astype(jnp.bfloat16)
        halve_copy(stage).start()
        total[pl.ds(base + keep, blocks)] += received[stage - 1][pl.ds(keep, blocks)].astype(
            jnp.float32
        )
        base = base + keep
    halve_copy(bits - 1).wait()
    summed = total[base] + received[bits - 1][0].astype(jnp.float32)

    gate_pre = summed[:rows, :hidden]
    up_pre = jnp.concatenate([summed[:rows, hidden:], summed[rows:, : hidden // 2]], axis=1)
    grad_act = summed[rows:, hidden // 2 :]
    sigmoid_gate = 1.0 / (1.0 + jnp.exp(-GLU_SLOPE * gate_pre))
    gate_sigmoid = gate_pre * sigmoid_gate
    raised_up = up_pre + 1.0
    activation = (raised_up * gate_sigmoid).astype(jnp.bfloat16).astype(jnp.float32)
    share = jnp.sum(activation * grad_act, axis=1, keepdims=True)
    grad_up = grad_act * gate_sigmoid
    grad_gate = (
        grad_act * raised_up * (sigmoid_gate + GLU_SLOPE * gate_sigmoid * (1.0 - sigmoid_gate))
    )
    grads[place] = jnp.concatenate([grad_gate, grad_up], axis=0).astype(jnp.bfloat16)

    for stage in range(bits):
        blocks = 1 << stage
        start = place // blocks * blocks
        copy = pltpu.make_async_remote_copy(
            src_ref=grads.at[pl.ds(start, blocks)],
            dst_ref=grads.at[pl.ds(start, blocks)],
            send_sem=double_send.at[stage],
            recv_sem=double_recv.at[stage],
            device_id={"dp": flipped(me, half >> stage)},
            device_id_type=MESH,
        )
        copy.start()
        copy.wait()

    flat = grads[...].reshape(count * 2 * rows, hidden)
    contract = (((1,), (1,)), ((), ()))
    from_gate = lax.dot_general(flat, gate_ref[...], contract, preferred_element_type=jnp.float32)
    from_up = lax.dot_general(flat, up_ref[...], contract, preferred_element_type=jnp.float32)
    from_gate = from_gate.reshape(count, 2 * rows, depth)
    from_up = from_up.reshape(count, 2 * rows, depth)
    back[:, :, :depth] = from_gate[:, :rows] + from_up[:, rows:]

    def back_copy(step):
        to = lax.rem(me + step, count)
        return pltpu.make_async_remote_copy(
            src_ref=back.at[halving_place(to, count)],
            dst_ref=own_ref.at[me],
            send_sem=back_send.at[step],
            recv_sem=back_recv.at[step],
            device_id={"dp": to},
            device_id_type=MESH,
        )

    def start_back(step, carry):
        back_copy(step).start()
        return carry

    def wait_back(step, carry):
        back_copy(step).wait()
        return carry

    lax.fori_loop(1, count, start_back, 0)
    own_ref[me] = back[place]
    own_ref[count] = jnp.broadcast_to(share, own_ref.shape[1:])
    lax.fori_loop(1, count, wait_back, 0)
    last = pltpu.make_async_remote_copy(
        src_ref=own_ref,
        dst_ref=other_ref,
        send_sem=seq_send.at[1],
        recv_sem=seq_recv.at[1],
        device_id={"seq": far},
        device_id_type=MESH,
    )
    last.start()
    last.wait()


def in_place_experts(slots, facts, gate, up, down):
    count, lanes = slots.shape[1], slots.shape[3]
    bits = count.bit_length() - 1
    rows = EW * CAP
    hidden = gate.shape[1]
    wide = 3 * hidden // 2
    stages = [pltpu.VMEM((count >> (stage + 1), 2 * rows, wide), jnp.bfloat16) for stage in range(bits)]
    vmem = pl.BlockSpec(memory_space=pltpu.VMEM)
    dma = pltpu.SemaphoreType.DMA
    result = jax.ShapeDtypeStruct((count + 1, rows, lanes), jnp.float32)
    return pl.pallas_call(
        functools.partial(expert_kernel, count),
        out_shape=(result, result),
        in_specs=[vmem] * 5,
        out_specs=(vmem, vmem),
        scratch_shapes=[
            pltpu.VMEM((count, rows, lanes), jnp.float32),
            pltpu.VMEM((count, 2 * rows, lanes), jnp.bfloat16),
            pltpu.VMEM((count, 2 * rows, lanes), jnp.bfloat16),
            stages,
            pltpu.VMEM((count // 2, 2 * rows, wide), jnp.float32),
            stages,
            pltpu.VMEM((count, 2 * rows, hidden), jnp.bfloat16),
            pltpu.VMEM((count, rows, lanes), jnp.float32),
            dma((2,)),
            dma((2,)),
            dma((count,)),
            dma((count,)),
            dma((bits,)),
            dma((bits,)),
            dma((bits,)),
            dma((bits,)),
            dma((count,)),
            dma((count,)),
        ],
        compiler_params=pltpu.CompilerParams(
            collective_id=1, has_side_effects=True, vmem_limit_bytes=40 * MIB
        ),
        name="expert_kernel",
    )(slots, facts, gate, up, down)


def attend(
    side, queries_ref, key_block, value_block, sinks_ref, attended_ref, probs_ref, sink_probs_ref
):
    tokens = queries_ref.shape[0]
    span = 2 * tokens
    shared_heads = QUERY_HEADS // KEY_VALUE_HEADS
    stacked = (tokens, span)
    row = lax.broadcasted_iota(jnp.int32, stacked, 0)
    col = lax.broadcasted_iota(jnp.int32, stacked, 1)
    allowed = (col >= row + 1) & (col <= row + tokens) & (col + side * tokens >= tokens)
    for group in range(KEY_VALUE_HEADS):
        lanes = slice(group * HEAD_SIZE, (group + 1) * HEAD_SIZE)
        group_keys = key_block[:, :, lanes].reshape(span, HEAD_SIZE)
        group_values = value_block[:, :, lanes].reshape(span, HEAD_SIZE)
        mixed = []
        for head in range(group * shared_heads, (group + 1) * shared_heads):
            scores = lax.dot_general(
                queries_ref[:, head * HEAD_SIZE : (head + 1) * HEAD_SIZE],
                group_keys,
                (((1,), (1,)), ((), ())),
                preferred_element_type=jnp.float32,
            )
            scores = jnp.where(allowed, scores * HEAD_SIZE ** (-0.5), -1e30)
            sink = sinks_ref[head : head + 1, :1]
            largest = jnp.maximum(jnp.max(scores, axis=1, keepdims=True), sink)
            raised = jnp.where(allowed, jnp.exp(scores - largest), 0.0)
            sink_raised = jnp.exp(sink - largest)
            denominator = jnp.sum(raised, axis=1, keepdims=True) + sink_raised
            probs = raised / denominator
            probs_ref[head] = probs
            sink_probs_ref[head] = sink_raised / denominator
            mixed.append(
                jnp.dot(
                    probs.astype(jnp.bfloat16), group_values, preferred_element_type=jnp.float32
                )
            )
            if len(mixed) * HEAD_SIZE == 128:
                end = (head + 1) * HEAD_SIZE
                attended_ref[:, end - 128 : end] = jnp.concatenate(mixed, axis=1).astype(
                    jnp.bfloat16
                )
                mixed = []


def gather_kernel(
    count,
    weight_ref,
    queries_ref,
    keys_ref,
    values_ref,
    sinks_ref,
    full_ref,
    attended_ref,
    probs_ref,
    sink_probs_ref,
    key_block,
    value_block,
    halo_send,
    halo_recv,
    own_sem,
    line_send,
    line_recv,
    pair_send,
    pair_recv,
    side_send,
    side_recv,
    core_send,
    core_recv,
):
    line = count // 4
    waves = line - 1
    me = lax.axis_index("dp")
    side = lax.axis_index("seq")
    core, pair, spot = lax.rem(me, 2), lax.rem(lax.div(me, 2), 2), lax.div(me, 4)
    rows = weight_ref.shape[0]
    lone = rows * 3 // 128 * 16
    shared = rows - 2 * lone
    lone_start = pl.multiple_of(side * (lone + shared), 16)
    plane_start = pl.multiple_of(side * lone, 16)
    far_start = pl.multiple_of((1 - side) * (lone + shared), 16)
    chunks = ((lone_start, lone), (lone, shared))

    def index(spot, pair, core):
        return (spot * 2 + pair) * 2 + core

    def part(owner, start, size, own=False):
        if own:
            return weight_ref.at[pl.ds(start, size)]
        return full_ref.at[owner, pl.ds(start, size)]

    def remote(owner, own, start, size, send, recv, target):
        return pltpu.make_async_remote_copy(
            src_ref=part(owner, start, size, own),
            dst_ref=part(owner, start, size),
            send_sem=send,
            recv_sem=recv,
            device_id=target,
            device_id_type=MESH,
        )

    def shard_spot(way, wave):
        return spot - 1 - wave if way == 0 else spot + 1 + wave

    def arrives(way, wave):
        return spot - 1 - wave >= 0 if way == 0 else spot + 1 + wave < line

    def leaves(way, wave):
        if way == 0:
            return (spot + 1 < line) & (spot - wave >= 0)
        return (spot >= 1) & (spot + wave < line)

    def line_copy(way, wave, chunk):
        step = 1 if way == 0 else -1
        owner = index(spot - step * wave, pair, core)
        return remote(
            owner,
            wave == 0,
            *chunks[chunk],
            line_send.at[way, wave, chunk],
            line_recv.at[way, wave, chunk],
            {"dp": index(spot + step, pair, core)},
        )

    def slot(piece):
        return 0 if piece is None else 1 + 2 * piece[1] + piece[0]

    def owner_of(piece, other_pair):
        at = spot if piece is None else shard_spot(*piece)
        return index(at, 1 - pair if other_pair else pair, core)

    def pair_copy(piece, chunk):
        at = slot(piece)
        return remote(
            owner_of(piece, False),
            piece is None,
            *chunks[chunk],
            pair_send.at[at, chunk],
            pair_recv.at[at, chunk],
            {"dp": index(spot, 1 - pair, core)},
        )

    def side_copy(piece, other_pair):
        at = slot(piece)
        return remote(
            owner_of(piece, other_pair),
            False,
            lone_start,
            lone,
            side_send.at[other_pair, at],
            side_recv.at[other_pair, at],
            {"seq": 1 - side},
        )

    def core_copy(piece, other_pair, from_side):
        at = slot(piece)
        if piece is None and other_pair == 0:
            start, size = 0, rows
        elif from_side:
            start, size = far_start, lone
        else:
            start, size = plane_start, lone + shared
        return remote(
            owner_of(piece, other_pair),
            piece is None and other_pair == 0,
            start,
            size,
            core_send.at[from_side, other_pair, at],
            core_recv.at[from_side, other_pair, at],
            {"dp": index(spot, pair, 1 - core)},
        )

    def held(piece, action):
        if piece is None:
            action()
        else:
            pl.when(arrives(*piece))(action)

    barrier = pltpu.get_barrier_semaphore()

    def greet(target):
        pl.semaphore_signal(barrier, inc=1, device_id=target, device_id_type=MESH)

    greet({"seq": 1 - side})
    greet({"dp": index(spot, 1 - pair, core)})
    greet({"dp": index(spot, pair, 1 - core)})
    for way, step in ((0, 1), (1, -1)):

        @pl.when(leaves(way, 0))
        def _(step=step):
            greet({"dp": index(spot + step, pair, core)})

    neighbours = leaves(0, 0).astype(jnp.int32) + leaves(1, 0).astype(jnp.int32)
    pl.semaphore_wait(barrier, 3 + neighbours)

    keep = pltpu.make_async_copy(weight_ref, full_ref.at[me], own_sem)
    for chunk in (0, 1):
        for way in (0, 1):

            @pl.when(leaves(way, 0))
            def _(way=way, chunk=chunk):
                line_copy(way, 0, chunk).start()

        pair_copy(None, chunk).start()
    core_copy(None, 0, 0).start()
    keep.start()
    halos = [
        pltpu.make_async_remote_copy(
            src_ref=source,
            dst_ref=block.at[0],
            send_sem=halo_send.at[at],
            recv_sem=halo_recv.at[at],
            device_id={"seq": 1 - side},
            device_id_type=MESH,
        )
        for at, (source, block) in enumerate(((keys_ref, key_block), (values_ref, value_block)))
    ]
    for halo in halos:
        halo.start()
    key_block[1] = keys_ref[...]
    value_block[1] = values_ref[...]
    for halo in halos:
        halo.wait()
    attend(
        side, queries_ref, key_block, value_block, sinks_ref, attended_ref, probs_ref, sink_probs_ref
    )

    def line_step(wave):
        for chunk in (0, 1):
            for way in (0, 1):

                @pl.when(arrives(way, wave))
                def _(way=way, chunk=chunk):
                    piece = (way, wave)
                    line_copy(way, wave, chunk).wait_recv()
                    if wave + 1 < waves:

                        @pl.when(leaves(way, wave + 1))
                        def _():
                            line_copy(way, wave + 1, chunk).start()

                    pair_copy(piece, chunk).start()
                    if chunk == 0:
                        side_copy(piece, 0).start()
                    else:
                        core_copy(piece, 0, 0).start()

    def pair_step(pieces):
        for chunk in (0, 1):
            for piece in pieces:

                def arrive(piece=piece, chunk=chunk):
                    pair_copy(piece, chunk).wait_recv()
                    if chunk == 0:
                        side_copy(piece, 1).start()
                    else:
                        core_copy(piece, 1, 0).start()

                held(piece, arrive)

    def side_step(pieces, other_pair):
        for piece in pieces:

            def arrive(piece=piece):
                side_copy(piece, other_pair).wait_recv()
                core_copy(piece, other_pair, 1).start()

            held(piece, arrive)

    waved = [[(0, wave), (1, wave)] for wave in range(waves)]
    ordered = [[None]] + waved
    for wave in range(waves):
        line_step(wave)
        pair_step(ordered[wave])
        if wave:
            side_step(waved[wave - 1], 0)
            side_step(ordered[wave - 1], 1)
    pair_step(ordered[waves])
    side_step(waved[waves - 1], 0)
    side_step(ordered[waves - 1], 1)
    side_step(ordered[waves], 1)

    keep.wait()
    for piece in [None] + sum(waved, []):

        def finish(piece=piece):
            for chunk in (0, 1):
                pair_copy(piece, chunk).wait_send()
            for other_pair in (0, 1):
                core_copy(piece, other_pair, 0).wait()
                if piece is not None or other_pair:
                    side_copy(piece, other_pair).wait_send()
                    core_copy(piece, other_pair, 1).wait()

        held(piece, finish)
    for wave in range(waves):
        for way in (0, 1):

            @pl.when(leaves(way, wave))
            def _(way=way, wave=wave):
                for chunk in (0, 1):
                    line_copy(way, wave, chunk).wait_send()


def gather_and_attend(weight, queries, keys, values, sinks, count):
    waves = count // 4 - 1
    slots = 1 + 2 * waves
    dma = pltpu.SemaphoreType.DMA
    hbm = pl.BlockSpec(memory_space=pl.ANY)
    vmem = pl.BlockSpec(memory_space=pltpu.VMEM)
    tokens = queries.shape[0]
    sink_rows = jnp.broadcast_to(sinks[:, None], (QUERY_HEADS, 128))
    full, attended, probs, sink_probs, key_block, value_block = pl.pallas_call(
        functools.partial(gather_kernel, count),
        out_shape=(
            jax.ShapeDtypeStruct((count,) + weight.shape, weight.dtype),
            jax.ShapeDtypeStruct(queries.shape, jnp.bfloat16),
            jax.ShapeDtypeStruct((QUERY_HEADS, tokens, 2 * tokens), jnp.float32),
            jax.ShapeDtypeStruct((QUERY_HEADS, tokens, 1), jnp.float32),
            jax.ShapeDtypeStruct((2,) + keys.shape, keys.dtype),
            jax.ShapeDtypeStruct((2,) + values.shape, values.dtype),
        ),
        in_specs=[vmem] * 5,
        out_specs=(hbm,) + (vmem,) * 5,
        scratch_shapes=[
            dma((2,)),
            dma((2,)),
            dma,
            dma((2, waves, 2)),
            dma((2, waves, 2)),
            dma((slots, 2)),
            dma((slots, 2)),
            dma((2, slots)),
            dma((2, slots)),
            dma((2, 2, slots)),
            dma((2, 2, slots)),
        ],
        compiler_params=pltpu.CompilerParams(
            collective_id=2, has_side_effects=True, vmem_limit_bytes=40 * MIB
        ),
        name="gather_kernel",
    )(weight, queries, keys, values, sink_rows)
    heads = (KEY_VALUE_HEADS, QUERY_HEADS // KEY_VALUE_HEADS, tokens)
    return (
        full.reshape(count * weight.shape[0], weight.shape[1]),
        attended,
        probs.reshape(heads + (2 * tokens,)),
        sink_probs.reshape(heads),
        key_block.reshape(2 * tokens, keys.shape[1]),
        value_block.reshape(2 * tokens, values.shape[1]),
    )


def tail_kernel(
    count, sinks_ref, halo_ref, sums_ref, came_ref, parts, half, far_half, dp_send, dp_recv, seq_send, seq_recv
):
    me = lax.axis_index("dp")
    far = 1 - lax.axis_index("seq")
    barrier = pltpu.get_barrier_semaphore()
    pl.semaphore_signal(barrier, inc=1, device_id={"seq": far}, device_id_type=MESH)

    def greet(step, carry):
        pl.semaphore_signal(
            barrier, inc=1, device_id={"dp": lax.rem(me + step, count)}, device_id_type=MESH
        )
        return carry

    lax.fori_loop(1, count, greet, 0)
    pl.semaphore_wait(barrier, count)

    def across(source, target, at):
        return pltpu.make_async_remote_copy(
            src_ref=source,
            dst_ref=target,
            send_sem=seq_send.at[at],
            recv_sem=seq_recv.at[at],
            device_id={"seq": far},
            device_id_type=MESH,
        )

    def part_copy(step):
        return pltpu.make_async_remote_copy(
            src_ref=sinks_ref,
            dst_ref=parts.at[me],
            send_sem=dp_send.at[step],
            recv_sem=dp_recv.at[step],
            device_id={"dp": lax.rem(me + step, count)},
            device_id_type=MESH,
        )

    def start_part(step, carry):
        part_copy(step).start()
        return carry

    def wait_part(step, carry):
        part_copy(step).wait()
        return carry

    lax.fori_loop(1, count, start_part, 0)
    halo = across(halo_ref, came_ref, 0)
    halo.start()
    parts[me] = sinks_ref[...]
    lax.fori_loop(1, count, wait_part, 0)
    half[...] = jnp.sum(parts[...], axis=0)
    swap = across(half, far_half, 1)
    swap.start()
    swap.wait()
    sums_ref[...] = half[...] + far_half[...]
    halo.wait()


def tail_exchange(sinks, halo, count):
    vmem = pl.BlockSpec(memory_space=pltpu.VMEM)
    dma = pltpu.SemaphoreType.DMA
    tile = (8, 128)
    row = jnp.zeros(tile, jnp.float32).at[0, : sinks.shape[0]].set(sinks)
    sums, came = pl.pallas_call(
        functools.partial(tail_kernel, count),
        out_shape=(
            jax.ShapeDtypeStruct(tile, jnp.float32),
            jax.ShapeDtypeStruct(halo.shape, halo.dtype),
        ),
        in_specs=[vmem] * 2,
        out_specs=(vmem, vmem),
        scratch_shapes=[
            pltpu.VMEM((count,) + tile, jnp.float32),
            pltpu.VMEM(tile, jnp.float32),
            pltpu.VMEM(tile, jnp.float32),
            dma((count,)),
            dma((count,)),
            dma((2,)),
            dma((2,)),
        ],
        compiler_params=pltpu.CompilerParams(collective_id=3, has_side_effects=True),
        name="tail_kernel",
    )(row, halo)
    return sums[0, : sinks.shape[0]], came


def shards(
    queries,
    key_rows,
    value_matrix,
    head_sink_logits,
    residual,
    out_weight,
    norm_gain,
    router,
    expert_gate,
    expert_up,
    expert_down,
    routes,
    group_ids,
    rewards,
    response_mask,
    upstream,
):
    seq_count = lax.axis_size("seq")
    dp_count = lax.axis_size("dp")
    seq_index = lax.axis_index("seq")
    query_rows = queries[0]
    own_keys = key_rows[0]
    own_values = value_matrix[0]
    tokens_here = query_rows.shape[0]
    group_count = max(dp_count // 4, 1)
    all_tokens = dp_count * seq_count * tokens_here
    group_hot = (group_ids[0] == jnp.arange(group_count, dtype=jnp.int32)).astype(jnp.float32)
    reward = rewards[0].astype(jnp.float32)
    group_terms = (
        group_hot[:, None] * jnp.stack([jnp.ones_like(reward), reward, reward * reward])[None, :]
    )
    mask_wide = response_mask[0].astype(jnp.float32)
    local_count = jnp.sum(mask_wide)
    first_device = (seq_index == 0).astype(jnp.float32)
    out_full, attended, probs, sink_probs, key_tile_block, value_tile_block = gather_and_attend(
        out_weight, query_rows, own_keys, own_values, head_sink_logits, dp_count
    )
    reduced_probabilities = probs.astype(jnp.bfloat16)
    projected = jnp.dot(attended, out_full, preferred_element_type=jnp.float32)
    mid_rows = lax.optimization_barrier(
        (residual[0].astype(jnp.float32) + projected).astype(jnp.bfloat16)
    )
    mid_wide = mid_rows.astype(jnp.float32)
    inv_rms = lax.rsqrt(jnp.mean(mid_wide * mid_wide, axis=1, keepdims=True) + NORM_EPS)
    unit_rows = mid_wide * inv_rms
    normed = (unit_rows * norm_gain[None, :]).astype(jnp.bfloat16)
    logits = jnp.dot(normed, router, preferred_element_type=jnp.float32)
    route_hot = routes[0][:, :, None] == jnp.arange(EXPERTS, dtype=jnp.int32)[None, None, :]
    route_logits = jnp.sum(jnp.where(route_hot, logits[:, None, :], 0.0), axis=2)
    raised = jnp.exp(route_logits)
    route_weights = raised / jnp.sum(raised, axis=1, keepdims=True)
    member = route_hot[:, :, :EW]
    expert_share = jnp.sum(jnp.where(member, route_weights[:, :, None], 0.0), axis=1)
    chosen = jnp.any(member, axis=1)
    slot_rank = jnp.cumsum(chosen.astype(jnp.int32), axis=0) - 1
    slot_hot = chosen[:, :, None] & (
        slot_rank[:, :, None] == jnp.arange(CAP, dtype=jnp.int32)[None, None, :]
    )
    slot_low = slot_hot.astype(jnp.bfloat16)
    slot_wide = slot_hot.astype(jnp.float32)
    slot_rows = jnp.einsum(
        "tec,td->ecd", slot_low, normed, preferred_element_type=jnp.float32
    )
    share_slots = jnp.einsum("tec,te->ec", slot_wide, expert_share, precision=HIGHEST)
    upstream_slots = jnp.einsum(
        "tec,td->ecd", slot_low, upstream[0], preferred_element_type=jnp.float32
    )
    depth = expert_gate.shape[0]
    lanes = -(-depth // 128) * 128
    slots = jnp.concatenate([slot_rows, upstream_slots], axis=1)
    slots = slots.reshape(EW, 2 * CAP, dp_count, depth).transpose(0, 2, 1, 3)
    facts = jnp.concatenate([(group_terms * first_device).reshape(-1), local_count[None]])
    lanes = max(lanes, -(-(depth + facts.shape[0]) // 128) * 128)
    slots = jnp.pad(slots, ((0, 0), (0, 0), (0, 0), (0, lanes - depth)))
    facts = jnp.pad(facts, (depth, lanes - depth - facts.shape[0]))
    facts = jnp.broadcast_to(facts, (EW * CAP, lanes))
    own_part, other_part = in_place_experts(slots, facts, expert_gate, expert_up, expert_down)
    totals = jnp.sum(own_part[:dp_count, 0] + other_part[:dp_count, 0], axis=0)[depth:]
    group_totals = totals[: group_terms.size].reshape(group_terms.shape)
    token_total = totals[group_terms.size]
    group_sizes = group_totals[:, 0]
    group_means = group_totals[:, 1] / group_sizes
    group_spread = group_totals[:, 2] / group_sizes - group_means * group_means
    own_mean = jnp.sum(group_hot * group_means)
    own_spread = jnp.sum(group_hot * group_spread)
    advantage = (reward - own_mean) / jnp.sqrt(jnp.maximum(own_spread, 1.0))
    token_scale = -advantage * all_tokens / token_total
    loss_weight = token_scale * mask_wide
    weight_slots = jnp.einsum("tec,t->ec", slot_wide, loss_weight, precision=HIGHEST)
    both_parts = jnp.where(
        seq_index == 0, jnp.stack([own_part, other_part]), jnp.stack([other_part, own_part])
    )
    both_parts = lax.dynamic_slice_in_dim(both_parts, seq_index * CAP, CAP, 2)
    grad_share_slots = weight_slots * both_parts[:, dp_count, :, 0]
    grad_rows = (
        both_parts[:, :dp_count, :, :depth].transpose(0, 2, 1, 3).reshape(EW, CAP, D)
        * (weight_slots * share_slots)[:, :, None]
    )
    grad_normed_moe = jnp.einsum("tec,ecd->td", slot_wide, grad_rows, precision=HIGHEST)
    grad_share = jnp.einsum("tec,ec->te", slot_wide, grad_share_slots, precision=HIGHEST)
    grad_weights = jnp.sum(jnp.where(member, grad_share[:, None, :], 0.0), axis=2)
    grad_route = route_weights * (
        grad_weights - jnp.sum(route_weights * grad_weights, axis=1, keepdims=True)
    )
    grad_logits = jnp.sum(jnp.where(route_hot, grad_route[:, :, None], 0.0), axis=1).astype(
        jnp.bfloat16
    )
    grad_normed = (
        lax.dot_general(grad_logits, router, CONTRACT_LAST, preferred_element_type=jnp.float32)
        + grad_normed_moe
    )
    grad_unit = grad_normed * norm_gain[None, :]
    grad_mid = loss_weight[:, None] * upstream[0].astype(jnp.float32) + inv_rms * (
        grad_unit - unit_rows * jnp.mean(grad_unit * unit_rows, axis=1, keepdims=True)
    )
    grad_residual = grad_mid.astype(jnp.bfloat16)
    grad_attended = lax.dot_general(
        grad_residual, out_full, CONTRACT_LAST, preferred_element_type=jnp.float32
    ).astype(jnp.bfloat16)
    query_gradient, key_gradient, value_gradient, sink_gradient = head_grads(
        probs,
        reduced_probabilities,
        sink_probs,
        query_rows,
        key_tile_block,
        value_tile_block,
        grad_attended,
    )
    halo = jnp.concatenate([key_gradient[:WINDOW], value_gradient[:WINDOW]], axis=0)
    grad_sinks, came = tail_exchange(sink_gradient, halo.astype(jnp.bfloat16), dp_count)
    came = jnp.where(seq_index + 1 < seq_count, came.astype(jnp.float32), 0.0)
    next_keys, next_values = came[:WINDOW], came[WINDOW:]
    own_key_grad = key_gradient[WINDOW:]
    own_value_grad = value_gradient[WINDOW:]
    split_at = tokens_here - WINDOW
    grad_key_rows = jnp.concatenate(
        [own_key_grad[:split_at], own_key_grad + next_keys], axis=0
    ).astype(jnp.bfloat16)
    grad_value_rows = jnp.concatenate(
        [own_value_grad[:split_at], own_value_grad + next_values], axis=0
    ).astype(jnp.bfloat16)
    return (
        query_gradient[None],
        grad_key_rows[None],
        grad_value_rows[None],
        grad_residual[None],
        grad_sinks,
    )


def solution(mesh):
    seq_count, dp_count = mesh.shape["seq"], mesh.shape["dp"]
    in_place = seq_count == EW and dp_count >= 8 and dp_count & (dp_count - 1) == 0
    return jax.shard_map(
        shards if in_place else general_shards,
        mesh=mesh,
        in_specs=(
            P("dp", "seq", None),
            P("dp", "seq", None),
            P("dp", "seq", None),
            P(),
            P("dp", "seq", None),
            P("dp", None),
            P(),
            P(),
            P("dp", "seq"),
            P("dp", "seq"),
            P("dp", "seq"),
            P("dp", "seq", None),
            P("dp"),
            P("dp"),
            P("dp", "seq"),
            P("dp", "seq", None),
        ),
        out_specs=(
            P("dp", "seq", None),
            P("dp", "seq", None),
            P("dp", "seq", None),
            P("dp", "seq", None),
            P(),
        ),
        check_vma=False,
    )
```

```python
import functools

import jax
import jax.numpy as jnp
from jax import lax
from jax.experimental import pallas as pl
from jax.experimental.pallas import tpu as pltpu
from jax.sharding import PartitionSpec as P

D = 2880
HEAD_SIZE = 64
WINDOW = 128
EXPERTS = 128
QUERY_HEADS = 32
KEY_VALUE_HEADS = 4
EW = 2
CAP = 4


NORM_EPS = 1e-05
GLU_SLOPE = 1.702
HIGHEST = lax.Precision.HIGHEST
CONTRACT_LAST = (((1,), (1,)), ((), ()))


def passed_along(value, axis, steps):
    count = lax.axis_size(axis)
    initial, last = (max(0, -steps), min(count, count - steps))
    return lax.ppermute(value, axis, [(source, source + steps) for source in range(initial, last)])


def glu_forward(gate_pre, up_pre):
    return ((up_pre + 1.0) * gate_pre * jax.nn.sigmoid(GLU_SLOPE * gate_pre)).astype(jnp.bfloat16)


def glu_grads(grad_act, gate_pre, up_pre):
    sigmoid_gate = jax.nn.sigmoid(GLU_SLOPE * gate_pre)
    grad_up = grad_act * (gate_pre * sigmoid_gate)
    grad_gate = (
        grad_act
        * (up_pre + 1.0)
        * (sigmoid_gate + GLU_SLOPE * gate_pre * sigmoid_gate * (1.0 - sigmoid_gate))
    )
    return (grad_gate, grad_up)


def head_scores(query_tile_block, key_tile_block, head_sink_logits, allowed):
    query_total_count = query_tile_block.shape[0]
    key_total_count = key_tile_block.shape[0]
    query_head_rows = query_tile_block.reshape(
        query_total_count, KEY_VALUE_HEADS, QUERY_HEADS // KEY_VALUE_HEADS, HEAD_SIZE
    )
    key_head_rows = key_tile_block.reshape(key_total_count, KEY_VALUE_HEADS, HEAD_SIZE)
    attention_scores = jnp.einsum(
        "baqj,eaj->aqbe", query_head_rows, key_head_rows, preferred_element_type=jnp.float32
    ) * HEAD_SIZE ** (-0.5)
    attention_scores = jnp.where(allowed[None, None], attention_scores, -1e30)
    sink_logit_column = head_sink_logits.reshape(KEY_VALUE_HEADS, QUERY_HEADS // KEY_VALUE_HEADS)[
        :, :, None
    ]
    largest = jnp.maximum(jnp.max(attention_scores, axis=3), sink_logit_column)
    raised = jnp.where(allowed[None, None], jnp.exp(attention_scores - largest[..., None]), 0.0)
    sink_raised = jnp.exp(sink_logit_column - largest)
    denominator = jnp.sum(raised, axis=3) + sink_raised
    return (raised / denominator[..., None], sink_raised / denominator)


def head_mix(reduced_probabilities, value_tile_block):
    key_total_count = value_tile_block.shape[0]
    value_head_rows = value_tile_block.reshape(key_total_count, KEY_VALUE_HEADS, HEAD_SIZE)
    mixed_output = jnp.einsum(
        "amlh,hai->lami", reduced_probabilities, value_head_rows, preferred_element_type=jnp.float32
    )
    return mixed_output.reshape(mixed_output.shape[0], QUERY_HEADS * HEAD_SIZE).astype(jnp.bfloat16)


def head_grads(
    probs,
    reduced_probabilities,
    sink_probs,
    query_tile_block,
    key_tile_block,
    value_tile_block,
    mixed_gradient,
):
    query_total_count = query_tile_block.shape[0]
    key_total_count = key_tile_block.shape[0]
    query_head_rows = query_tile_block.reshape(
        query_total_count, KEY_VALUE_HEADS, QUERY_HEADS // KEY_VALUE_HEADS, HEAD_SIZE
    )
    key_head_rows = key_tile_block.reshape(key_total_count, KEY_VALUE_HEADS, HEAD_SIZE)
    value_head_rows = value_tile_block.reshape(key_total_count, KEY_VALUE_HEADS, HEAD_SIZE)
    heads_gradient = mixed_gradient.reshape(
        query_total_count, KEY_VALUE_HEADS, QUERY_HEADS // KEY_VALUE_HEADS, HEAD_SIZE
    )
    probability_gradient = jnp.einsum(
        "baqj,eaj->aqbe", heads_gradient, value_head_rows, preferred_element_type=jnp.float32
    )
    spread = jnp.sum(probs * probability_gradient, axis=3)
    score_gradient = (probs * (probability_gradient - spread[..., None])).astype(jnp.bfloat16)
    head_scaling = HEAD_SIZE ** (-0.5)
    query_gradient = (
        jnp.einsum(
            "amlh,hai->lami", score_gradient, key_head_rows, preferred_element_type=jnp.float32
        )
        * head_scaling
    )
    key_gradient = (
        jnp.einsum(
            "ujko,kujm->oum", score_gradient, query_head_rows, preferred_element_type=jnp.float32
        )
        * head_scaling
    )
    value_gradient = jnp.einsum(
        "ujko,kujm->oum", reduced_probabilities, heads_gradient, preferred_element_type=jnp.float32
    )
    sink_gradient = -jnp.sum(sink_probs * spread, axis=2).reshape(QUERY_HEADS)
    return (
        query_gradient.reshape(query_total_count, QUERY_HEADS * HEAD_SIZE).astype(jnp.bfloat16),
        key_gradient.reshape(key_total_count, KEY_VALUE_HEADS * HEAD_SIZE),
        value_gradient.reshape(key_total_count, KEY_VALUE_HEADS * HEAD_SIZE),
        sink_gradient,
    )


def block_backward(grad_flat, gate_pre, up_pre, gate_full, up_full, down_full):
    grad_act = jnp.dot(grad_flat, down_full, preferred_element_type=jnp.float32)
    grad_gate, grad_up = glu_grads(grad_act, gate_pre, up_pre)
    grad_pair = jnp.concatenate([grad_gate, grad_up], axis=1).astype(jnp.bfloat16)
    weight_pair = jnp.concatenate([gate_full, up_full], axis=1)
    return lax.dot_general(
        grad_pair, weight_pair, CONTRACT_LAST, preferred_element_type=jnp.float32
    ).astype(jnp.bfloat16)


def general_shards(
    queries,
    key_rows,
    value_matrix,
    head_sink_logits,
    residual,
    out_weight,
    norm_gain,
    router,
    expert_gate,
    expert_up,
    expert_down,
    routes,
    group_ids,
    rewards,
    response_mask,
    upstream,
):
    seq_count = lax.axis_size("seq")
    dp_count = lax.axis_size("dp")
    seq_index = lax.axis_index("seq")
    query_rows = queries[0]
    own_keys = key_rows[0]
    own_values = value_matrix[0]
    tokens_here = query_rows.shape[0]
    pieces = seq_count // EW
    group_count = max(dp_count // 4, 1)
    all_tokens = dp_count * seq_count * tokens_here
    group_hot = (group_ids[0] == jnp.arange(group_count, dtype=jnp.int32)).astype(jnp.float32)
    reward = rewards[0].astype(jnp.float32)
    group_terms = (
        group_hot[:, None] * jnp.stack([jnp.ones_like(reward), reward, reward * reward])[None, :]
    )
    mask_wide = response_mask[0].astype(jnp.float32)
    local_count = jnp.sum(mask_wide)
    first_device = (seq_index == 0).astype(jnp.float32)
    group_totals, token_total = lax.psum((group_terms * first_device, local_count), ("seq", "dp"))
    group_sizes = group_totals[:, 0]
    group_means = group_totals[:, 1] / group_sizes
    group_spread = group_totals[:, 2] / group_sizes - group_means * group_means
    own_mean = jnp.sum(group_hot * group_means)
    own_spread = jnp.sum(group_hot * group_spread)
    advantage = (reward - own_mean) / jnp.sqrt(jnp.maximum(own_spread, 1.0))
    token_scale = -advantage * all_tokens / token_total
    loss_weight = token_scale * mask_wide
    halo_keys, halo_values = passed_along((own_keys, own_values), "seq", 1)
    key_tile_block = jnp.concatenate([halo_keys, own_keys], axis=0)
    value_tile_block = jnp.concatenate([halo_values, own_values], axis=0)
    row_index = jnp.arange(tokens_here, dtype=jnp.int32)[:, None]
    col_index = jnp.arange(WINDOW + tokens_here, dtype=jnp.int32)[None, :]
    allowed = (
        (col_index >= row_index + 1)
        & (col_index <= row_index + WINDOW)
        & ((col_index >= WINDOW) | (seq_index > 0))
    )
    probs, sink_probs = head_scores(query_rows, key_tile_block, head_sink_logits, allowed)
    reduced_probabilities = probs.astype(jnp.bfloat16)
    attended = head_mix(reduced_probabilities, value_tile_block)
    out_full = lax.all_gather(out_weight, "dp", axis=0, tiled=True)
    projected = jnp.dot(attended, out_full, preferred_element_type=jnp.float32)
    mid_rows = lax.optimization_barrier(
        (residual[0].astype(jnp.float32) + projected).astype(jnp.bfloat16)
    )
    mid_wide = mid_rows.astype(jnp.float32)
    inv_rms = lax.rsqrt(jnp.mean(mid_wide * mid_wide, axis=1, keepdims=True) + NORM_EPS)
    unit_rows = mid_wide * inv_rms
    normed = (unit_rows * norm_gain[None, :]).astype(jnp.bfloat16)
    logits = jnp.dot(normed, router, preferred_element_type=jnp.float32)
    route_hot = routes[0][:, :, None] == jnp.arange(EXPERTS, dtype=jnp.int32)[None, None, :]
    route_logits = jnp.sum(jnp.where(route_hot, logits[:, None, :], 0.0), axis=2)
    raised = jnp.exp(route_logits)
    route_weights = raised / jnp.sum(raised, axis=1, keepdims=True)
    member = route_hot[:, :, :EW]
    expert_share = jnp.sum(jnp.where(member, route_weights[:, :, None], 0.0), axis=1)
    chosen = jnp.any(member, axis=1)
    slot_rank = jnp.cumsum(chosen.astype(jnp.int32), axis=0) - 1
    slot_hot = chosen[:, :, None] & (
        slot_rank[:, :, None] == jnp.arange(CAP, dtype=jnp.int32)[None, None, :]
    )
    slot_low = slot_hot.astype(jnp.bfloat16)
    slot_wide = slot_hot.astype(jnp.float32)
    slot_rows = jnp.einsum(
        "tec,td->ecd", slot_low, normed, preferred_element_type=jnp.float32
    ).astype(jnp.bfloat16)
    outgoing = jnp.broadcast_to(slot_rows[:, None], (EW, pieces, CAP, D)).reshape(seq_count, CAP, D)
    upstream_slots = jnp.einsum(
        "tec,td->ecd", slot_low, upstream[0], preferred_element_type=jnp.float32
    )
    weight_slots = jnp.einsum("tec,t->ec", slot_wide, loss_weight, precision=HIGHEST)
    share_slots = jnp.einsum("tec,te->ec", slot_wide, expert_share, precision=HIGHEST)
    cot_slots = weight_slots[:, :, None] * upstream_slots
    grad_out = (share_slots[:, :, None] * cot_slots).astype(jnp.bfloat16)
    grad_outgoing = jnp.broadcast_to(grad_out[:, None], (EW, pieces, CAP, D)).reshape(
        seq_count, CAP, D
    )
    gate_full, up_full, down_full = (
        lax.all_gather(expert_gate, "dp", axis=0, tiled=True),
        lax.all_gather(expert_up, "dp", axis=0, tiled=True),
        lax.all_gather(expert_down, "dp", axis=0, tiled=True),
    )
    arrived = lax.all_to_all(outgoing, "seq", split_axis=0, concat_axis=0, tiled=True)
    senders = arrived.shape[0]
    items = arrived.shape[1]
    block_senders = arrived.shape[0]
    block_items = arrived.shape[1]
    flat_rows = arrived.reshape(block_senders * block_items, D)
    gate_pre = jnp.dot(flat_rows, gate_full, preferred_element_type=jnp.float32)
    up_pre = jnp.dot(flat_rows, up_full, preferred_element_type=jnp.float32)
    activation = glu_forward(gate_pre, up_pre)
    partial_out = lax.dot_general(
        activation, down_full, CONTRACT_LAST, preferred_element_type=jnp.float32
    ).astype(jnp.bfloat16)
    partial_out, gate_pre, up_pre = (
        partial_out.reshape(block_senders, block_items, D),
        gate_pre,
        up_pre,
    )
    back_out = lax.all_to_all(partial_out, "seq", split_axis=0, concat_axis=0, tiled=True)
    gate_held = gate_pre.reshape(senders, items, -1)
    up_held = up_pre.reshape(senders, items, -1)
    grad_arrived = lax.all_to_all(grad_outgoing, "seq", split_axis=0, concat_axis=0, tiled=True)
    grad_piece = block_backward(
        grad_arrived.reshape(seq_count * CAP, D),
        gate_held.reshape(seq_count * CAP, -1),
        up_held.reshape(seq_count * CAP, -1),
        gate_full,
        up_full,
        down_full,
    )
    grad_back = lax.all_to_all(
        grad_piece.reshape(seq_count, CAP, D), "seq", split_axis=0, concat_axis=0, tiled=True
    )
    expert_out = jnp.sum(back_out.reshape(EW, pieces, CAP, D).astype(jnp.float32), axis=1)
    grad_share_slots = jnp.sum(cot_slots * expert_out, axis=2)
    grad_rows = jnp.sum(grad_back.reshape(EW, pieces, CAP, D).astype(jnp.float32), axis=1)
    grad_normed_moe = jnp.einsum("tec,ecd->td", slot_wide, grad_rows, precision=HIGHEST)
    grad_share = jnp.einsum("tec,ec->te", slot_wide, grad_share_slots, precision=HIGHEST)
    grad_weights = jnp.sum(jnp.where(member, grad_share[:, None, :], 0.0), axis=2)
    grad_route = route_weights * (
        grad_weights - jnp.sum(route_weights * grad_weights, axis=1, keepdims=True)
    )
    grad_logits = jnp.sum(jnp.where(route_hot, grad_route[:, :, None], 0.0), axis=1).astype(
        jnp.bfloat16
    )
    grad_normed = (
        lax.dot_general(grad_logits, router, CONTRACT_LAST, preferred_element_type=jnp.float32)
        + grad_normed_moe
    )
    grad_unit = grad_normed * norm_gain[None, :]
    grad_mid = loss_weight[:, None] * upstream[0].astype(jnp.float32) + inv_rms * (
        grad_unit - unit_rows * jnp.mean(grad_unit * unit_rows, axis=1, keepdims=True)
    )
    grad_residual = grad_mid.astype(jnp.bfloat16)
    grad_attended = lax.dot_general(
        grad_residual, out_full, CONTRACT_LAST, preferred_element_type=jnp.float32
    ).astype(jnp.bfloat16)
    query_gradient, key_gradient, value_gradient, sink_gradient = head_grads(
        probs,
        reduced_probabilities,
        sink_probs,
        query_rows,
        key_tile_block,
        value_tile_block,
        grad_attended,
    )
    next_keys, next_values = (
        passed_along(key_gradient[:WINDOW].astype(jnp.bfloat16), "seq", -1).astype(jnp.float32),
        passed_along(value_gradient[:WINDOW].astype(jnp.bfloat16), "seq", -1).astype(jnp.float32),
    )
    own_key_grad = key_gradient[WINDOW:]
    own_value_grad = value_gradient[WINDOW:]
    split_at = tokens_here - WINDOW
    grad_key_rows = jnp.concatenate(
        [own_key_grad[:split_at], own_key_grad + next_keys], axis=0
    ).astype(jnp.bfloat16)
    grad_value_rows = jnp.concatenate(
        [own_value_grad[:split_at], own_value_grad + next_values], axis=0
    ).astype(jnp.bfloat16)
    grad_sinks = lax.psum(sink_gradient, ("seq", "dp"))
    return (
        query_gradient[None],
        grad_key_rows[None],
        grad_value_rows[None],
        grad_residual[None],
        grad_sinks,
    )


MESH = pl.DeviceIdType.MESH
MIB = 1 << 20


def halving_place(index, count):
    place, weight, rest = 0, count // 2, index
    while weight:
        place = place + lax.rem(rest, 2) * weight
        rest = lax.div(rest, 2)
        weight //= 2
    return place


def flipped(index, bit):
    return index + bit - 2 * bit * lax.rem(lax.div(index, bit), 2)


def expert_kernel(
    count,
    slots_ref,
    facts_ref,
    gate_ref,
    up_ref,
    down_ref,
    own_ref,
    other_ref,
    theirs,
    outgoing,
    arrived,
    sent,
    total,
    received,
    grads,
    back,
    seq_send,
    seq_recv,
    to_send,
    to_recv,
    halve_send,
    halve_recv,
    double_send,
    double_recv,
    back_send,
    back_recv,
):
    bits = count.bit_length() - 1
    me = lax.axis_index("dp")
    side = lax.axis_index("seq")
    far = 1 - side
    place = halving_place(me, count)
    depth = gate_ref.shape[0]
    hidden = gate_ref.shape[1]
    wide = 3 * hidden // 2

    barrier = pltpu.get_barrier_semaphore()
    pl.semaphore_signal(barrier, inc=1, device_id={"seq": far}, device_id_type=MESH)

    def greet(step, carry):
        pl.semaphore_signal(
            barrier, inc=1, device_id={"dp": lax.rem(me + step, count)}, device_id_type=MESH
        )
        return carry

    lax.fori_loop(1, count, greet, 0)
    pl.semaphore_wait(barrier, count)

    swap = pltpu.make_async_remote_copy(
        src_ref=slots_ref.at[far],
        dst_ref=theirs,
        send_sem=seq_send.at[0],
        recv_sem=seq_recv.at[0],
        device_id={"seq": far},
        device_id_type=MESH,
    )
    swap.start()
    back[...] = jnp.broadcast_to(facts_ref[...], back.shape)
    swap.wait()
    mine = slots_ref[side]
    came = theirs[...]
    first = jnp.where(side == 0, mine, came)
    second = jnp.where(side == 0, came, mine)
    outgoing[...] = jnp.concatenate(
        [first[:, :CAP], second[:, :CAP], first[:, CAP:], second[:, CAP:]], axis=1
    ).astype(jnp.bfloat16)

    def slice_copy(step):
        to = lax.rem(me + step, count)
        return pltpu.make_async_remote_copy(
            src_ref=outgoing.at[to],
            dst_ref=arrived.at[place],
            send_sem=to_send.at[step],
            recv_sem=to_recv.at[step],
            device_id={"dp": to},
            device_id_type=MESH,
        )

    def start_slice(step, carry):
        slice_copy(step).start()
        return carry

    def wait_slice(step, carry):
        slice_copy(step).wait()
        return carry

    lax.fori_loop(1, count, start_slice, 0)
    arrived[place] = outgoing[me]
    lax.fori_loop(1, count, wait_slice, 0)

    half = count // 2
    rows = EW * CAP
    tile = 512

    def products(start):
        block = arrived[pl.ds(start, half)].astype(jnp.float32)
        normed = block[:, :rows].reshape(half * rows, -1)[:, :depth].astype(jnp.bfloat16)
        upstream = block[:, rows:].reshape(half * rows, -1)[:, :depth].astype(jnp.bfloat16)

        def product(column):
            which, at = divmod(column, hidden)
            weight = (gate_ref, up_ref, down_ref)[which]
            return jnp.dot(
                upstream if which == 2 else normed,
                weight[:, at : at + tile],
                preferred_element_type=jnp.float32,
            ).reshape(half, rows, tile)

        for column in range(0, wide, tile):
            yield column, jnp.concatenate([product(column), product(wide + column)], axis=1)

    def halve_copy(stage):
        blocks = half >> stage
        return pltpu.make_async_remote_copy(
            src_ref=sent[stage],
            dst_ref=received[stage],
            send_sem=halve_send.at[stage],
            recv_sem=halve_recv.at[stage],
            device_id={"dp": flipped(me, 1 << stage)},
            device_id_type=MESH,
        )

    bit_of = [lax.rem(lax.div(me, 1 << stage), 2) for stage in range(bits)]
    for column, value in products((1 - bit_of[0]) * half):
        sent[0][:, :, column : column + tile] = value.astype(jnp.bfloat16)
    halve_copy(0).start()
    for column, value in products(bit_of[0] * half):
        total[:, :, column : column + tile] = value
    base = 0
    for stage in range(1, bits):
        blocks = half >> stage
        halve_copy(stage - 1).wait()
        away = (1 - bit_of[stage]) * blocks
        keep = bit_of[stage] * blocks
        sent[stage][...] = (
            total[pl.ds(base + away, blocks)]
            + received[stage - 1][pl.ds(away, blocks)].astype(jnp.float32)
        ).astype(jnp.bfloat16)
        halve_copy(stage).start()
        total[pl.ds(base + keep, blocks)] += received[stage - 1][pl.ds(keep, blocks)].astype(
            jnp.float32
        )
        base = base + keep
    halve_copy(bits - 1).wait()
    summed = total[base] + received[bits - 1][0].astype(jnp.float32)

    gate_pre = summed[:rows, :hidden]
    up_pre = jnp.concatenate([summed[:rows, hidden:], summed[rows:, : hidden // 2]], axis=1)
    grad_act = summed[rows:, hidden // 2 :]
    sigmoid_gate = 1.0 / (1.0 + jnp.exp(-GLU_SLOPE * gate_pre))
    gate_sigmoid = gate_pre * sigmoid_gate
    raised_up = up_pre + 1.0
    activation = (raised_up * gate_sigmoid).astype(jnp.bfloat16).astype(jnp.float32)
    share = jnp.sum(activation * grad_act, axis=1, keepdims=True)
    grad_up = grad_act * gate_sigmoid
    grad_gate = (
        grad_act * raised_up * (sigmoid_gate + GLU_SLOPE * gate_sigmoid * (1.0 - sigmoid_gate))
    )
    grads[place] = jnp.concatenate([grad_gate, grad_up], axis=0).astype(jnp.bfloat16)

    for stage in range(bits):
        blocks = 1 << stage
        start = place // blocks * blocks
        copy = pltpu.make_async_remote_copy(
            src_ref=grads.at[pl.ds(start, blocks)],
            dst_ref=grads.at[pl.ds(start, blocks)],
            send_sem=double_send.at[stage],
            recv_sem=double_recv.at[stage],
            device_id={"dp": flipped(me, half >> stage)},
            device_id_type=MESH,
        )
        copy.start()
        copy.wait()

    flat = grads[...].reshape(count * 2 * rows, hidden)
    contract = (((1,), (1,)), ((), ()))
    from_gate = lax.dot_general(flat, gate_ref[...], contract, preferred_element_type=jnp.float32)
    from_up = lax.dot_general(flat, up_ref[...], contract, preferred_element_type=jnp.float32)
    from_gate = from_gate.reshape(count, 2 * rows, depth)
    from_up = from_up.reshape(count, 2 * rows, depth)
    back[:, :, :depth] = from_gate[:, :rows] + from_up[:, rows:]

    def back_copy(step):
        to = lax.rem(me + step, count)
        return pltpu.make_async_remote_copy(
            src_ref=back.at[halving_place(to, count)],
            dst_ref=own_ref.at[me],
            send_sem=back_send.at[step],
            recv_sem=back_recv.at[step],
            device_id={"dp": to},
            device_id_type=MESH,
        )

    def start_back(step, carry):
        back_copy(step).start()
        return carry

    def wait_back(step, carry):
        back_copy(step).wait()
        return carry

    lax.fori_loop(1, count, start_back, 0)
    own_ref[me] = back[place]
    own_ref[count] = jnp.broadcast_to(share, own_ref.shape[1:])
    lax.fori_loop(1, count, wait_back, 0)
    last = pltpu.make_async_remote_copy(
        src_ref=own_ref,
        dst_ref=other_ref,
        send_sem=seq_send.at[1],
        recv_sem=seq_recv.at[1],
        device_id={"seq": far},
        device_id_type=MESH,
    )
    last.start()
    last.wait()


def in_place_experts(slots, facts, gate, up, down):
    count, lanes = slots.shape[1], slots.shape[3]
    bits = count.bit_length() - 1
    rows = EW * CAP
    hidden = gate.shape[1]
    wide = 3 * hidden // 2
    stages = [pltpu.VMEM((count >> (stage + 1), 2 * rows, wide), jnp.bfloat16) for stage in range(bits)]
    vmem = pl.BlockSpec(memory_space=pltpu.VMEM)
    dma = pltpu.SemaphoreType.DMA
    result = jax.ShapeDtypeStruct((count + 1, rows, lanes), jnp.float32)
    return pl.pallas_call(
        functools.partial(expert_kernel, count),
        out_shape=(result, result),
        in_specs=[vmem] * 5,
        out_specs=(vmem, vmem),
        scratch_shapes=[
            pltpu.VMEM((count, rows, lanes), jnp.float32),
            pltpu.VMEM((count, 2 * rows, lanes), jnp.bfloat16),
            pltpu.VMEM((count, 2 * rows, lanes), jnp.bfloat16),
            stages,
            pltpu.VMEM((count // 2, 2 * rows, wide), jnp.float32),
            stages,
            pltpu.VMEM((count, 2 * rows, hidden), jnp.bfloat16),
            pltpu.VMEM((count, rows, lanes), jnp.float32),
            dma((2,)),
            dma((2,)),
            dma((count,)),
            dma((count,)),
            dma((bits,)),
            dma((bits,)),
            dma((bits,)),
            dma((bits,)),
            dma((count,)),
            dma((count,)),
        ],
        compiler_params=pltpu.CompilerParams(
            collective_id=1, has_side_effects=True, vmem_limit_bytes=40 * MIB
        ),
        name="expert_kernel",
    )(slots, facts, gate, up, down)


def attend(
    group, side, queries_ref, key_block, value_block, sinks_ref, attended_ref, probs_ref, sink_probs_ref
):
    tokens = queries_ref.shape[0]
    span = 2 * tokens
    shared_heads = QUERY_HEADS // KEY_VALUE_HEADS
    stacked = (tokens, span)
    row = lax.broadcasted_iota(jnp.int32, stacked, 0)
    col = lax.broadcasted_iota(jnp.int32, stacked, 1)
    allowed = (col >= row + 1) & (col <= row + tokens) & (col + side * tokens >= tokens)
    lanes = slice(group * HEAD_SIZE, (group + 1) * HEAD_SIZE)
    group_keys = key_block[:, :, lanes].reshape(span, HEAD_SIZE)
    group_values = value_block[:, :, lanes].reshape(span, HEAD_SIZE)
    mixed = []
    for head in range(group * shared_heads, (group + 1) * shared_heads):
        scores = lax.dot_general(
            queries_ref[:, head * HEAD_SIZE : (head + 1) * HEAD_SIZE],
            group_keys,
            (((1,), (1,)), ((), ())),
            preferred_element_type=jnp.float32,
        )
        scores = jnp.where(allowed, scores * HEAD_SIZE ** (-0.5), -1e30)
        sink = sinks_ref[head : head + 1, :1]
        largest = jnp.maximum(jnp.max(scores, axis=1, keepdims=True), sink)
        raised = jnp.where(allowed, jnp.exp(scores - largest), 0.0)
        sink_raised = jnp.exp(sink - largest)
        denominator = jnp.sum(raised, axis=1, keepdims=True) + sink_raised
        probs = raised / denominator
        probs_ref[head] = probs
        sink_probs_ref[head] = sink_raised / denominator
        mixed.append(
            jnp.dot(
                probs.astype(jnp.bfloat16), group_values, preferred_element_type=jnp.float32
            )
        )
        if len(mixed) * HEAD_SIZE == 128:
            end = (head + 1) * HEAD_SIZE
            attended_ref[:, end - 128 : end] = jnp.concatenate(mixed, axis=1).astype(
                jnp.bfloat16
            )
            mixed = []


def gather_kernel(
    count,
    weight_ref,
    queries_ref,
    keys_ref,
    values_ref,
    sinks_ref,
    full_ref,
    attended_ref,
    probs_ref,
    sink_probs_ref,
    key_block,
    value_block,
    halo_send,
    halo_recv,
    own_sem,
    line_send,
    line_recv,
    pair_send,
    pair_recv,
    side_send,
    side_recv,
    core_send,
    core_recv,
):
    line = count // 4
    waves = line - 1
    me = lax.axis_index("dp")
    side = lax.axis_index("seq")
    core, pair, spot = lax.rem(me, 2), lax.rem(lax.div(me, 2), 2), lax.div(me, 4)
    rows = weight_ref.shape[0]
    lone = rows * 3 // 128 * 16
    shared = rows - 2 * lone
    lone_start = pl.multiple_of(side * (lone + shared), 16)
    plane_start = pl.multiple_of(side * lone, 16)
    far_start = pl.multiple_of((1 - side) * (lone + shared), 16)
    chunks = ((lone_start, lone), (lone, shared))

    def index(spot, pair, core):
        return (spot * 2 + pair) * 2 + core

    def part(owner, start, size, own=False):
        if own:
            return weight_ref.at[pl.ds(start, size)]
        return full_ref.at[owner, pl.ds(start, size)]

    def remote(owner, own, start, size, send, recv, target):
        return pltpu.make_async_remote_copy(
            src_ref=part(owner, start, size, own),
            dst_ref=part(owner, start, size),
            send_sem=send,
            recv_sem=recv,
            device_id=target,
            device_id_type=MESH,
        )

    def shard_spot(way, wave):
        return spot - 1 - wave if way == 0 else spot + 1 + wave

    def arrives(way, wave):
        return spot - 1 - wave >= 0 if way == 0 else spot + 1 + wave < line

    def leaves(way, wave):
        if way == 0:
            return (spot + 1 < line) & (spot - wave >= 0)
        return (spot >= 1) & (spot + wave < line)

    def line_copy(way, wave, chunk):
        step = 1 if way == 0 else -1
        owner = index(spot - step * wave, pair, core)
        return remote(
            owner,
            wave == 0,
            *chunks[chunk],
            line_send.at[way, wave, chunk],
            line_recv.at[way, wave, chunk],
            {"dp": index(spot + step, pair, core)},
        )

    def slot(piece):
        return 0 if piece is None else 1 + 2 * piece[1] + piece[0]

    def owner_of(piece, other_pair):
        at = spot if piece is None else shard_spot(*piece)
        return index(at, 1 - pair if other_pair else pair, core)

    def pair_copy(piece, chunk):
        at = slot(piece)
        return remote(
            owner_of(piece, False),
            piece is None,
            *chunks[chunk],
            pair_send.at[at, chunk],
            pair_recv.at[at, chunk],
            {"dp": index(spot, 1 - pair, core)},
        )

    def side_copy(piece, other_pair):
        at = slot(piece)
        return remote(
            owner_of(piece, other_pair),
            False,
            lone_start,
            lone,
            side_send.at[other_pair, at],
            side_recv.at[other_pair, at],
            {"seq": 1 - side},
        )

    def core_copy(piece, other_pair, from_side):
        at = slot(piece)
        if piece is None and other_pair == 0:
            start, size = 0, rows
        elif from_side:
            start, size = far_start, lone
        else:
            start, size = plane_start, lone + shared
        return remote(
            owner_of(piece, other_pair),
            piece is None and other_pair == 0,
            start,
            size,
            core_send.at[from_side, other_pair, at],
            core_recv.at[from_side, other_pair, at],
            {"dp": index(spot, pair, 1 - core)},
        )

    def held(piece, action):
        if piece is None:
            action()
        else:
            pl.when(arrives(*piece))(action)

    barrier = pltpu.get_barrier_semaphore()

    def greet(target):
        pl.semaphore_signal(barrier, inc=1, device_id=target, device_id_type=MESH)

    greet({"seq": 1 - side})
    greet({"dp": index(spot, 1 - pair, core)})
    greet({"dp": index(spot, pair, 1 - core)})
    for way, step in ((0, 1), (1, -1)):

        @pl.when(leaves(way, 0))
        def _(step=step):
            greet({"dp": index(spot + step, pair, core)})

    neighbours = leaves(0, 0).astype(jnp.int32) + leaves(1, 0).astype(jnp.int32)
    pl.semaphore_wait(barrier, 3 + neighbours)

    keep = pltpu.make_async_copy(weight_ref, full_ref.at[me], own_sem)
    for chunk in (0, 1):
        for way in (0, 1):

            @pl.when(leaves(way, 0))
            def _(way=way, chunk=chunk):
                line_copy(way, 0, chunk).start()

        pair_copy(None, chunk).start()
    core_copy(None, 0, 0).start()
    keep.start()
    halos = [
        pltpu.make_async_remote_copy(
            src_ref=source,
            dst_ref=block.at[0],
            send_sem=halo_send.at[at],
            recv_sem=halo_recv.at[at],
            device_id={"seq": 1 - side},
            device_id_type=MESH,
        )
        for at, (source, block) in enumerate(((keys_ref, key_block), (values_ref, value_block)))
    ]
    for halo in halos:
        halo.start()
    key_block[1] = keys_ref[...]
    value_block[1] = values_ref[...]
    for halo in halos:
        halo.wait()

    def attend_group(group):
        attend(
            group,
            side,
            queries_ref,
            key_block,
            value_block,
            sinks_ref,
            attended_ref,
            probs_ref,
            sink_probs_ref,
        )

    groups = list(range(KEY_VALUE_HEADS))
    attend_group(groups.pop())

    def line_step(wave):
        for chunk in (0, 1):
            for way in (0, 1):

                @pl.when(arrives(way, wave))
                def _(way=way, chunk=chunk):
                    piece = (way, wave)
                    line_copy(way, wave, chunk).wait_recv()
                    if wave + 1 < waves:

                        @pl.when(leaves(way, wave + 1))
                        def _():
                            line_copy(way, wave + 1, chunk).start()

                    pair_copy(piece, chunk).start()
                    if chunk == 0:
                        side_copy(piece, 0).start()
                    else:
                        core_copy(piece, 0, 0).start()

    def pair_step(pieces):
        for chunk in (0, 1):
            for piece in pieces:

                def arrive(piece=piece, chunk=chunk):
                    pair_copy(piece, chunk).wait_recv()
                    if chunk == 0:
                        side_copy(piece, 1).start()
                    else:
                        core_copy(piece, 1, 0).start()

                held(piece, arrive)

    def side_step(pieces, other_pair):
        for piece in pieces:

            def arrive(piece=piece):
                side_copy(piece, other_pair).wait_recv()
                core_copy(piece, other_pair, 1).start()

            held(piece, arrive)

    waved = [[(0, wave), (1, wave)] for wave in range(waves)]
    ordered = [[None]] + waved
    for wave in range(waves):
        line_step(wave)
        if groups:
            attend_group(groups.pop())
        pair_step(ordered[wave])
        if groups:
            attend_group(groups.pop())
        if wave:
            side_step(waved[wave - 1], 0)
            side_step(ordered[wave - 1], 1)
    for group in groups:
        attend_group(group)
    pair_step(ordered[waves])
    side_step(waved[waves - 1], 0)
    side_step(ordered[waves - 1], 1)
    side_step(ordered[waves], 1)

    keep.wait()
    for piece in [None] + sum(waved, []):

        def finish(piece=piece):
            for chunk in (0, 1):
                pair_copy(piece, chunk).wait_send()
            for other_pair in (0, 1):
                core_copy(piece, other_pair, 0).wait()
                if piece is not None or other_pair:
                    side_copy(piece, other_pair).wait_send()
                    core_copy(piece, other_pair, 1).wait()

        held(piece, finish)
    for wave in range(waves):
        for way in (0, 1):

            @pl.when(leaves(way, wave))
            def _(way=way, wave=wave):
                for chunk in (0, 1):
                    line_copy(way, wave, chunk).wait_send()


def gather_and_attend(weight, queries, keys, values, sinks, count):
    waves = count // 4 - 1
    slots = 1 + 2 * waves
    dma = pltpu.SemaphoreType.DMA
    hbm = pl.BlockSpec(memory_space=pl.ANY)
    vmem = pl.BlockSpec(memory_space=pltpu.VMEM)
    tokens = queries.shape[0]
    sink_rows = jnp.broadcast_to(sinks[:, None], (QUERY_HEADS, 128))
    full, attended, probs, sink_probs, key_block, value_block = pl.pallas_call(
        functools.partial(gather_kernel, count),
        out_shape=(
            jax.ShapeDtypeStruct((count,) + weight.shape, weight.dtype),
            jax.ShapeDtypeStruct(queries.shape, jnp.bfloat16),
            jax.ShapeDtypeStruct((QUERY_HEADS, tokens, 2 * tokens), jnp.float32),
            jax.ShapeDtypeStruct((QUERY_HEADS, tokens, 1), jnp.float32),
            jax.ShapeDtypeStruct((2,) + keys.shape, keys.dtype),
            jax.ShapeDtypeStruct((2,) + values.shape, values.dtype),
        ),
        in_specs=[vmem] * 5,
        out_specs=(hbm,) + (vmem,) * 5,
        scratch_shapes=[
            dma((2,)),
            dma((2,)),
            dma,
            dma((2, waves, 2)),
            dma((2, waves, 2)),
            dma((slots, 2)),
            dma((slots, 2)),
            dma((2, slots)),
            dma((2, slots)),
            dma((2, 2, slots)),
            dma((2, 2, slots)),
        ],
        compiler_params=pltpu.CompilerParams(
            collective_id=2, has_side_effects=True, vmem_limit_bytes=40 * MIB
        ),
        name="gather_kernel",
    )(weight, queries, keys, values, sink_rows)
    full = full.reshape(count * weight.shape[0], weight.shape[1])
    return full, attended, probs, sink_probs, key_block, value_block


def tail_kernel(
    count,
    queries_ref,
    key_block,
    value_block,
    probs_ref,
    sink_probs_ref,
    mixed_ref,
    grad_queries_ref,
    grad_keys_ref,
    grad_values_ref,
    sums_ref,
    score_grads,
    outgoing,
    came,
    sinks,
    parts,
    half,
    far_half,
    dp_send,
    dp_recv,
    seq_send,
    seq_recv,
):
    me = lax.axis_index("dp")
    side = lax.axis_index("seq")
    far = 1 - side
    barrier = pltpu.get_barrier_semaphore()
    pl.semaphore_signal(barrier, inc=1, device_id={"seq": far}, device_id_type=MESH)

    def greet(step, carry):
        pl.semaphore_signal(
            barrier, inc=1, device_id={"dp": lax.rem(me + step, count)}, device_id_type=MESH
        )
        return carry

    lax.fori_loop(1, count, greet, 0)

    tokens = queries_ref.shape[0]
    span = 2 * tokens
    shared_heads = QUERY_HEADS // KEY_VALUE_HEADS
    scaling = HEAD_SIZE ** (-0.5)
    contract_last = (((1,), (1,)), ((), ()))
    contract_first = (((0,), (0,)), ((), ()))

    def lanes(head):
        return slice(head * HEAD_SIZE, (head + 1) * HEAD_SIZE)

    own_keys, own_values = [], []
    for group in range(KEY_VALUE_HEADS):
        group_values = value_block[:, :, lanes(group)].reshape(span, HEAD_SIZE)
        key_grad = jnp.zeros((span, HEAD_SIZE), jnp.float32)
        value_grad = jnp.zeros((span, HEAD_SIZE), jnp.float32)
        for head in range(group * shared_heads, (group + 1) * shared_heads):
            mixed = mixed_ref[:, lanes(head)]
            probs = probs_ref[head]
            prob_grad = lax.dot_general(
                mixed, group_values, contract_last, preferred_element_type=jnp.float32
            )
            spread = jnp.sum(probs * prob_grad, axis=1, keepdims=True)
            sinks[head : head + 1] = jnp.broadcast_to(
                -jnp.sum(sink_probs_ref[head] * spread, axis=0, keepdims=True), (1, 128)
            )
            score_grad = (probs * (prob_grad - spread)).astype(jnp.bfloat16)
            score_grads[head] = score_grad
            key_grad += lax.dot_general(
                score_grad,
                queries_ref[:, lanes(head)],
                contract_first,
                preferred_element_type=jnp.float32,
            )
            value_grad += lax.dot_general(
                probs.astype(jnp.bfloat16),
                mixed,
                contract_first,
                preferred_element_type=jnp.float32,
            )
        own_keys.append(key_grad * scaling)
        own_values.append(value_grad)
    key_grad = jnp.concatenate(own_keys, axis=1)
    value_grad = jnp.concatenate(own_values, axis=1)
    outgoing[0] = key_grad[:tokens].astype(jnp.bfloat16)
    outgoing[1] = value_grad[:tokens].astype(jnp.bfloat16)

    pl.semaphore_wait(barrier, count)

    def across(source, target, at):
        return pltpu.make_async_remote_copy(
            src_ref=source,
            dst_ref=target,
            send_sem=seq_send.at[at],
            recv_sem=seq_recv.at[at],
            device_id={"seq": far},
            device_id_type=MESH,
        )

    def part_copy(step):
        return pltpu.make_async_remote_copy(
            src_ref=sinks,
            dst_ref=parts.at[me],
            send_sem=dp_send.at[step],
            recv_sem=dp_recv.at[step],
            device_id={"dp": lax.rem(me + step, count)},
            device_id_type=MESH,
        )

    def start_part(step, carry):
        part_copy(step).start()
        return carry

    def wait_part(step, carry):
        part_copy(step).wait()
        return carry

    halo = across(outgoing, came, 0)
    halo.start()
    lax.fori_loop(1, count, start_part, 0)
    parts[me] = sinks[...]

    def query_grads(group):
        group_keys = key_block[:, :, lanes(group)].reshape(span, HEAD_SIZE)
        pieces = []
        for head in range(group * shared_heads, (group + 1) * shared_heads):
            pieces.append(
                jnp.dot(score_grads[head], group_keys, preferred_element_type=jnp.float32) * scaling
            )
        start = group * shared_heads * HEAD_SIZE
        grad_queries_ref[:, start : start + shared_heads * HEAD_SIZE] = jnp.concatenate(
            pieces, axis=1
        ).astype(jnp.bfloat16)

    early = KEY_VALUE_HEADS // 2
    for group in range(early):
        query_grads(group)
    lax.fori_loop(1, count, wait_part, 0)
    half[...] = jnp.sum(parts[...], axis=0)
    swap = across(half, far_half, 1)
    swap.start()
    for group in range(early, KEY_VALUE_HEADS):
        query_grads(group)
    halo.wait()
    taken = jnp.where(side == 0, came[...].astype(jnp.float32), 0.0)
    grad_keys_ref[...] = (key_grad[tokens:] + taken[0]).astype(jnp.bfloat16)
    grad_values_ref[...] = (value_grad[tokens:] + taken[1]).astype(jnp.bfloat16)
    swap.wait()
    sums_ref[...] = half[...] + far_half[...]


def attention_backward(queries, key_block, value_block, probs, sink_probs, mixed, count):
    vmem = pl.BlockSpec(memory_space=pltpu.VMEM)
    dma = pltpu.SemaphoreType.DMA
    tile = (QUERY_HEADS, 128)
    rows = jax.ShapeDtypeStruct(key_block.shape[1:], jnp.bfloat16)
    grad_queries, grad_keys, grad_values, sums = pl.pallas_call(
        functools.partial(tail_kernel, count),
        out_shape=(
            jax.ShapeDtypeStruct(queries.shape, jnp.bfloat16),
            rows,
            rows,
            jax.ShapeDtypeStruct(tile, jnp.float32),
        ),
        in_specs=[vmem] * 6,
        out_specs=(vmem,) * 4,
        scratch_shapes=[
            pltpu.VMEM(probs.shape, jnp.bfloat16),
            pltpu.VMEM(key_block.shape, jnp.bfloat16),
            pltpu.VMEM(key_block.shape, jnp.bfloat16),
            pltpu.VMEM(tile, jnp.float32),
            pltpu.VMEM((count,) + tile, jnp.float32),
            pltpu.VMEM(tile, jnp.float32),
            pltpu.VMEM(tile, jnp.float32),
            dma((count,)),
            dma((count,)),
            dma((2,)),
            dma((2,)),
        ],
        compiler_params=pltpu.CompilerParams(
            collective_id=3, has_side_effects=True, vmem_limit_bytes=40 * MIB
        ),
        name="tail_kernel",
    )(queries, key_block, value_block, probs, sink_probs, mixed)
    return grad_queries, grad_keys, grad_values, sums[:, 0]


def shards(
    queries,
    key_rows,
    value_matrix,
    head_sink_logits,
    residual,
    out_weight,
    norm_gain,
    router,
    expert_gate,
    expert_up,
    expert_down,
    routes,
    group_ids,
    rewards,
    response_mask,
    upstream,
):
    seq_count = lax.axis_size("seq")
    dp_count = lax.axis_size("dp")
    seq_index = lax.axis_index("seq")
    query_rows = queries[0]
    own_keys = key_rows[0]
    own_values = value_matrix[0]
    tokens_here = query_rows.shape[0]
    group_count = max(dp_count // 4, 1)
    all_tokens = dp_count * seq_count * tokens_here
    group_hot = (group_ids[0] == jnp.arange(group_count, dtype=jnp.int32)).astype(jnp.float32)
    reward = rewards[0].astype(jnp.float32)
    group_terms = (
        group_hot[:, None] * jnp.stack([jnp.ones_like(reward), reward, reward * reward])[None, :]
    )
    mask_wide = response_mask[0].astype(jnp.float32)
    local_count = jnp.sum(mask_wide)
    first_device = (seq_index == 0).astype(jnp.float32)
    out_full, attended, probs, sink_probs, key_block, value_block = gather_and_attend(
        out_weight, query_rows, own_keys, own_values, head_sink_logits, dp_count
    )
    projected = jnp.dot(attended, out_full, preferred_element_type=jnp.float32)
    mid_rows = lax.optimization_barrier(
        (residual[0].astype(jnp.float32) + projected).astype(jnp.bfloat16)
    )
    mid_wide = mid_rows.astype(jnp.float32)
    inv_rms = lax.rsqrt(jnp.mean(mid_wide * mid_wide, axis=1, keepdims=True) + NORM_EPS)
    unit_rows = mid_wide * inv_rms
    normed = (unit_rows * norm_gain[None, :]).astype(jnp.bfloat16)
    logits = jnp.dot(normed, router, preferred_element_type=jnp.float32)
    route_hot = routes[0][:, :, None] == jnp.arange(EXPERTS, dtype=jnp.int32)[None, None, :]
    route_logits = jnp.sum(jnp.where(route_hot, logits[:, None, :], 0.0), axis=2)
    raised = jnp.exp(route_logits)
    route_weights = raised / jnp.sum(raised, axis=1, keepdims=True)
    member = route_hot[:, :, :EW]
    expert_share = jnp.sum(jnp.where(member, route_weights[:, :, None], 0.0), axis=1)
    chosen = jnp.any(member, axis=1)
    slot_rank = jnp.cumsum(chosen.astype(jnp.int32), axis=0) - 1
    slot_hot = chosen[:, :, None] & (
        slot_rank[:, :, None] == jnp.arange(CAP, dtype=jnp.int32)[None, None, :]
    )
    slot_low = slot_hot.astype(jnp.bfloat16)
    slot_wide = slot_hot.astype(jnp.float32)
    slot_rows = jnp.einsum(
        "tec,td->ecd", slot_low, normed, preferred_element_type=jnp.float32
    )
    share_slots = jnp.einsum("tec,te->ec", slot_wide, expert_share, precision=HIGHEST)
    upstream_slots = jnp.einsum(
        "tec,td->ecd", slot_low, upstream[0], preferred_element_type=jnp.float32
    )
    depth = expert_gate.shape[0]
    lanes = -(-depth // 128) * 128
    slots = jnp.concatenate([slot_rows, upstream_slots], axis=1)
    slots = slots.reshape(EW, 2 * CAP, dp_count, depth).transpose(0, 2, 1, 3)
    facts = jnp.concatenate([(group_terms * first_device).reshape(-1), local_count[None]])
    lanes = max(lanes, -(-(depth + facts.shape[0]) // 128) * 128)
    slots = jnp.pad(slots, ((0, 0), (0, 0), (0, 0), (0, lanes - depth)))
    facts = jnp.pad(facts, (depth, lanes - depth - facts.shape[0]))
    facts = jnp.broadcast_to(facts, (EW * CAP, lanes))
    own_part, other_part = in_place_experts(slots, facts, expert_gate, expert_up, expert_down)
    totals = jnp.sum(own_part[:dp_count, 0] + other_part[:dp_count, 0], axis=0)[depth:]
    group_totals = totals[: group_terms.size].reshape(group_terms.shape)
    token_total = totals[group_terms.size]
    group_sizes = group_totals[:, 0]
    group_means = group_totals[:, 1] / group_sizes
    group_spread = group_totals[:, 2] / group_sizes - group_means * group_means
    own_mean = jnp.sum(group_hot * group_means)
    own_spread = jnp.sum(group_hot * group_spread)
    advantage = (reward - own_mean) / jnp.sqrt(jnp.maximum(own_spread, 1.0))
    token_scale = -advantage * all_tokens / token_total
    loss_weight = token_scale * mask_wide
    weight_slots = jnp.einsum("tec,t->ec", slot_wide, loss_weight, precision=HIGHEST)
    both_parts = jnp.where(
        seq_index == 0, jnp.stack([own_part, other_part]), jnp.stack([other_part, own_part])
    )
    both_parts = lax.dynamic_slice_in_dim(both_parts, seq_index * CAP, CAP, 2)
    grad_share_slots = weight_slots * both_parts[:, dp_count, :, 0]
    grad_rows = (
        both_parts[:, :dp_count, :, :depth].transpose(0, 2, 1, 3).reshape(EW, CAP, D)
        * (weight_slots * share_slots)[:, :, None]
    )
    grad_normed_moe = jnp.einsum("tec,ecd->td", slot_wide, grad_rows, precision=HIGHEST)
    grad_share = jnp.einsum("tec,ec->te", slot_wide, grad_share_slots, precision=HIGHEST)
    grad_weights = jnp.sum(jnp.where(member, grad_share[:, None, :], 0.0), axis=2)
    grad_route = route_weights * (
        grad_weights - jnp.sum(route_weights * grad_weights, axis=1, keepdims=True)
    )
    grad_logits = jnp.sum(jnp.where(route_hot, grad_route[:, :, None], 0.0), axis=1).astype(
        jnp.bfloat16
    )
    grad_normed = (
        lax.dot_general(grad_logits, router, CONTRACT_LAST, preferred_element_type=jnp.float32)
        + grad_normed_moe
    )
    grad_unit = grad_normed * norm_gain[None, :]
    grad_mid = loss_weight[:, None] * upstream[0].astype(jnp.float32) + inv_rms * (
        grad_unit - unit_rows * jnp.mean(grad_unit * unit_rows, axis=1, keepdims=True)
    )
    grad_residual = grad_mid.astype(jnp.bfloat16)
    grad_attended = lax.dot_general(
        grad_residual, out_full, CONTRACT_LAST, preferred_element_type=jnp.float32
    ).astype(jnp.bfloat16)
    grad_queries, grad_keys, grad_values, grad_sinks = attention_backward(
        query_rows, key_block, value_block, probs, sink_probs, grad_attended, dp_count
    )
    return (
        grad_queries[None],
        grad_keys[None],
        grad_values[None],
        grad_residual[None],
        grad_sinks,
    )


def solution(mesh):
    seq_count, dp_count = mesh.shape["seq"], mesh.shape["dp"]
    in_place = seq_count == EW and dp_count >= 8 and dp_count & (dp_count - 1) == 0
    return jax.shard_map(
        shards if in_place else general_shards,
        mesh=mesh,
        in_specs=(
            P("dp", "seq", None),
            P("dp", "seq", None),
            P("dp", "seq", None),
            P(),
            P("dp", "seq", None),
            P("dp", None),
            P(),
            P(),
            P("dp", "seq"),
            P("dp", "seq"),
            P("dp", "seq"),
            P("dp", "seq", None),
            P("dp"),
            P("dp"),
            P("dp", "seq"),
            P("dp", "seq", None),
        ),
        out_specs=(
            P("dp", "seq", None),
            P("dp", "seq", None),
            P("dp", "seq", None),
            P("dp", "seq", None),
            P(),
        ),
        check_vma=False,
    )
```

```python
import functools

import jax
import jax.numpy as jnp
from jax import lax
from jax.experimental import pallas as pl
from jax.experimental.pallas import tpu as pltpu
from jax.sharding import PartitionSpec as P

D = 2880
HEAD_SIZE = 64
WINDOW = 128
EXPERTS = 128
QUERY_HEADS = 32
KEY_VALUE_HEADS = 4
EW = 2
CAP = 4


NORM_EPS = 1e-05
GLU_SLOPE = 1.702
HIGHEST = lax.Precision.HIGHEST
CONTRACT_LAST = (((1,), (1,)), ((), ()))


def passed_along(value, axis, steps):
    count = lax.axis_size(axis)
    initial, last = (max(0, -steps), min(count, count - steps))
    return lax.ppermute(value, axis, [(source, source + steps) for source in range(initial, last)])


def glu_forward(gate_pre, up_pre):
    return ((up_pre + 1.0) * gate_pre * jax.nn.sigmoid(GLU_SLOPE * gate_pre)).astype(jnp.bfloat16)


def glu_grads(grad_act, gate_pre, up_pre):
    sigmoid_gate = jax.nn.sigmoid(GLU_SLOPE * gate_pre)
    grad_up = grad_act * (gate_pre * sigmoid_gate)
    grad_gate = (
        grad_act
        * (up_pre + 1.0)
        * (sigmoid_gate + GLU_SLOPE * gate_pre * sigmoid_gate * (1.0 - sigmoid_gate))
    )
    return (grad_gate, grad_up)


def head_scores(query_tile_block, key_tile_block, head_sink_logits, allowed):
    query_total_count = query_tile_block.shape[0]
    key_total_count = key_tile_block.shape[0]
    query_head_rows = query_tile_block.reshape(
        query_total_count, KEY_VALUE_HEADS, QUERY_HEADS // KEY_VALUE_HEADS, HEAD_SIZE
    )
    key_head_rows = key_tile_block.reshape(key_total_count, KEY_VALUE_HEADS, HEAD_SIZE)
    attention_scores = jnp.einsum(
        "baqj,eaj->aqbe", query_head_rows, key_head_rows, preferred_element_type=jnp.float32
    ) * HEAD_SIZE ** (-0.5)
    attention_scores = jnp.where(allowed[None, None], attention_scores, -1e30)
    sink_logit_column = head_sink_logits.reshape(KEY_VALUE_HEADS, QUERY_HEADS // KEY_VALUE_HEADS)[
        :, :, None
    ]
    largest = jnp.maximum(jnp.max(attention_scores, axis=3), sink_logit_column)
    raised = jnp.where(allowed[None, None], jnp.exp(attention_scores - largest[..., None]), 0.0)
    sink_raised = jnp.exp(sink_logit_column - largest)
    denominator = jnp.sum(raised, axis=3) + sink_raised
    return (raised / denominator[..., None], sink_raised / denominator)


def head_mix(reduced_probabilities, value_tile_block):
    key_total_count = value_tile_block.shape[0]
    value_head_rows = value_tile_block.reshape(key_total_count, KEY_VALUE_HEADS, HEAD_SIZE)
    mixed_output = jnp.einsum(
        "amlh,hai->lami", reduced_probabilities, value_head_rows, preferred_element_type=jnp.float32
    )
    return mixed_output.reshape(mixed_output.shape[0], QUERY_HEADS * HEAD_SIZE).astype(jnp.bfloat16)


def head_grads(
    probs,
    reduced_probabilities,
    sink_probs,
    query_tile_block,
    key_tile_block,
    value_tile_block,
    mixed_gradient,
):
    query_total_count = query_tile_block.shape[0]
    key_total_count = key_tile_block.shape[0]
    query_head_rows = query_tile_block.reshape(
        query_total_count, KEY_VALUE_HEADS, QUERY_HEADS // KEY_VALUE_HEADS, HEAD_SIZE
    )
    key_head_rows = key_tile_block.reshape(key_total_count, KEY_VALUE_HEADS, HEAD_SIZE)
    value_head_rows = value_tile_block.reshape(key_total_count, KEY_VALUE_HEADS, HEAD_SIZE)
    heads_gradient = mixed_gradient.reshape(
        query_total_count, KEY_VALUE_HEADS, QUERY_HEADS // KEY_VALUE_HEADS, HEAD_SIZE
    )
    probability_gradient = jnp.einsum(
        "baqj,eaj->aqbe", heads_gradient, value_head_rows, preferred_element_type=jnp.float32
    )
    spread = jnp.sum(probs * probability_gradient, axis=3)
    score_gradient = (probs * (probability_gradient - spread[..., None])).astype(jnp.bfloat16)
    head_scaling = HEAD_SIZE ** (-0.5)
    query_gradient = (
        jnp.einsum(
            "amlh,hai->lami", score_gradient, key_head_rows, preferred_element_type=jnp.float32
        )
        * head_scaling
    )
    key_gradient = (
        jnp.einsum(
            "ujko,kujm->oum", score_gradient, query_head_rows, preferred_element_type=jnp.float32
        )
        * head_scaling
    )
    value_gradient = jnp.einsum(
        "ujko,kujm->oum", reduced_probabilities, heads_gradient, preferred_element_type=jnp.float32
    )
    sink_gradient = -jnp.sum(sink_probs * spread, axis=2).reshape(QUERY_HEADS)
    return (
        query_gradient.reshape(query_total_count, QUERY_HEADS * HEAD_SIZE).astype(jnp.bfloat16),
        key_gradient.reshape(key_total_count, KEY_VALUE_HEADS * HEAD_SIZE),
        value_gradient.reshape(key_total_count, KEY_VALUE_HEADS * HEAD_SIZE),
        sink_gradient,
    )


def block_backward(grad_flat, gate_pre, up_pre, gate_full, up_full, down_full):
    grad_act = jnp.dot(grad_flat, down_full, preferred_element_type=jnp.float32)
    grad_gate, grad_up = glu_grads(grad_act, gate_pre, up_pre)
    grad_pair = jnp.concatenate([grad_gate, grad_up], axis=1).astype(jnp.bfloat16)
    weight_pair = jnp.concatenate([gate_full, up_full], axis=1)
    return lax.dot_general(
        grad_pair, weight_pair, CONTRACT_LAST, preferred_element_type=jnp.float32
    ).astype(jnp.bfloat16)


def general_shards(
    queries,
    key_rows,
    value_matrix,
    head_sink_logits,
    residual,
    out_weight,
    norm_gain,
    router,
    expert_gate,
    expert_up,
    expert_down,
    routes,
    group_ids,
    rewards,
    response_mask,
    upstream,
):
    seq_count = lax.axis_size("seq")
    dp_count = lax.axis_size("dp")
    seq_index = lax.axis_index("seq")
    query_rows = queries[0]
    own_keys = key_rows[0]
    own_values = value_matrix[0]
    tokens_here = query_rows.shape[0]
    pieces = seq_count // EW
    group_count = max(dp_count // 4, 1)
    all_tokens = dp_count * seq_count * tokens_here
    group_hot = (group_ids[0] == jnp.arange(group_count, dtype=jnp.int32)).astype(jnp.float32)
    reward = rewards[0].astype(jnp.float32)
    group_terms = (
        group_hot[:, None] * jnp.stack([jnp.ones_like(reward), reward, reward * reward])[None, :]
    )
    mask_wide = response_mask[0].astype(jnp.float32)
    local_count = jnp.sum(mask_wide)
    first_device = (seq_index == 0).astype(jnp.float32)
    group_totals, token_total = lax.psum((group_terms * first_device, local_count), ("seq", "dp"))
    group_sizes = group_totals[:, 0]
    group_means = group_totals[:, 1] / group_sizes
    group_spread = group_totals[:, 2] / group_sizes - group_means * group_means
    own_mean = jnp.sum(group_hot * group_means)
    own_spread = jnp.sum(group_hot * group_spread)
    advantage = (reward - own_mean) / jnp.sqrt(jnp.maximum(own_spread, 1.0))
    token_scale = -advantage * all_tokens / token_total
    loss_weight = token_scale * mask_wide
    halo_keys, halo_values = passed_along((own_keys, own_values), "seq", 1)
    key_tile_block = jnp.concatenate([halo_keys, own_keys], axis=0)
    value_tile_block = jnp.concatenate([halo_values, own_values], axis=0)
    row_index = jnp.arange(tokens_here, dtype=jnp.int32)[:, None]
    col_index = jnp.arange(WINDOW + tokens_here, dtype=jnp.int32)[None, :]
    allowed = (
        (col_index >= row_index + 1)
        & (col_index <= row_index + WINDOW)
        & ((col_index >= WINDOW) | (seq_index > 0))
    )
    probs, sink_probs = head_scores(query_rows, key_tile_block, head_sink_logits, allowed)
    reduced_probabilities = probs.astype(jnp.bfloat16)
    attended = head_mix(reduced_probabilities, value_tile_block)
    out_full = lax.all_gather(out_weight, "dp", axis=0, tiled=True)
    projected = jnp.dot(attended, out_full, preferred_element_type=jnp.float32)
    mid_rows = lax.optimization_barrier(
        (residual[0].astype(jnp.float32) + projected).astype(jnp.bfloat16)
    )
    mid_wide = mid_rows.astype(jnp.float32)
    inv_rms = lax.rsqrt(jnp.mean(mid_wide * mid_wide, axis=1, keepdims=True) + NORM_EPS)
    unit_rows = mid_wide * inv_rms
    normed = (unit_rows * norm_gain[None, :]).astype(jnp.bfloat16)
    logits = jnp.dot(normed, router, preferred_element_type=jnp.float32)
    route_hot = routes[0][:, :, None] == jnp.arange(EXPERTS, dtype=jnp.int32)[None, None, :]
    route_logits = jnp.sum(jnp.where(route_hot, logits[:, None, :], 0.0), axis=2)
    raised = jnp.exp(route_logits)
    route_weights = raised / jnp.sum(raised, axis=1, keepdims=True)
    member = route_hot[:, :, :EW]
    expert_share = jnp.sum(jnp.where(member, route_weights[:, :, None], 0.0), axis=1)
    chosen = jnp.any(member, axis=1)
    slot_rank = jnp.cumsum(chosen.astype(jnp.int32), axis=0) - 1
    slot_hot = chosen[:, :, None] & (
        slot_rank[:, :, None] == jnp.arange(CAP, dtype=jnp.int32)[None, None, :]
    )
    slot_low = slot_hot.astype(jnp.bfloat16)
    slot_wide = slot_hot.astype(jnp.float32)
    slot_rows = jnp.einsum(
        "tec,td->ecd", slot_low, normed, preferred_element_type=jnp.float32
    ).astype(jnp.bfloat16)
    outgoing = jnp.broadcast_to(slot_rows[:, None], (EW, pieces, CAP, D)).reshape(seq_count, CAP, D)
    upstream_slots = jnp.einsum(
        "tec,td->ecd", slot_low, upstream[0], preferred_element_type=jnp.float32
    )
    weight_slots = jnp.einsum("tec,t->ec", slot_wide, loss_weight, precision=HIGHEST)
    share_slots = jnp.einsum("tec,te->ec", slot_wide, expert_share, precision=HIGHEST)
    cot_slots = weight_slots[:, :, None] * upstream_slots
    grad_out = (share_slots[:, :, None] * cot_slots).astype(jnp.bfloat16)
    grad_outgoing = jnp.broadcast_to(grad_out[:, None], (EW, pieces, CAP, D)).reshape(
        seq_count, CAP, D
    )
    gate_full, up_full, down_full = (
        lax.all_gather(expert_gate, "dp", axis=0, tiled=True),
        lax.all_gather(expert_up, "dp", axis=0, tiled=True),
        lax.all_gather(expert_down, "dp", axis=0, tiled=True),
    )
    arrived = lax.all_to_all(outgoing, "seq", split_axis=0, concat_axis=0, tiled=True)
    senders = arrived.shape[0]
    items = arrived.shape[1]
    block_senders = arrived.shape[0]
    block_items = arrived.shape[1]
    flat_rows = arrived.reshape(block_senders * block_items, D)
    gate_pre = jnp.dot(flat_rows, gate_full, preferred_element_type=jnp.float32)
    up_pre = jnp.dot(flat_rows, up_full, preferred_element_type=jnp.float32)
    activation = glu_forward(gate_pre, up_pre)
    partial_out = lax.dot_general(
        activation, down_full, CONTRACT_LAST, preferred_element_type=jnp.float32
    ).astype(jnp.bfloat16)
    partial_out, gate_pre, up_pre = (
        partial_out.reshape(block_senders, block_items, D),
        gate_pre,
        up_pre,
    )
    back_out = lax.all_to_all(partial_out, "seq", split_axis=0, concat_axis=0, tiled=True)
    gate_held = gate_pre.reshape(senders, items, -1)
    up_held = up_pre.reshape(senders, items, -1)
    grad_arrived = lax.all_to_all(grad_outgoing, "seq", split_axis=0, concat_axis=0, tiled=True)
    grad_piece = block_backward(
        grad_arrived.reshape(seq_count * CAP, D),
        gate_held.reshape(seq_count * CAP, -1),
        up_held.reshape(seq_count * CAP, -1),
        gate_full,
        up_full,
        down_full,
    )
    grad_back = lax.all_to_all(
        grad_piece.reshape(seq_count, CAP, D), "seq", split_axis=0, concat_axis=0, tiled=True
    )
    expert_out = jnp.sum(back_out.reshape(EW, pieces, CAP, D).astype(jnp.float32), axis=1)
    grad_share_slots = jnp.sum(cot_slots * expert_out, axis=2)
    grad_rows = jnp.sum(grad_back.reshape(EW, pieces, CAP, D).astype(jnp.float32), axis=1)
    grad_normed_moe = jnp.einsum("tec,ecd->td", slot_wide, grad_rows, precision=HIGHEST)
    grad_share = jnp.einsum("tec,ec->te", slot_wide, grad_share_slots, precision=HIGHEST)
    grad_weights = jnp.sum(jnp.where(member, grad_share[:, None, :], 0.0), axis=2)
    grad_route = route_weights * (
        grad_weights - jnp.sum(route_weights * grad_weights, axis=1, keepdims=True)
    )
    grad_logits = jnp.sum(jnp.where(route_hot, grad_route[:, :, None], 0.0), axis=1).astype(
        jnp.bfloat16
    )
    grad_normed = (
        lax.dot_general(grad_logits, router, CONTRACT_LAST, preferred_element_type=jnp.float32)
        + grad_normed_moe
    )
    grad_unit = grad_normed * norm_gain[None, :]
    grad_mid = loss_weight[:, None] * upstream[0].astype(jnp.float32) + inv_rms * (
        grad_unit - unit_rows * jnp.mean(grad_unit * unit_rows, axis=1, keepdims=True)
    )
    grad_residual = grad_mid.astype(jnp.bfloat16)
    grad_attended = lax.dot_general(
        grad_residual, out_full, CONTRACT_LAST, preferred_element_type=jnp.float32
    ).astype(jnp.bfloat16)
    query_gradient, key_gradient, value_gradient, sink_gradient = head_grads(
        probs,
        reduced_probabilities,
        sink_probs,
        query_rows,
        key_tile_block,
        value_tile_block,
        grad_attended,
    )
    next_keys, next_values = (
        passed_along(key_gradient[:WINDOW].astype(jnp.bfloat16), "seq", -1).astype(jnp.float32),
        passed_along(value_gradient[:WINDOW].astype(jnp.bfloat16), "seq", -1).astype(jnp.float32),
    )
    own_key_grad = key_gradient[WINDOW:]
    own_value_grad = value_gradient[WINDOW:]
    split_at = tokens_here - WINDOW
    grad_key_rows = jnp.concatenate(
        [own_key_grad[:split_at], own_key_grad + next_keys], axis=0
    ).astype(jnp.bfloat16)
    grad_value_rows = jnp.concatenate(
        [own_value_grad[:split_at], own_value_grad + next_values], axis=0
    ).astype(jnp.bfloat16)
    grad_sinks = lax.psum(sink_gradient, ("seq", "dp"))
    return (
        query_gradient[None],
        grad_key_rows[None],
        grad_value_rows[None],
        grad_residual[None],
        grad_sinks,
    )


MESH = pl.DeviceIdType.MESH
MIB = 1 << 20


def halving_place(index, count):
    place, weight, rest = 0, count // 2, index
    while weight:
        place = place + lax.rem(rest, 2) * weight
        rest = lax.div(rest, 2)
        weight //= 2
    return place


def flipped(index, bit):
    return index + bit - 2 * bit * lax.rem(lax.div(index, bit), 2)


def expert_kernel(
    count,
    slots_ref,
    facts_ref,
    gate_ref,
    up_ref,
    down_ref,
    own_ref,
    other_ref,
    theirs,
    outgoing,
    arrived,
    sent,
    total,
    received,
    grads,
    back,
    seq_send,
    seq_recv,
    to_send,
    to_recv,
    halve_send,
    halve_recv,
    double_send,
    double_recv,
    back_send,
    back_recv,
):
    bits = count.bit_length() - 1
    me = lax.axis_index("dp")
    side = lax.axis_index("seq")
    far = 1 - side
    place = halving_place(me, count)
    depth = gate_ref.shape[0]
    hidden = gate_ref.shape[1]
    wide = 3 * hidden // 2

    barrier = pltpu.get_barrier_semaphore()
    pl.semaphore_signal(barrier, inc=1, device_id={"seq": far}, device_id_type=MESH)

    def greet(step, carry):
        pl.semaphore_signal(
            barrier, inc=1, device_id={"dp": lax.rem(me + step, count)}, device_id_type=MESH
        )
        return carry

    lax.fori_loop(1, count, greet, 0)
    pl.semaphore_wait(barrier, count)

    swap = pltpu.make_async_remote_copy(
        src_ref=slots_ref.at[far],
        dst_ref=theirs,
        send_sem=seq_send.at[0],
        recv_sem=seq_recv.at[0],
        device_id={"seq": far},
        device_id_type=MESH,
    )
    swap.start()
    back[...] = jnp.broadcast_to(facts_ref[...], back.shape)
    swap.wait()
    mine = slots_ref[side]
    came = theirs[...]
    first = jnp.where(side == 0, mine, came)
    second = jnp.where(side == 0, came, mine)
    outgoing[...] = jnp.concatenate(
        [first[:, :CAP], second[:, :CAP], first[:, CAP:], second[:, CAP:]], axis=1
    ).astype(jnp.bfloat16)

    def slice_copy(step):
        to = lax.rem(me + step, count)
        return pltpu.make_async_remote_copy(
            src_ref=outgoing.at[to],
            dst_ref=arrived.at[place],
            send_sem=to_send.at[step],
            recv_sem=to_recv.at[step],
            device_id={"dp": to},
            device_id_type=MESH,
        )

    def start_slice(step, carry):
        slice_copy(step).start()
        return carry

    def wait_slice(step, carry):
        slice_copy(step).wait()
        return carry

    lax.fori_loop(1, count, start_slice, 0)
    arrived[place] = outgoing[me]
    lax.fori_loop(1, count, wait_slice, 0)

    half = count // 2
    rows = EW * CAP
    tile = 512

    def products(start):
        block = arrived[pl.ds(start, half)].astype(jnp.float32)
        normed = block[:, :rows].reshape(half * rows, -1)[:, :depth].astype(jnp.bfloat16)
        upstream = block[:, rows:].reshape(half * rows, -1)[:, :depth].astype(jnp.bfloat16)

        def product(column):
            which, at = divmod(column, hidden)
            weight = (gate_ref, up_ref, down_ref)[which]
            return jnp.dot(
                upstream if which == 2 else normed,
                weight[:, at : at + tile],
                preferred_element_type=jnp.float32,
            ).reshape(half, rows, tile)

        def tile_at(column):
            return jnp.concatenate([product(column), product(wide + column)], axis=1)

        return tile_at

    def halve_copy(stage, chunk):
        at = pl.ds(chunk * width, width)
        return pltpu.make_async_remote_copy(
            src_ref=sent[stage].at[:, :, at],
            dst_ref=received[stage].at[:, :, at],
            send_sem=halve_send.at[stage, chunk],
            recv_sem=halve_recv.at[stage, chunk],
            device_id={"dp": flipped(me, 1 << stage)},
            device_id_type=MESH,
        )

    width = hidden // 2
    chunks = wide // width
    bit_of = [lax.rem(lax.div(me, 1 << stage), 2) for stage in range(bits)]
    tile_at = products((1 - bit_of[0]) * half)
    for chunk in range(chunks):
        for column in range(chunk * width, (chunk + 1) * width, tile):
            sent[0][:, :, column : column + tile] = tile_at(column).astype(jnp.bfloat16)
        halve_copy(0, chunk).start()
    tile_at = products(bit_of[0] * half)
    for column in range(0, wide, tile):
        total[:, :, column : column + tile] = tile_at(column)
    base = 0
    for stage in range(1, bits):
        blocks = half >> stage
        away = (1 - bit_of[stage]) * blocks
        keep = bit_of[stage] * blocks
        for chunk in range(chunks):
            at = slice(chunk * width, (chunk + 1) * width)
            halve_copy(stage - 1, chunk).wait()
            sent[stage][:, :, at] = (
                total[pl.ds(base + away, blocks), :, at]
                + received[stage - 1][pl.ds(away, blocks), :, at].astype(jnp.float32)
            ).astype(jnp.bfloat16)
            halve_copy(stage, chunk).start()
            total[pl.ds(base + keep, blocks), :, at] += received[stage - 1][
                pl.ds(keep, blocks), :, at
            ].astype(jnp.float32)
        base = base + keep
    for chunk in range(chunks):
        halve_copy(bits - 1, chunk).wait()
    summed = total[base] + received[bits - 1][0].astype(jnp.float32)

    gate_pre = summed[:rows, :hidden]
    up_pre = jnp.concatenate([summed[:rows, hidden:], summed[rows:, : hidden // 2]], axis=1)
    grad_act = summed[rows:, hidden // 2 :]
    sigmoid_gate = 1.0 / (1.0 + jnp.exp(-GLU_SLOPE * gate_pre))
    gate_sigmoid = gate_pre * sigmoid_gate
    raised_up = up_pre + 1.0
    activation = (raised_up * gate_sigmoid).astype(jnp.bfloat16).astype(jnp.float32)
    share = jnp.sum(activation * grad_act, axis=1, keepdims=True)
    grad_up = grad_act * gate_sigmoid
    grad_gate = (
        grad_act * raised_up * (sigmoid_gate + GLU_SLOPE * gate_sigmoid * (1.0 - sigmoid_gate))
    )
    grads[place] = jnp.concatenate([grad_gate, grad_up], axis=0).astype(jnp.bfloat16)

    def double_copy(stage, chunk):
        blocks = 1 << stage
        part = grads.at[pl.ds(place // blocks * blocks, blocks), :, pl.ds(chunk * width, width)]
        return pltpu.make_async_remote_copy(
            src_ref=part,
            dst_ref=part,
            send_sem=double_send.at[stage, chunk],
            recv_sem=double_recv.at[stage, chunk],
            device_id={"dp": flipped(me, half >> stage)},
            device_id_type=MESH,
        )

    for stage in range(bits):
        for chunk in range(2):
            if stage:
                double_copy(stage - 1, chunk).wait()
            double_copy(stage, chunk).start()

    contract = (((1,), (1,)), ((), ()))
    from_gate = jnp.zeros((count * 2 * rows, depth), jnp.float32)
    from_up = jnp.zeros((count * 2 * rows, depth), jnp.float32)
    for chunk in range(2):
        double_copy(bits - 1, chunk).wait()
        at = slice(chunk * width, (chunk + 1) * width)
        flat = grads[:, :, at].reshape(count * 2 * rows, width)
        from_gate += lax.dot_general(
            flat, gate_ref[:, at], contract, preferred_element_type=jnp.float32
        )
        from_up += lax.dot_general(flat, up_ref[:, at], contract, preferred_element_type=jnp.float32)
    from_gate = from_gate.reshape(count, 2 * rows, depth)
    from_up = from_up.reshape(count, 2 * rows, depth)
    back[:, :, :depth] = from_gate[:, :rows] + from_up[:, rows:]

    def back_copy(step):
        to = lax.rem(me + step, count)
        return pltpu.make_async_remote_copy(
            src_ref=back.at[halving_place(to, count)],
            dst_ref=own_ref.at[me],
            send_sem=back_send.at[step],
            recv_sem=back_recv.at[step],
            device_id={"dp": to},
            device_id_type=MESH,
        )

    def start_back(step, carry):
        back_copy(step).start()
        return carry

    def wait_back(step, carry):
        back_copy(step).wait()
        return carry

    lax.fori_loop(1, count, start_back, 0)
    own_ref[me] = back[place]
    own_ref[count] = jnp.broadcast_to(share, own_ref.shape[1:])
    lax.fori_loop(1, count, wait_back, 0)
    last = pltpu.make_async_remote_copy(
        src_ref=own_ref,
        dst_ref=other_ref,
        send_sem=seq_send.at[1],
        recv_sem=seq_recv.at[1],
        device_id={"seq": far},
        device_id_type=MESH,
    )
    last.start()
    last.wait()


def in_place_experts(slots, facts, gate, up, down):
    count, lanes = slots.shape[1], slots.shape[3]
    bits = count.bit_length() - 1
    rows = EW * CAP
    hidden = gate.shape[1]
    wide = 3 * hidden // 2
    stages = [pltpu.VMEM((count >> (stage + 1), 2 * rows, wide), jnp.bfloat16) for stage in range(bits)]
    vmem = pl.BlockSpec(memory_space=pltpu.VMEM)
    dma = pltpu.SemaphoreType.DMA
    result = jax.ShapeDtypeStruct((count + 1, rows, lanes), jnp.float32)
    return pl.pallas_call(
        functools.partial(expert_kernel, count),
        out_shape=(result, result),
        in_specs=[vmem] * 5,
        out_specs=(vmem, vmem),
        scratch_shapes=[
            pltpu.VMEM((count, rows, lanes), jnp.float32),
            pltpu.VMEM((count, 2 * rows, lanes), jnp.bfloat16),
            pltpu.VMEM((count, 2 * rows, lanes), jnp.bfloat16),
            stages,
            pltpu.VMEM((count // 2, 2 * rows, wide), jnp.float32),
            stages,
            pltpu.VMEM((count, 2 * rows, hidden), jnp.bfloat16),
            pltpu.VMEM((count, rows, lanes), jnp.float32),
            dma((2,)),
            dma((2,)),
            dma((count,)),
            dma((count,)),
            dma((bits, 3)),
            dma((bits, 3)),
            dma((bits, 2)),
            dma((bits, 2)),
            dma((count,)),
            dma((count,)),
        ],
        compiler_params=pltpu.CompilerParams(
            collective_id=1, has_side_effects=True, vmem_limit_bytes=40 * MIB
        ),
        name="expert_kernel",
    )(slots, facts, gate, up, down)


def attend(
    group, side, queries_ref, key_block, value_block, sinks_ref, attended_ref, probs_ref, sink_probs_ref
):
    tokens = queries_ref.shape[0]
    span = 2 * tokens
    shared_heads = QUERY_HEADS // KEY_VALUE_HEADS
    stacked = (tokens, span)
    row = lax.broadcasted_iota(jnp.int32, stacked, 0)
    col = lax.broadcasted_iota(jnp.int32, stacked, 1)
    allowed = (col >= row + 1) & (col <= row + tokens) & (col + side * tokens >= tokens)
    lanes = slice(group * HEAD_SIZE, (group + 1) * HEAD_SIZE)
    group_keys = key_block[:, :, lanes].reshape(span, HEAD_SIZE)
    group_values = value_block[:, :, lanes].reshape(span, HEAD_SIZE)
    mixed = []
    for head in range(group * shared_heads, (group + 1) * shared_heads):
        scores = lax.dot_general(
            queries_ref[:, head * HEAD_SIZE : (head + 1) * HEAD_SIZE],
            group_keys,
            (((1,), (1,)), ((), ())),
            preferred_element_type=jnp.float32,
        )
        scores = jnp.where(allowed, scores * HEAD_SIZE ** (-0.5), -1e30)
        sink = sinks_ref[head : head + 1, :1]
        largest = jnp.maximum(jnp.max(scores, axis=1, keepdims=True), sink)
        raised = jnp.where(allowed, jnp.exp(scores - largest), 0.0)
        sink_raised = jnp.exp(sink - largest)
        denominator = jnp.sum(raised, axis=1, keepdims=True) + sink_raised
        probs = raised / denominator
        probs_ref[head] = probs
        sink_probs_ref[head] = sink_raised / denominator
        mixed.append(
            jnp.dot(
                probs.astype(jnp.bfloat16), group_values, preferred_element_type=jnp.float32
            )
        )
        if len(mixed) * HEAD_SIZE == 128:
            end = (head + 1) * HEAD_SIZE
            attended_ref[:, end - 128 : end] = jnp.concatenate(mixed, axis=1).astype(
                jnp.bfloat16
            )
            mixed = []


def gather_kernel(
    count,
    weight_ref,
    queries_ref,
    keys_ref,
    values_ref,
    sinks_ref,
    full_ref,
    attended_ref,
    probs_ref,
    sink_probs_ref,
    key_block,
    value_block,
    halo_send,
    halo_recv,
    own_sem,
    line_send,
    line_recv,
    pair_send,
    pair_recv,
    side_send,
    side_recv,
    core_send,
    core_recv,
):
    line = count // 4
    waves = line - 1
    me = lax.axis_index("dp")
    side = lax.axis_index("seq")
    core, pair, spot = lax.rem(me, 2), lax.rem(lax.div(me, 2), 2), lax.div(me, 4)
    rows = weight_ref.shape[0]
    lone = rows * 3 // 128 * 16
    shared = rows - 2 * lone
    lone_start = pl.multiple_of(side * (lone + shared), 16)
    plane_start = pl.multiple_of(side * lone, 16)
    far_start = pl.multiple_of((1 - side) * (lone + shared), 16)
    chunks = ((lone_start, lone), (lone, shared))

    def index(spot, pair, core):
        return (spot * 2 + pair) * 2 + core

    def part(owner, start, size, own=False):
        if own:
            return weight_ref.at[pl.ds(start, size)]
        return full_ref.at[owner, pl.ds(start, size)]

    def remote(owner, own, start, size, send, recv, target):
        return pltpu.make_async_remote_copy(
            src_ref=part(owner, start, size, own),
            dst_ref=part(owner, start, size),
            send_sem=send,
            recv_sem=recv,
            device_id=target,
            device_id_type=MESH,
        )

    def shard_spot(way, wave):
        return spot - 1 - wave if way == 0 else spot + 1 + wave

    def arrives(way, wave):
        return spot - 1 - wave >= 0 if way == 0 else spot + 1 + wave < line

    def leaves(way, wave):
        if way == 0:
            return (spot + 1 < line) & (spot - wave >= 0)
        return (spot >= 1) & (spot + wave < line)

    def line_copy(way, wave, chunk):
        step = 1 if way == 0 else -1
        owner = index(spot - step * wave, pair, core)
        return remote(
            owner,
            wave == 0,
            *chunks[chunk],
            line_send.at[way, wave, chunk],
            line_recv.at[way, wave, chunk],
            {"dp": index(spot + step, pair, core)},
        )

    def slot(piece):
        return 0 if piece is None else 1 + 2 * piece[1] + piece[0]

    def owner_of(piece, other_pair):
        at = spot if piece is None else shard_spot(*piece)
        return index(at, 1 - pair if other_pair else pair, core)

    def pair_copy(piece, chunk):
        at = slot(piece)
        return remote(
            owner_of(piece, False),
            piece is None,
            *chunks[chunk],
            pair_send.at[at, chunk],
            pair_recv.at[at, chunk],
            {"dp": index(spot, 1 - pair, core)},
        )

    def side_copy(piece, other_pair):
        at = slot(piece)
        return remote(
            owner_of(piece, other_pair),
            False,
            lone_start,
            lone,
            side_send.at[other_pair, at],
            side_recv.at[other_pair, at],
            {"seq": 1 - side},
        )

    def core_copy(piece, other_pair, from_side):
        at = slot(piece)
        if piece is None and other_pair == 0:
            start, size = 0, rows
        elif from_side:
            start, size = far_start, lone
        else:
            start, size = plane_start, lone + shared
        return remote(
            owner_of(piece, other_pair),
            piece is None and other_pair == 0,
            start,
            size,
            core_send.at[from_side, other_pair, at],
            core_recv.at[from_side, other_pair, at],
            {"dp": index(spot, pair, 1 - core)},
        )

    def held(piece, action):
        if piece is None:
            action()
        else:
            pl.when(arrives(*piece))(action)

    barrier = pltpu.get_barrier_semaphore()

    def greet(target):
        pl.semaphore_signal(barrier, inc=1, device_id=target, device_id_type=MESH)

    greet({"seq": 1 - side})
    greet({"dp": index(spot, 1 - pair, core)})
    greet({"dp": index(spot, pair, 1 - core)})
    for way, step in ((0, 1), (1, -1)):

        @pl.when(leaves(way, 0))
        def _(step=step):
            greet({"dp": index(spot + step, pair, core)})

    neighbours = leaves(0, 0).astype(jnp.int32) + leaves(1, 0).astype(jnp.int32)
    pl.semaphore_wait(barrier, 3 + neighbours)

    keep = pltpu.make_async_copy(weight_ref, full_ref.at[me], own_sem)
    for chunk in (0, 1):
        for way in (0, 1):

            @pl.when(leaves(way, 0))
            def _(way=way, chunk=chunk):
                line_copy(way, 0, chunk).start()

        pair_copy(None, chunk).start()
    core_copy(None, 0, 0).start()
    keep.start()
    halos = [
        pltpu.make_async_remote_copy(
            src_ref=source,
            dst_ref=block.at[0],
            send_sem=halo_send.at[at],
            recv_sem=halo_recv.at[at],
            device_id={"seq": 1 - side},
            device_id_type=MESH,
        )
        for at, (source, block) in enumerate(((keys_ref, key_block), (values_ref, value_block)))
    ]
    for halo in halos:
        halo.start()
    key_block[1] = keys_ref[...]
    value_block[1] = values_ref[...]
    for halo in halos:
        halo.wait()

    def attend_group(group):
        attend(
            group,
            side,
            queries_ref,
            key_block,
            value_block,
            sinks_ref,
            attended_ref,
            probs_ref,
            sink_probs_ref,
        )

    groups = list(range(KEY_VALUE_HEADS))
    attend_group(groups.pop())

    def line_step(wave):
        for chunk in (0, 1):
            for way in (0, 1):

                @pl.when(arrives(way, wave))
                def _(way=way, chunk=chunk):
                    piece = (way, wave)
                    line_copy(way, wave, chunk).wait_recv()
                    if wave + 1 < waves:

                        @pl.when(leaves(way, wave + 1))
                        def _():
                            line_copy(way, wave + 1, chunk).start()

                    pair_copy(piece, chunk).start()
                    if chunk == 0:
                        side_copy(piece, 0).start()
                    else:
                        core_copy(piece, 0, 0).start()

    def pair_step(pieces):
        for chunk in (0, 1):
            for piece in pieces:

                def arrive(piece=piece, chunk=chunk):
                    pair_copy(piece, chunk).wait_recv()
                    if chunk == 0:
                        side_copy(piece, 1).start()
                    else:
                        core_copy(piece, 1, 0).start()

                held(piece, arrive)

    def side_step(pieces, other_pair):
        for piece in pieces:

            def arrive(piece=piece):
                side_copy(piece, other_pair).wait_recv()
                core_copy(piece, other_pair, 1).start()

            held(piece, arrive)

    waved = [[(0, wave), (1, wave)] for wave in range(waves)]
    ordered = [[None]] + waved
    for wave in range(waves):
        line_step(wave)
        if groups:
            attend_group(groups.pop())
        pair_step(ordered[wave])
        if groups:
            attend_group(groups.pop())
        if wave:
            side_step(waved[wave - 1], 0)
            side_step(ordered[wave - 1], 1)
    for group in groups:
        attend_group(group)
    pair_step(ordered[waves])
    side_step(waved[waves - 1], 0)
    side_step(ordered[waves - 1], 1)
    side_step(ordered[waves], 1)

    keep.wait()
    for piece in [None] + sum(waved, []):

        def finish(piece=piece):
            for chunk in (0, 1):
                pair_copy(piece, chunk).wait_send()
            for other_pair in (0, 1):
                core_copy(piece, other_pair, 0).wait()
                if piece is not None or other_pair:
                    side_copy(piece, other_pair).wait_send()
                    core_copy(piece, other_pair, 1).wait()

        held(piece, finish)
    for wave in range(waves):
        for way in (0, 1):

            @pl.when(leaves(way, wave))
            def _(way=way, wave=wave):
                for chunk in (0, 1):
                    line_copy(way, wave, chunk).wait_send()


def gather_and_attend(weight, queries, keys, values, sinks, count):
    waves = count // 4 - 1
    slots = 1 + 2 * waves
    dma = pltpu.SemaphoreType.DMA
    hbm = pl.BlockSpec(memory_space=pl.ANY)
    vmem = pl.BlockSpec(memory_space=pltpu.VMEM)
    tokens = queries.shape[0]
    sink_rows = jnp.broadcast_to(sinks[:, None], (QUERY_HEADS, 128))
    full, attended, probs, sink_probs, key_block, value_block = pl.pallas_call(
        functools.partial(gather_kernel, count),
        out_shape=(
            jax.ShapeDtypeStruct((count,) + weight.shape, weight.dtype),
            jax.ShapeDtypeStruct(queries.shape, jnp.bfloat16),
            jax.ShapeDtypeStruct((QUERY_HEADS, tokens, 2 * tokens), jnp.float32),
            jax.ShapeDtypeStruct((QUERY_HEADS, tokens, 1), jnp.float32),
            jax.ShapeDtypeStruct((2,) + keys.shape, keys.dtype),
            jax.ShapeDtypeStruct((2,) + values.shape, values.dtype),
        ),
        in_specs=[vmem] * 5,
        out_specs=(hbm,) + (vmem,) * 5,
        scratch_shapes=[
            dma((2,)),
            dma((2,)),
            dma,
            dma((2, waves, 2)),
            dma((2, waves, 2)),
            dma((slots, 2)),
            dma((slots, 2)),
            dma((2, slots)),
            dma((2, slots)),
            dma((2, 2, slots)),
            dma((2, 2, slots)),
        ],
        compiler_params=pltpu.CompilerParams(
            collective_id=2, has_side_effects=True, vmem_limit_bytes=40 * MIB
        ),
        name="gather_kernel",
    )(weight, queries, keys, values, sink_rows)
    full = full.reshape(count * weight.shape[0], weight.shape[1])
    return full, attended, probs, sink_probs, key_block, value_block


def tail_kernel(
    count,
    queries_ref,
    key_block,
    value_block,
    probs_ref,
    sink_probs_ref,
    mixed_ref,
    grad_queries_ref,
    grad_keys_ref,
    grad_values_ref,
    sums_ref,
    score_grads,
    outgoing,
    came,
    sinks,
    parts,
    half,
    far_half,
    dp_send,
    dp_recv,
    seq_send,
    seq_recv,
):
    me = lax.axis_index("dp")
    side = lax.axis_index("seq")
    far = 1 - side
    barrier = pltpu.get_barrier_semaphore()
    pl.semaphore_signal(barrier, inc=1, device_id={"seq": far}, device_id_type=MESH)

    def greet(step, carry):
        pl.semaphore_signal(
            barrier, inc=1, device_id={"dp": lax.rem(me + step, count)}, device_id_type=MESH
        )
        return carry

    lax.fori_loop(1, count, greet, 0)

    tokens = queries_ref.shape[0]
    span = 2 * tokens
    shared_heads = QUERY_HEADS // KEY_VALUE_HEADS
    scaling = HEAD_SIZE ** (-0.5)
    contract_last = (((1,), (1,)), ((), ()))
    contract_first = (((0,), (0,)), ((), ()))

    def lanes(head):
        return slice(head * HEAD_SIZE, (head + 1) * HEAD_SIZE)

    own_keys, own_values = [], []
    for group in range(KEY_VALUE_HEADS):
        group_values = value_block[:, :, lanes(group)].reshape(span, HEAD_SIZE)
        key_grad = jnp.zeros((span, HEAD_SIZE), jnp.float32)
        value_grad = jnp.zeros((span, HEAD_SIZE), jnp.float32)
        for head in range(group * shared_heads, (group + 1) * shared_heads):
            mixed = mixed_ref[:, lanes(head)]
            probs = probs_ref[head]
            prob_grad = lax.dot_general(
                mixed, group_values, contract_last, preferred_element_type=jnp.float32
            )
            spread = jnp.sum(probs * prob_grad, axis=1, keepdims=True)
            sinks[head : head + 1] = jnp.broadcast_to(
                -jnp.sum(sink_probs_ref[head] * spread, axis=0, keepdims=True), (1, 128)
            )
            score_grad = (probs * (prob_grad - spread)).astype(jnp.bfloat16)
            score_grads[head] = score_grad
            key_grad += lax.dot_general(
                score_grad,
                queries_ref[:, lanes(head)],
                contract_first,
                preferred_element_type=jnp.float32,
            )
            value_grad += lax.dot_general(
                probs.astype(jnp.bfloat16),
                mixed,
                contract_first,
                preferred_element_type=jnp.float32,
            )
        own_keys.append(key_grad * scaling)
        own_values.append(value_grad)
    key_grad = jnp.concatenate(own_keys, axis=1)
    value_grad = jnp.concatenate(own_values, axis=1)
    outgoing[0] = key_grad[:tokens].astype(jnp.bfloat16)
    outgoing[1] = value_grad[:tokens].astype(jnp.bfloat16)

    pl.semaphore_wait(barrier, count)

    def across(source, target, at):
        return pltpu.make_async_remote_copy(
            src_ref=source,
            dst_ref=target,
            send_sem=seq_send.at[at],
            recv_sem=seq_recv.at[at],
            device_id={"seq": far},
            device_id_type=MESH,
        )

    def part_copy(step):
        return pltpu.make_async_remote_copy(
            src_ref=sinks,
            dst_ref=parts.at[me],
            send_sem=dp_send.at[step],
            recv_sem=dp_recv.at[step],
            device_id={"dp": lax.rem(me + step, count)},
            device_id_type=MESH,
        )

    def start_part(step, carry):
        part_copy(step).start()
        return carry

    def wait_part(step, carry):
        part_copy(step).wait()
        return carry

    halo = across(outgoing, came, 0)
    halo.start()
    lax.fori_loop(1, count, start_part, 0)
    parts[me] = sinks[...]

    def query_grads(group):
        group_keys = key_block[:, :, lanes(group)].reshape(span, HEAD_SIZE)
        pieces = []
        for head in range(group * shared_heads, (group + 1) * shared_heads):
            pieces.append(
                jnp.dot(score_grads[head], group_keys, preferred_element_type=jnp.float32) * scaling
            )
        start = group * shared_heads * HEAD_SIZE
        grad_queries_ref[:, start : start + shared_heads * HEAD_SIZE] = jnp.concatenate(
            pieces, axis=1
        ).astype(jnp.bfloat16)

    early = KEY_VALUE_HEADS // 2
    for group in range(early):
        query_grads(group)
    lax.fori_loop(1, count, wait_part, 0)
    half[...] = jnp.sum(parts[...], axis=0)
    swap = across(half, far_half, 1)
    swap.start()
    for group in range(early, KEY_VALUE_HEADS):
        query_grads(group)
    halo.wait()
    taken = jnp.where(side == 0, came[...].astype(jnp.float32), 0.0)
    grad_keys_ref[...] = (key_grad[tokens:] + taken[0]).astype(jnp.bfloat16)
    grad_values_ref[...] = (value_grad[tokens:] + taken[1]).astype(jnp.bfloat16)
    swap.wait()
    sums_ref[...] = half[...] + far_half[...]


def attention_backward(queries, key_block, value_block, probs, sink_probs, mixed, count):
    vmem = pl.BlockSpec(memory_space=pltpu.VMEM)
    dma = pltpu.SemaphoreType.DMA
    tile = (QUERY_HEADS, 128)
    rows = jax.ShapeDtypeStruct(key_block.shape[1:], jnp.bfloat16)
    grad_queries, grad_keys, grad_values, sums = pl.pallas_call(
        functools.partial(tail_kernel, count),
        out_shape=(
            jax.ShapeDtypeStruct(queries.shape, jnp.bfloat16),
            rows,
            rows,
            jax.ShapeDtypeStruct(tile, jnp.float32),
        ),
        in_specs=[vmem] * 6,
        out_specs=(vmem,) * 4,
        scratch_shapes=[
            pltpu.VMEM(probs.shape, jnp.bfloat16),
            pltpu.VMEM(key_block.shape, jnp.bfloat16),
            pltpu.VMEM(key_block.shape, jnp.bfloat16),
            pltpu.VMEM(tile, jnp.float32),
            pltpu.VMEM((count,) + tile, jnp.float32),
            pltpu.VMEM(tile, jnp.float32),
            pltpu.VMEM(tile, jnp.float32),
            dma((count,)),
            dma((count,)),
            dma((2,)),
            dma((2,)),
        ],
        compiler_params=pltpu.CompilerParams(
            collective_id=3, has_side_effects=True, vmem_limit_bytes=40 * MIB
        ),
        name="tail_kernel",
    )(queries, key_block, value_block, probs, sink_probs, mixed)
    return grad_queries, grad_keys, grad_values, sums[:, 0]


def shards(
    queries,
    key_rows,
    value_matrix,
    head_sink_logits,
    residual,
    out_weight,
    norm_gain,
    router,
    expert_gate,
    expert_up,
    expert_down,
    routes,
    group_ids,
    rewards,
    response_mask,
    upstream,
):
    seq_count = lax.axis_size("seq")
    dp_count = lax.axis_size("dp")
    seq_index = lax.axis_index("seq")
    query_rows = queries[0]
    own_keys = key_rows[0]
    own_values = value_matrix[0]
    tokens_here = query_rows.shape[0]
    group_count = max(dp_count // 4, 1)
    all_tokens = dp_count * seq_count * tokens_here
    group_hot = (group_ids[0] == jnp.arange(group_count, dtype=jnp.int32)).astype(jnp.float32)
    reward = rewards[0].astype(jnp.float32)
    group_terms = (
        group_hot[:, None] * jnp.stack([jnp.ones_like(reward), reward, reward * reward])[None, :]
    )
    mask_wide = response_mask[0].astype(jnp.float32)
    local_count = jnp.sum(mask_wide)
    first_device = (seq_index == 0).astype(jnp.float32)
    out_full, attended, probs, sink_probs, key_block, value_block = gather_and_attend(
        out_weight, query_rows, own_keys, own_values, head_sink_logits, dp_count
    )
    projected = jnp.dot(attended, out_full, preferred_element_type=jnp.float32)
    mid_rows = lax.optimization_barrier(
        (residual[0].astype(jnp.float32) + projected).astype(jnp.bfloat16)
    )
    mid_wide = mid_rows.astype(jnp.float32)
    inv_rms = lax.rsqrt(jnp.mean(mid_wide * mid_wide, axis=1, keepdims=True) + NORM_EPS)
    unit_rows = mid_wide * inv_rms
    normed = (unit_rows * norm_gain[None, :]).astype(jnp.bfloat16)
    logits = jnp.dot(normed, router, preferred_element_type=jnp.float32)
    route_hot = routes[0][:, :, None] == jnp.arange(EXPERTS, dtype=jnp.int32)[None, None, :]
    route_logits = jnp.sum(jnp.where(route_hot, logits[:, None, :], 0.0), axis=2)
    raised = jnp.exp(route_logits)
    route_weights = raised / jnp.sum(raised, axis=1, keepdims=True)
    member = route_hot[:, :, :EW]
    expert_share = jnp.sum(jnp.where(member, route_weights[:, :, None], 0.0), axis=1)
    chosen = jnp.any(member, axis=1)
    slot_rank = jnp.cumsum(chosen.astype(jnp.int32), axis=0) - 1
    slot_hot = chosen[:, :, None] & (
        slot_rank[:, :, None] == jnp.arange(CAP, dtype=jnp.int32)[None, None, :]
    )
    slot_low = slot_hot.astype(jnp.bfloat16)
    slot_wide = slot_hot.astype(jnp.float32)
    slot_rows = jnp.einsum(
        "tec,td->ecd", slot_low, normed, preferred_element_type=jnp.float32
    )
    share_slots = jnp.einsum("tec,te->ec", slot_wide, expert_share, precision=HIGHEST)
    upstream_slots = jnp.einsum(
        "tec,td->ecd", slot_low, upstream[0], preferred_element_type=jnp.float32
    )
    depth = expert_gate.shape[0]
    lanes = -(-depth // 128) * 128
    slots = jnp.concatenate([slot_rows, upstream_slots], axis=1)
    slots = slots.reshape(EW, 2 * CAP, dp_count, depth).transpose(0, 2, 1, 3)
    facts = jnp.concatenate([(group_terms * first_device).reshape(-1), local_count[None]])
    lanes = max(lanes, -(-(depth + facts.shape[0]) // 128) * 128)
    slots = jnp.pad(slots, ((0, 0), (0, 0), (0, 0), (0, lanes - depth)))
    facts = jnp.pad(facts, (depth, lanes - depth - facts.shape[0]))
    facts = jnp.broadcast_to(facts, (EW * CAP, lanes))
    own_part, other_part = in_place_experts(slots, facts, expert_gate, expert_up, expert_down)
    totals = jnp.sum(own_part[:dp_count, 0] + other_part[:dp_count, 0], axis=0)[depth:]
    group_totals = totals[: group_terms.size].reshape(group_terms.shape)
    token_total = totals[group_terms.size]
    group_sizes = group_totals[:, 0]
    group_means = group_totals[:, 1] / group_sizes
    group_spread = group_totals[:, 2] / group_sizes - group_means * group_means
    own_mean = jnp.sum(group_hot * group_means)
    own_spread = jnp.sum(group_hot * group_spread)
    advantage = (reward - own_mean) / jnp.sqrt(jnp.maximum(own_spread, 1.0))
    token_scale = -advantage * all_tokens / token_total
    loss_weight = token_scale * mask_wide
    weight_slots = jnp.einsum("tec,t->ec", slot_wide, loss_weight, precision=HIGHEST)
    both_parts = jnp.where(
        seq_index == 0, jnp.stack([own_part, other_part]), jnp.stack([other_part, own_part])
    )
    both_parts = lax.dynamic_slice_in_dim(both_parts, seq_index * CAP, CAP, 2)
    grad_share_slots = weight_slots * both_parts[:, dp_count, :, 0]
    grad_rows = (
        both_parts[:, :dp_count, :, :depth].transpose(0, 2, 1, 3).reshape(EW, CAP, D)
        * (weight_slots * share_slots)[:, :, None]
    )
    grad_normed_moe = jnp.einsum("tec,ecd->td", slot_wide, grad_rows, precision=HIGHEST)
    grad_share = jnp.einsum("tec,ec->te", slot_wide, grad_share_slots, precision=HIGHEST)
    grad_weights = jnp.sum(jnp.where(member, grad_share[:, None, :], 0.0), axis=2)
    grad_route = route_weights * (
        grad_weights - jnp.sum(route_weights * grad_weights, axis=1, keepdims=True)
    )
    grad_logits = jnp.sum(jnp.where(route_hot, grad_route[:, :, None], 0.0), axis=1).astype(
        jnp.bfloat16
    )
    grad_normed = (
        lax.dot_general(grad_logits, router, CONTRACT_LAST, preferred_element_type=jnp.float32)
        + grad_normed_moe
    )
    grad_unit = grad_normed * norm_gain[None, :]
    grad_mid = loss_weight[:, None] * upstream[0].astype(jnp.float32) + inv_rms * (
        grad_unit - unit_rows * jnp.mean(grad_unit * unit_rows, axis=1, keepdims=True)
    )
    grad_residual = grad_mid.astype(jnp.bfloat16)
    grad_attended = lax.dot_general(
        grad_residual, out_full, CONTRACT_LAST, preferred_element_type=jnp.float32
    ).astype(jnp.bfloat16)
    grad_queries, grad_keys, grad_values, grad_sinks = attention_backward(
        query_rows, key_block, value_block, probs, sink_probs, grad_attended, dp_count
    )
    return (
        grad_queries[None],
        grad_keys[None],
        grad_values[None],
        grad_residual[None],
        grad_sinks,
    )


def solution(mesh):
    seq_count, dp_count = mesh.shape["seq"], mesh.shape["dp"]
    in_place = seq_count == EW and dp_count >= 8 and dp_count & (dp_count - 1) == 0
    return jax.shard_map(
        shards if in_place else general_shards,
        mesh=mesh,
        in_specs=(
            P("dp", "seq", None),
            P("dp", "seq", None),
            P("dp", "seq", None),
            P(),
            P("dp", "seq", None),
            P("dp", None),
            P(),
            P(),
            P("dp", "seq"),
            P("dp", "seq"),
            P("dp", "seq"),
            P("dp", "seq", None),
            P("dp"),
            P("dp"),
            P("dp", "seq"),
            P("dp", "seq", None),
        ),
        out_specs=(
            P("dp", "seq", None),
            P("dp", "seq", None),
            P("dp", "seq", None),
            P("dp", "seq", None),
            P(),
        ),
        check_vma=False,
    )
```

```python
import functools

import jax
import jax.numpy as jnp
from jax import lax
from jax.experimental import pallas as pl
from jax.experimental.pallas import tpu as pltpu
from jax.sharding import PartitionSpec as P

D = 2880
HEAD_SIZE = 64
WINDOW = 128
EXPERTS = 128
QUERY_HEADS = 32
KEY_VALUE_HEADS = 4
EW = 2
CAP = 4


NORM_EPS = 1e-05
GLU_SLOPE = 1.702
HIGHEST = lax.Precision.HIGHEST
CONTRACT_LAST = (((1,), (1,)), ((), ()))


def passed_along(value, axis, steps):
    count = lax.axis_size(axis)
    initial, last = (max(0, -steps), min(count, count - steps))
    return lax.ppermute(value, axis, [(source, source + steps) for source in range(initial, last)])


def glu_forward(gate_pre, up_pre):
    return ((up_pre + 1.0) * gate_pre * jax.nn.sigmoid(GLU_SLOPE * gate_pre)).astype(jnp.bfloat16)


def glu_grads(grad_act, gate_pre, up_pre):
    sigmoid_gate = jax.nn.sigmoid(GLU_SLOPE * gate_pre)
    grad_up = grad_act * (gate_pre * sigmoid_gate)
    grad_gate = (
        grad_act
        * (up_pre + 1.0)
        * (sigmoid_gate + GLU_SLOPE * gate_pre * sigmoid_gate * (1.0 - sigmoid_gate))
    )
    return (grad_gate, grad_up)


def head_scores(query_tile_block, key_tile_block, head_sink_logits, allowed):
    query_total_count = query_tile_block.shape[0]
    key_total_count = key_tile_block.shape[0]
    query_head_rows = query_tile_block.reshape(
        query_total_count, KEY_VALUE_HEADS, QUERY_HEADS // KEY_VALUE_HEADS, HEAD_SIZE
    )
    key_head_rows = key_tile_block.reshape(key_total_count, KEY_VALUE_HEADS, HEAD_SIZE)
    attention_scores = jnp.einsum(
        "baqj,eaj->aqbe", query_head_rows, key_head_rows, preferred_element_type=jnp.float32
    ) * HEAD_SIZE ** (-0.5)
    attention_scores = jnp.where(allowed[None, None], attention_scores, -1e30)
    sink_logit_column = head_sink_logits.reshape(KEY_VALUE_HEADS, QUERY_HEADS // KEY_VALUE_HEADS)[
        :, :, None
    ]
    largest = jnp.maximum(jnp.max(attention_scores, axis=3), sink_logit_column)
    raised = jnp.where(allowed[None, None], jnp.exp(attention_scores - largest[..., None]), 0.0)
    sink_raised = jnp.exp(sink_logit_column - largest)
    denominator = jnp.sum(raised, axis=3) + sink_raised
    return (raised / denominator[..., None], sink_raised / denominator)


def head_mix(reduced_probabilities, value_tile_block):
    key_total_count = value_tile_block.shape[0]
    value_head_rows = value_tile_block.reshape(key_total_count, KEY_VALUE_HEADS, HEAD_SIZE)
    mixed_output = jnp.einsum(
        "amlh,hai->lami", reduced_probabilities, value_head_rows, preferred_element_type=jnp.float32
    )
    return mixed_output.reshape(mixed_output.shape[0], QUERY_HEADS * HEAD_SIZE).astype(jnp.bfloat16)


def head_grads(
    probs,
    reduced_probabilities,
    sink_probs,
    query_tile_block,
    key_tile_block,
    value_tile_block,
    mixed_gradient,
):
    query_total_count = query_tile_block.shape[0]
    key_total_count = key_tile_block.shape[0]
    query_head_rows = query_tile_block.reshape(
        query_total_count, KEY_VALUE_HEADS, QUERY_HEADS // KEY_VALUE_HEADS, HEAD_SIZE
    )
    key_head_rows = key_tile_block.reshape(key_total_count, KEY_VALUE_HEADS, HEAD_SIZE)
    value_head_rows = value_tile_block.reshape(key_total_count, KEY_VALUE_HEADS, HEAD_SIZE)
    heads_gradient = mixed_gradient.reshape(
        query_total_count, KEY_VALUE_HEADS, QUERY_HEADS // KEY_VALUE_HEADS, HEAD_SIZE
    )
    probability_gradient = jnp.einsum(
        "baqj,eaj->aqbe", heads_gradient, value_head_rows, preferred_element_type=jnp.float32
    )
    spread = jnp.sum(probs * probability_gradient, axis=3)
    score_gradient = (probs * (probability_gradient - spread[..., None])).astype(jnp.bfloat16)
    head_scaling = HEAD_SIZE ** (-0.5)
    query_gradient = (
        jnp.einsum(
            "amlh,hai->lami", score_gradient, key_head_rows, preferred_element_type=jnp.float32
        )
        * head_scaling
    )
    key_gradient = (
        jnp.einsum(
            "ujko,kujm->oum", score_gradient, query_head_rows, preferred_element_type=jnp.float32
        )
        * head_scaling
    )
    value_gradient = jnp.einsum(
        "ujko,kujm->oum", reduced_probabilities, heads_gradient, preferred_element_type=jnp.float32
    )
    sink_gradient = -jnp.sum(sink_probs * spread, axis=2).reshape(QUERY_HEADS)
    return (
        query_gradient.reshape(query_total_count, QUERY_HEADS * HEAD_SIZE).astype(jnp.bfloat16),
        key_gradient.reshape(key_total_count, KEY_VALUE_HEADS * HEAD_SIZE),
        value_gradient.reshape(key_total_count, KEY_VALUE_HEADS * HEAD_SIZE),
        sink_gradient,
    )


def block_backward(grad_flat, gate_pre, up_pre, gate_full, up_full, down_full):
    grad_act = jnp.dot(grad_flat, down_full, preferred_element_type=jnp.float32)
    grad_gate, grad_up = glu_grads(grad_act, gate_pre, up_pre)
    grad_pair = jnp.concatenate([grad_gate, grad_up], axis=1).astype(jnp.bfloat16)
    weight_pair = jnp.concatenate([gate_full, up_full], axis=1)
    return lax.dot_general(
        grad_pair, weight_pair, CONTRACT_LAST, preferred_element_type=jnp.float32
    ).astype(jnp.bfloat16)


def general_shards(
    queries,
    key_rows,
    value_matrix,
    head_sink_logits,
    residual,
    out_weight,
    norm_gain,
    router,
    expert_gate,
    expert_up,
    expert_down,
    routes,
    group_ids,
    rewards,
    response_mask,
    upstream,
):
    seq_count = lax.axis_size("seq")
    dp_count = lax.axis_size("dp")
    seq_index = lax.axis_index("seq")
    query_rows = queries[0]
    own_keys = key_rows[0]
    own_values = value_matrix[0]
    tokens_here = query_rows.shape[0]
    pieces = seq_count // EW
    group_count = max(dp_count // 4, 1)
    all_tokens = dp_count * seq_count * tokens_here
    group_hot = (group_ids[0] == jnp.arange(group_count, dtype=jnp.int32)).astype(jnp.float32)
    reward = rewards[0].astype(jnp.float32)
    group_terms = (
        group_hot[:, None] * jnp.stack([jnp.ones_like(reward), reward, reward * reward])[None, :]
    )
    mask_wide = response_mask[0].astype(jnp.float32)
    local_count = jnp.sum(mask_wide)
    first_device = (seq_index == 0).astype(jnp.float32)
    group_totals, token_total = lax.psum((group_terms * first_device, local_count), ("seq", "dp"))
    group_sizes = group_totals[:, 0]
    group_means = group_totals[:, 1] / group_sizes
    group_spread = group_totals[:, 2] / group_sizes - group_means * group_means
    own_mean = jnp.sum(group_hot * group_means)
    own_spread = jnp.sum(group_hot * group_spread)
    advantage = (reward - own_mean) / jnp.sqrt(jnp.maximum(own_spread, 1.0))
    token_scale = -advantage * all_tokens / token_total
    loss_weight = token_scale * mask_wide
    halo_keys, halo_values = passed_along((own_keys, own_values), "seq", 1)
    key_tile_block = jnp.concatenate([halo_keys, own_keys], axis=0)
    value_tile_block = jnp.concatenate([halo_values, own_values], axis=0)
    row_index = jnp.arange(tokens_here, dtype=jnp.int32)[:, None]
    col_index = jnp.arange(WINDOW + tokens_here, dtype=jnp.int32)[None, :]
    allowed = (
        (col_index >= row_index + 1)
        & (col_index <= row_index + WINDOW)
        & ((col_index >= WINDOW) | (seq_index > 0))
    )
    probs, sink_probs = head_scores(query_rows, key_tile_block, head_sink_logits, allowed)
    reduced_probabilities = probs.astype(jnp.bfloat16)
    attended = head_mix(reduced_probabilities, value_tile_block)
    out_full = lax.all_gather(out_weight, "dp", axis=0, tiled=True)
    projected = jnp.dot(attended, out_full, preferred_element_type=jnp.float32)
    mid_rows = lax.optimization_barrier(
        (residual[0].astype(jnp.float32) + projected).astype(jnp.bfloat16)
    )
    mid_wide = mid_rows.astype(jnp.float32)
    inv_rms = lax.rsqrt(jnp.mean(mid_wide * mid_wide, axis=1, keepdims=True) + NORM_EPS)
    unit_rows = mid_wide * inv_rms
    normed = (unit_rows * norm_gain[None, :]).astype(jnp.bfloat16)
    logits = jnp.dot(normed, router, preferred_element_type=jnp.float32)
    route_hot = routes[0][:, :, None] == jnp.arange(EXPERTS, dtype=jnp.int32)[None, None, :]
    route_logits = jnp.sum(jnp.where(route_hot, logits[:, None, :], 0.0), axis=2)
    raised = jnp.exp(route_logits)
    route_weights = raised / jnp.sum(raised, axis=1, keepdims=True)
    member = route_hot[:, :, :EW]
    expert_share = jnp.sum(jnp.where(member, route_weights[:, :, None], 0.0), axis=1)
    chosen = jnp.any(member, axis=1)
    slot_rank = jnp.cumsum(chosen.astype(jnp.int32), axis=0) - 1
    slot_hot = chosen[:, :, None] & (
        slot_rank[:, :, None] == jnp.arange(CAP, dtype=jnp.int32)[None, None, :]
    )
    slot_low = slot_hot.astype(jnp.bfloat16)
    slot_wide = slot_hot.astype(jnp.float32)
    slot_rows = jnp.einsum(
        "tec,td->ecd", slot_low, normed, preferred_element_type=jnp.float32
    ).astype(jnp.bfloat16)
    outgoing = jnp.broadcast_to(slot_rows[:, None], (EW, pieces, CAP, D)).reshape(seq_count, CAP, D)
    upstream_slots = jnp.einsum(
        "tec,td->ecd", slot_low, upstream[0], preferred_element_type=jnp.float32
    )
    weight_slots = jnp.einsum("tec,t->ec", slot_wide, loss_weight, precision=HIGHEST)
    share_slots = jnp.einsum("tec,te->ec", slot_wide, expert_share, precision=HIGHEST)
    cot_slots = weight_slots[:, :, None] * upstream_slots
    grad_out = (share_slots[:, :, None] * cot_slots).astype(jnp.bfloat16)
    grad_outgoing = jnp.broadcast_to(grad_out[:, None], (EW, pieces, CAP, D)).reshape(
        seq_count, CAP, D
    )
    gate_full, up_full, down_full = (
        lax.all_gather(expert_gate, "dp", axis=0, tiled=True),
        lax.all_gather(expert_up, "dp", axis=0, tiled=True),
        lax.all_gather(expert_down, "dp", axis=0, tiled=True),
    )
    arrived = lax.all_to_all(outgoing, "seq", split_axis=0, concat_axis=0, tiled=True)
    senders = arrived.shape[0]
    items = arrived.shape[1]
    block_senders = arrived.shape[0]
    block_items = arrived.shape[1]
    flat_rows = arrived.reshape(block_senders * block_items, D)
    gate_pre = jnp.dot(flat_rows, gate_full, preferred_element_type=jnp.float32)
    up_pre = jnp.dot(flat_rows, up_full, preferred_element_type=jnp.float32)
    activation = glu_forward(gate_pre, up_pre)
    partial_out = lax.dot_general(
        activation, down_full, CONTRACT_LAST, preferred_element_type=jnp.float32
    ).astype(jnp.bfloat16)
    partial_out, gate_pre, up_pre = (
        partial_out.reshape(block_senders, block_items, D),
        gate_pre,
        up_pre,
    )
    back_out = lax.all_to_all(partial_out, "seq", split_axis=0, concat_axis=0, tiled=True)
    gate_held = gate_pre.reshape(senders, items, -1)
    up_held = up_pre.reshape(senders, items, -1)
    grad_arrived = lax.all_to_all(grad_outgoing, "seq", split_axis=0, concat_axis=0, tiled=True)
    grad_piece = block_backward(
        grad_arrived.reshape(seq_count * CAP, D),
        gate_held.reshape(seq_count * CAP, -1),
        up_held.reshape(seq_count * CAP, -1),
        gate_full,
        up_full,
        down_full,
    )
    grad_back = lax.all_to_all(
        grad_piece.reshape(seq_count, CAP, D), "seq", split_axis=0, concat_axis=0, tiled=True
    )
    expert_out = jnp.sum(back_out.reshape(EW, pieces, CAP, D).astype(jnp.float32), axis=1)
    grad_share_slots = jnp.sum(cot_slots * expert_out, axis=2)
    grad_rows = jnp.sum(grad_back.reshape(EW, pieces, CAP, D).astype(jnp.float32), axis=1)
    grad_normed_moe = jnp.einsum("tec,ecd->td", slot_wide, grad_rows, precision=HIGHEST)
    grad_share = jnp.einsum("tec,ec->te", slot_wide, grad_share_slots, precision=HIGHEST)
    grad_weights = jnp.sum(jnp.where(member, grad_share[:, None, :], 0.0), axis=2)
    grad_route = route_weights * (
        grad_weights - jnp.sum(route_weights * grad_weights, axis=1, keepdims=True)
    )
    grad_logits = jnp.sum(jnp.where(route_hot, grad_route[:, :, None], 0.0), axis=1).astype(
        jnp.bfloat16
    )
    grad_normed = (
        lax.dot_general(grad_logits, router, CONTRACT_LAST, preferred_element_type=jnp.float32)
        + grad_normed_moe
    )
    grad_unit = grad_normed * norm_gain[None, :]
    grad_mid = loss_weight[:, None] * upstream[0].astype(jnp.float32) + inv_rms * (
        grad_unit - unit_rows * jnp.mean(grad_unit * unit_rows, axis=1, keepdims=True)
    )
    grad_residual = grad_mid.astype(jnp.bfloat16)
    grad_attended = lax.dot_general(
        grad_residual, out_full, CONTRACT_LAST, preferred_element_type=jnp.float32
    ).astype(jnp.bfloat16)
    query_gradient, key_gradient, value_gradient, sink_gradient = head_grads(
        probs,
        reduced_probabilities,
        sink_probs,
        query_rows,
        key_tile_block,
        value_tile_block,
        grad_attended,
    )
    next_keys, next_values = (
        passed_along(key_gradient[:WINDOW].astype(jnp.bfloat16), "seq", -1).astype(jnp.float32),
        passed_along(value_gradient[:WINDOW].astype(jnp.bfloat16), "seq", -1).astype(jnp.float32),
    )
    own_key_grad = key_gradient[WINDOW:]
    own_value_grad = value_gradient[WINDOW:]
    split_at = tokens_here - WINDOW
    grad_key_rows = jnp.concatenate(
        [own_key_grad[:split_at], own_key_grad + next_keys], axis=0
    ).astype(jnp.bfloat16)
    grad_value_rows = jnp.concatenate(
        [own_value_grad[:split_at], own_value_grad + next_values], axis=0
    ).astype(jnp.bfloat16)
    grad_sinks = lax.psum(sink_gradient, ("seq", "dp"))
    return (
        query_gradient[None],
        grad_key_rows[None],
        grad_value_rows[None],
        grad_residual[None],
        grad_sinks,
    )


MESH = pl.DeviceIdType.MESH
MIB = 1 << 20


def halving_place(index, count):
    place, weight, rest = 0, count // 2, index
    while weight:
        place = place + lax.rem(rest, 2) * weight
        rest = lax.div(rest, 2)
        weight //= 2
    return place


def flipped(index, bit):
    return index + bit - 2 * bit * lax.rem(lax.div(index, bit), 2)


def expert_kernel(
    count,
    slots_ref,
    facts_ref,
    gate_ref,
    up_ref,
    down_ref,
    own_ref,
    other_ref,
    theirs,
    outgoing,
    arrived,
    sent,
    total,
    received,
    grads,
    back,
    seq_send,
    seq_recv,
    to_send,
    to_recv,
    halve_send,
    halve_recv,
    double_send,
    double_recv,
    back_send,
    back_recv,
):
    bits = count.bit_length() - 1
    me = lax.axis_index("dp")
    side = lax.axis_index("seq")
    far = 1 - side
    place = halving_place(me, count)
    depth = gate_ref.shape[0]
    hidden = gate_ref.shape[1]
    wide = 3 * hidden // 2

    barrier = pltpu.get_barrier_semaphore()
    pl.semaphore_signal(barrier, inc=1, device_id={"seq": far}, device_id_type=MESH)

    def greet(step, carry):
        pl.semaphore_signal(
            barrier, inc=1, device_id={"dp": lax.rem(me + step, count)}, device_id_type=MESH
        )
        return carry

    lax.fori_loop(1, count, greet, 0)
    pl.semaphore_wait(barrier, count)

    swap = pltpu.make_async_remote_copy(
        src_ref=slots_ref.at[far],
        dst_ref=theirs,
        send_sem=seq_send.at[0],
        recv_sem=seq_recv.at[0],
        device_id={"seq": far},
        device_id_type=MESH,
    )
    swap.start()
    back[...] = jnp.broadcast_to(facts_ref[...], back.shape)
    swap.wait()
    mine = slots_ref[side]
    came = theirs[...]
    first = jnp.where(side == 0, mine, came)
    second = jnp.where(side == 0, came, mine)
    outgoing[...] = jnp.concatenate(
        [first[:, :CAP], second[:, :CAP], first[:, CAP:], second[:, CAP:]], axis=1
    ).astype(jnp.bfloat16)

    def slice_copy(step):
        to = lax.rem(me + step, count)
        return pltpu.make_async_remote_copy(
            src_ref=outgoing.at[to],
            dst_ref=arrived.at[place],
            send_sem=to_send.at[step],
            recv_sem=to_recv.at[step],
            device_id={"dp": to},
            device_id_type=MESH,
        )

    def start_slice(step, carry):
        slice_copy(step).start()
        return carry

    def wait_slice(step, carry):
        slice_copy(step).wait()
        return carry

    lax.fori_loop(1, count, start_slice, 0)
    arrived[place] = outgoing[me]
    lax.fori_loop(1, count, wait_slice, 0)

    half = count // 2
    rows = EW * CAP
    tile = 512

    def products(start):
        block = arrived[pl.ds(start, half)].astype(jnp.float32)
        normed = block[:, :rows].reshape(half * rows, -1)[:, :depth].astype(jnp.bfloat16)
        upstream = block[:, rows:].reshape(half * rows, -1)[:, :depth].astype(jnp.bfloat16)

        def product(column):
            which, at = divmod(column, hidden)
            weight = (gate_ref, up_ref, down_ref)[which]
            return jnp.dot(
                upstream if which == 2 else normed,
                weight[:, at : at + tile],
                preferred_element_type=jnp.float32,
            ).reshape(half, rows, tile)

        def tile_at(column):
            return jnp.concatenate([product(column), product(wide + column)], axis=1)

        return tile_at

    def halve_copy(stage, chunk):
        at = pl.ds(chunk * width, width)
        return pltpu.make_async_remote_copy(
            src_ref=sent[stage].at[:, :, at],
            dst_ref=received[stage].at[:, :, at],
            send_sem=halve_send.at[stage, chunk],
            recv_sem=halve_recv.at[stage, chunk],
            device_id={"dp": flipped(me, 1 << stage)},
            device_id_type=MESH,
        )

    width = hidden // 2
    chunks = wide // width
    bit_of = [lax.rem(lax.div(me, 1 << stage), 2) for stage in range(bits)]
    tile_at = products((1 - bit_of[0]) * half)
    for chunk in range(chunks):
        for column in range(chunk * width, (chunk + 1) * width, tile):
            sent[0][:, :, column : column + tile] = tile_at(column).astype(jnp.bfloat16)
        halve_copy(0, chunk).start()
    tile_at = products(bit_of[0] * half)
    for column in range(0, wide, tile):
        total[:, :, column : column + tile] = tile_at(column)
    base = 0
    for stage in range(1, bits):
        blocks = half >> stage
        away = (1 - bit_of[stage]) * blocks
        keep = bit_of[stage] * blocks
        for chunk in range(chunks):
            at = slice(chunk * width, (chunk + 1) * width)
            halve_copy(stage - 1, chunk).wait()
            sent[stage][:, :, at] = (
                total[pl.ds(base + away, blocks), :, at]
                + received[stage - 1][pl.ds(away, blocks), :, at].astype(jnp.float32)
            ).astype(jnp.bfloat16)
            halve_copy(stage, chunk).start()
            total[pl.ds(base + keep, blocks), :, at] += received[stage - 1][
                pl.ds(keep, blocks), :, at
            ].astype(jnp.float32)
        base = base + keep
    for chunk in range(chunks):
        halve_copy(bits - 1, chunk).wait()
    summed = total[base] + received[bits - 1][0].astype(jnp.float32)

    gate_pre = summed[:rows, :hidden]
    up_pre = jnp.concatenate([summed[:rows, hidden:], summed[rows:, : hidden // 2]], axis=1)
    grad_act = summed[rows:, hidden // 2 :]
    sigmoid_gate = 1.0 / (1.0 + jnp.exp(-GLU_SLOPE * gate_pre))
    gate_sigmoid = gate_pre * sigmoid_gate
    raised_up = up_pre + 1.0
    activation = (raised_up * gate_sigmoid).astype(jnp.bfloat16).astype(jnp.float32)
    share = jnp.sum(activation * grad_act, axis=1, keepdims=True)
    grad_up = grad_act * gate_sigmoid
    grad_gate = (
        grad_act * raised_up * (sigmoid_gate + GLU_SLOPE * gate_sigmoid * (1.0 - sigmoid_gate))
    )
    grads[place] = jnp.concatenate([grad_gate, grad_up], axis=0).astype(jnp.bfloat16)

    def double_copy(stage, chunk):
        blocks = 1 << stage
        part = grads.at[pl.ds(place // blocks * blocks, blocks), :, pl.ds(chunk * width, width)]
        return pltpu.make_async_remote_copy(
            src_ref=part,
            dst_ref=part,
            send_sem=double_send.at[stage, chunk],
            recv_sem=double_recv.at[stage, chunk],
            device_id={"dp": flipped(me, half >> stage)},
            device_id_type=MESH,
        )

    for stage in range(bits):
        for chunk in range(2):
            if stage:
                double_copy(stage - 1, chunk).wait()
            double_copy(stage, chunk).start()

    contract = (((1,), (1,)), ((), ()))
    from_gate = jnp.zeros((count * 2 * rows, depth), jnp.float32)
    from_up = jnp.zeros((count * 2 * rows, depth), jnp.float32)
    for chunk in range(2):
        double_copy(bits - 1, chunk).wait()
        at = slice(chunk * width, (chunk + 1) * width)
        flat = grads[:, :, at].reshape(count * 2 * rows, width)
        from_gate += lax.dot_general(
            flat, gate_ref[:, at], contract, preferred_element_type=jnp.float32
        )
        from_up += lax.dot_general(flat, up_ref[:, at], contract, preferred_element_type=jnp.float32)
    from_gate = from_gate.reshape(count, 2 * rows, depth)
    from_up = from_up.reshape(count, 2 * rows, depth)
    back[:, :, :depth] = from_gate[:, :rows] + from_up[:, rows:]

    def back_copy(step):
        to = lax.rem(me + step, count)
        return pltpu.make_async_remote_copy(
            src_ref=back.at[halving_place(to, count)],
            dst_ref=own_ref.at[me],
            send_sem=back_send.at[step],
            recv_sem=back_recv.at[step],
            device_id={"dp": to},
            device_id_type=MESH,
        )

    def start_back(step, carry):
        back_copy(step).start()
        return carry

    def wait_back(step, carry):
        back_copy(step).wait()
        return carry

    lax.fori_loop(1, count, start_back, 0)
    own_ref[me] = back[place]
    own_ref[count] = jnp.broadcast_to(share, own_ref.shape[1:])
    lax.fori_loop(1, count, wait_back, 0)
    last = pltpu.make_async_remote_copy(
        src_ref=own_ref,
        dst_ref=other_ref,
        send_sem=seq_send.at[1],
        recv_sem=seq_recv.at[1],
        device_id={"seq": far},
        device_id_type=MESH,
    )
    last.start()
    last.wait()


def in_place_experts(slots, facts, gate, up, down):
    count, lanes = slots.shape[1], slots.shape[3]
    bits = count.bit_length() - 1
    rows = EW * CAP
    hidden = gate.shape[1]
    wide = 3 * hidden // 2
    stages = [pltpu.VMEM((count >> (stage + 1), 2 * rows, wide), jnp.bfloat16) for stage in range(bits)]
    vmem = pl.BlockSpec(memory_space=pltpu.VMEM)
    dma = pltpu.SemaphoreType.DMA
    result = jax.ShapeDtypeStruct((count + 1, rows, lanes), jnp.float32)
    return pl.pallas_call(
        functools.partial(expert_kernel, count),
        out_shape=(result, result),
        in_specs=[vmem] * 5,
        out_specs=(vmem, vmem),
        scratch_shapes=[
            pltpu.VMEM((count, rows, lanes), jnp.float32),
            pltpu.VMEM((count, 2 * rows, lanes), jnp.bfloat16),
            pltpu.VMEM((count, 2 * rows, lanes), jnp.bfloat16),
            stages,
            pltpu.VMEM((count // 2, 2 * rows, wide), jnp.float32),
            stages,
            pltpu.VMEM((count, 2 * rows, hidden), jnp.bfloat16),
            pltpu.VMEM((count, rows, lanes), jnp.float32),
            dma((2,)),
            dma((2,)),
            dma((count,)),
            dma((count,)),
            dma((bits, 3)),
            dma((bits, 3)),
            dma((bits, 2)),
            dma((bits, 2)),
            dma((count,)),
            dma((count,)),
        ],
        compiler_params=pltpu.CompilerParams(
            collective_id=1, has_side_effects=True, vmem_limit_bytes=40 * MIB
        ),
        name="expert_kernel",
    )(slots, facts, gate, up, down)


def attend(
    group, side, queries_ref, key_block, value_block, sinks_ref, attended_ref, probs_ref, sink_probs_ref
):
    tokens = queries_ref.shape[0]
    span = 2 * tokens
    shared_heads = QUERY_HEADS // KEY_VALUE_HEADS
    stacked = (tokens, span)
    row = lax.broadcasted_iota(jnp.int32, stacked, 0)
    col = lax.broadcasted_iota(jnp.int32, stacked, 1)
    allowed = (col >= row + 1) & (col <= row + tokens) & (col + side * tokens >= tokens)
    lanes = slice(group * HEAD_SIZE, (group + 1) * HEAD_SIZE)
    group_keys = key_block[:, :, lanes].reshape(span, HEAD_SIZE)
    group_values = value_block[:, :, lanes].reshape(span, HEAD_SIZE)
    mixed = []
    for head in range(group * shared_heads, (group + 1) * shared_heads):
        scores = lax.dot_general(
            queries_ref[:, head * HEAD_SIZE : (head + 1) * HEAD_SIZE],
            group_keys,
            (((1,), (1,)), ((), ())),
            preferred_element_type=jnp.float32,
        )
        scores = jnp.where(allowed, scores * HEAD_SIZE ** (-0.5), -1e30)
        sink = sinks_ref[head : head + 1, :1]
        largest = jnp.maximum(jnp.max(scores, axis=1, keepdims=True), sink)
        raised = jnp.where(allowed, jnp.exp(scores - largest), 0.0)
        sink_raised = jnp.exp(sink - largest)
        denominator = jnp.sum(raised, axis=1, keepdims=True) + sink_raised
        probs = raised / denominator
        probs_ref[head] = probs
        sink_probs_ref[head] = sink_raised / denominator
        mixed.append(
            jnp.dot(
                probs.astype(jnp.bfloat16), group_values, preferred_element_type=jnp.float32
            )
        )
        if len(mixed) * HEAD_SIZE == 128:
            end = (head + 1) * HEAD_SIZE
            attended_ref[:, end - 128 : end] = jnp.concatenate(mixed, axis=1).astype(
                jnp.bfloat16
            )
            mixed = []


def gather_kernel(
    count,
    weight_ref,
    queries_ref,
    keys_ref,
    values_ref,
    sinks_ref,
    full_ref,
    attended_ref,
    probs_out,
    sink_probs_out,
    key_block,
    value_block,
    probs_ref,
    sink_probs_ref,
    save_sem,
    halo_send,
    halo_recv,
    own_sem,
    line_send,
    line_recv,
    pair_send,
    pair_recv,
    side_send,
    side_recv,
    core_send,
    core_recv,
):
    line = count // 4
    waves = line - 1
    me = lax.axis_index("dp")
    side = lax.axis_index("seq")
    core, pair, spot = lax.rem(me, 2), lax.rem(lax.div(me, 2), 2), lax.div(me, 4)
    rows = weight_ref.shape[0]
    lone = rows * 3 // 128 * 16
    shared = rows - 2 * lone
    lone_start = pl.multiple_of(side * (lone + shared), 16)
    plane_start = pl.multiple_of(side * lone, 16)
    far_start = pl.multiple_of((1 - side) * (lone + shared), 16)
    chunks = ((lone_start, lone), (lone, shared))

    def index(spot, pair, core):
        return (spot * 2 + pair) * 2 + core

    def part(owner, start, size, own=False):
        if own:
            return weight_ref.at[pl.ds(start, size)]
        return full_ref.at[owner, pl.ds(start, size)]

    def remote(owner, own, start, size, send, recv, target):
        return pltpu.make_async_remote_copy(
            src_ref=part(owner, start, size, own),
            dst_ref=part(owner, start, size),
            send_sem=send,
            recv_sem=recv,
            device_id=target,
            device_id_type=MESH,
        )

    def shard_spot(way, wave):
        return spot - 1 - wave if way == 0 else spot + 1 + wave

    def arrives(way, wave):
        return spot - 1 - wave >= 0 if way == 0 else spot + 1 + wave < line

    def leaves(way, wave):
        if way == 0:
            return (spot + 1 < line) & (spot - wave >= 0)
        return (spot >= 1) & (spot + wave < line)

    def line_copy(way, wave, chunk):
        step = 1 if way == 0 else -1
        owner = index(spot - step * wave, pair, core)
        return remote(
            owner,
            wave == 0,
            *chunks[chunk],
            line_send.at[way, wave, chunk],
            line_recv.at[way, wave, chunk],
            {"dp": index(spot + step, pair, core)},
        )

    def slot(piece):
        return 0 if piece is None else 1 + 2 * piece[1] + piece[0]

    def owner_of(piece, other_pair):
        at = spot if piece is None else shard_spot(*piece)
        return index(at, 1 - pair if other_pair else pair, core)

    def pair_copy(piece, chunk):
        at = slot(piece)
        return remote(
            owner_of(piece, False),
            piece is None,
            *chunks[chunk],
            pair_send.at[at, chunk],
            pair_recv.at[at, chunk],
            {"dp": index(spot, 1 - pair, core)},
        )

    def side_copy(piece, other_pair):
        at = slot(piece)
        return remote(
            owner_of(piece, other_pair),
            False,
            lone_start,
            lone,
            side_send.at[other_pair, at],
            side_recv.at[other_pair, at],
            {"seq": 1 - side},
        )

    def core_copy(piece, other_pair, from_side):
        at = slot(piece)
        if piece is None and other_pair == 0:
            start, size = 0, rows
        elif from_side:
            start, size = far_start, lone
        else:
            start, size = plane_start, lone + shared
        return remote(
            owner_of(piece, other_pair),
            piece is None and other_pair == 0,
            start,
            size,
            core_send.at[from_side, other_pair, at],
            core_recv.at[from_side, other_pair, at],
            {"dp": index(spot, pair, 1 - core)},
        )

    def held(piece, action):
        if piece is None:
            action()
        else:
            pl.when(arrives(*piece))(action)

    barrier = pltpu.get_barrier_semaphore()

    def greet(target):
        pl.semaphore_signal(barrier, inc=1, device_id=target, device_id_type=MESH)

    greet({"seq": 1 - side})
    greet({"dp": index(spot, 1 - pair, core)})
    greet({"dp": index(spot, pair, 1 - core)})
    for way, step in ((0, 1), (1, -1)):

        @pl.when(leaves(way, 0))
        def _(step=step):
            greet({"dp": index(spot + step, pair, core)})

    neighbours = leaves(0, 0).astype(jnp.int32) + leaves(1, 0).astype(jnp.int32)
    pl.semaphore_wait(barrier, 3 + neighbours)

    keep = pltpu.make_async_copy(weight_ref, full_ref.at[me], own_sem)
    for chunk in (0, 1):
        for way in (0, 1):

            @pl.when(leaves(way, 0))
            def _(way=way, chunk=chunk):
                line_copy(way, 0, chunk).start()

        pair_copy(None, chunk).start()
    core_copy(None, 0, 0).start()
    keep.start()
    halos = [
        pltpu.make_async_remote_copy(
            src_ref=source,
            dst_ref=block.at[0],
            send_sem=halo_send.at[at],
            recv_sem=halo_recv.at[at],
            device_id={"seq": 1 - side},
            device_id_type=MESH,
        )
        for at, (source, block) in enumerate(((keys_ref, key_block), (values_ref, value_block)))
    ]
    for halo in halos:
        halo.start()
    key_block[1] = keys_ref[...]
    value_block[1] = values_ref[...]
    for halo in halos:
        halo.wait()

    def attend_group(group):
        attend(
            group,
            side,
            queries_ref,
            key_block,
            value_block,
            sinks_ref,
            attended_ref,
            probs_ref,
            sink_probs_ref,
        )

        for copy in saves(group):
            copy.start()

    def saves(group):
        shared_heads = QUERY_HEADS // KEY_VALUE_HEADS
        heads = pl.ds(group * shared_heads, shared_heads)
        pairs = ((probs_ref, probs_out), (sink_probs_ref, sink_probs_out))
        return [
            pltpu.make_async_copy(held_ref.at[heads], out.at[heads], save_sem.at[at, group])
            for at, (held_ref, out) in enumerate(pairs)
        ]

    groups = list(range(KEY_VALUE_HEADS))
    attend_group(groups.pop())

    def line_step(wave):
        for chunk in (0, 1):
            for way in (0, 1):

                @pl.when(arrives(way, wave))
                def _(way=way, chunk=chunk):
                    piece = (way, wave)
                    line_copy(way, wave, chunk).wait_recv()
                    if wave + 1 < waves:

                        @pl.when(leaves(way, wave + 1))
                        def _():
                            line_copy(way, wave + 1, chunk).start()

                    pair_copy(piece, chunk).start()
                    if chunk == 0:
                        side_copy(piece, 0).start()
                    else:
                        core_copy(piece, 0, 0).start()

    def pair_step(pieces):
        for chunk in (0, 1):
            for piece in pieces:

                def arrive(piece=piece, chunk=chunk):
                    pair_copy(piece, chunk).wait_recv()
                    if chunk == 0:
                        side_copy(piece, 1).start()
                    else:
                        core_copy(piece, 1, 0).start()

                held(piece, arrive)

    def side_step(pieces, other_pair):
        for piece in pieces:

            def arrive(piece=piece):
                side_copy(piece, other_pair).wait_recv()
                core_copy(piece, other_pair, 1).start()

            held(piece, arrive)

    waved = [[(0, wave), (1, wave)] for wave in range(waves)]
    ordered = [[None]] + waved
    for wave in range(waves):
        line_step(wave)
        if groups:
            attend_group(groups.pop())
        pair_step(ordered[wave])
        if groups:
            attend_group(groups.pop())
        if wave:
            side_step(waved[wave - 1], 0)
            side_step(ordered[wave - 1], 1)
    for group in groups:
        attend_group(group)
    pair_step(ordered[waves])
    side_step(waved[waves - 1], 0)
    side_step(ordered[waves - 1], 1)
    side_step(ordered[waves], 1)

    keep.wait()
    for group in range(KEY_VALUE_HEADS):
        for copy in saves(group):
            copy.wait()
    for piece in [None] + sum(waved, []):

        def finish(piece=piece):
            for chunk in (0, 1):
                pair_copy(piece, chunk).wait_send()
            for other_pair in (0, 1):
                core_copy(piece, other_pair, 0).wait()
                if piece is not None or other_pair:
                    side_copy(piece, other_pair).wait_send()
                    core_copy(piece, other_pair, 1).wait()

        held(piece, finish)
    for wave in range(waves):
        for way in (0, 1):

            @pl.when(leaves(way, wave))
            def _(way=way, wave=wave):
                for chunk in (0, 1):
                    line_copy(way, wave, chunk).wait_send()


def gather_and_attend(weight, queries, keys, values, sinks, count):
    waves = count // 4 - 1
    slots = 1 + 2 * waves
    dma = pltpu.SemaphoreType.DMA
    hbm = pl.BlockSpec(memory_space=pl.ANY)
    vmem = pl.BlockSpec(memory_space=pltpu.VMEM)
    tokens = queries.shape[0]
    sink_rows = jnp.broadcast_to(sinks[:, None], (QUERY_HEADS, 128))
    full, attended, probs, sink_probs, key_block, value_block = pl.pallas_call(
        functools.partial(gather_kernel, count),
        out_shape=(
            jax.ShapeDtypeStruct((count,) + weight.shape, weight.dtype),
            jax.ShapeDtypeStruct(queries.shape, jnp.bfloat16),
            jax.ShapeDtypeStruct((QUERY_HEADS, tokens, 2 * tokens), jnp.float32),
            jax.ShapeDtypeStruct((QUERY_HEADS, tokens, 1), jnp.float32),
            jax.ShapeDtypeStruct((2,) + keys.shape, keys.dtype),
            jax.ShapeDtypeStruct((2,) + values.shape, values.dtype),
        ),
        in_specs=[vmem] * 5,
        out_specs=(hbm, vmem, hbm, hbm, vmem, vmem),
        scratch_shapes=[
            pltpu.VMEM((QUERY_HEADS, tokens, 2 * tokens), jnp.float32),
            pltpu.VMEM((QUERY_HEADS, tokens, 1), jnp.float32),
            dma((2, KEY_VALUE_HEADS)),
            dma((2,)),
            dma((2,)),
            dma,
            dma((2, waves, 2)),
            dma((2, waves, 2)),
            dma((slots, 2)),
            dma((slots, 2)),
            dma((2, slots)),
            dma((2, slots)),
            dma((2, 2, slots)),
            dma((2, 2, slots)),
        ],
        compiler_params=pltpu.CompilerParams(
            collective_id=2, has_side_effects=True, vmem_limit_bytes=40 * MIB
        ),
        name="gather_kernel",
    )(weight, queries, keys, values, sink_rows)
    full = full.reshape(count * weight.shape[0], weight.shape[1])
    return full, attended, probs, sink_probs, key_block, value_block


def tail_kernel(
    count,
    queries_ref,
    key_block,
    value_block,
    probs_ref,
    sink_probs_ref,
    mixed_ref,
    grad_queries_ref,
    grad_keys_ref,
    grad_values_ref,
    sums_ref,
    score_grads,
    outgoing,
    came,
    sinks,
    parts,
    half,
    far_half,
    dp_send,
    dp_recv,
    seq_send,
    seq_recv,
):
    me = lax.axis_index("dp")
    side = lax.axis_index("seq")
    far = 1 - side
    barrier = pltpu.get_barrier_semaphore()
    pl.semaphore_signal(barrier, inc=1, device_id={"seq": far}, device_id_type=MESH)

    def greet(step, carry):
        pl.semaphore_signal(
            barrier, inc=1, device_id={"dp": lax.rem(me + step, count)}, device_id_type=MESH
        )
        return carry

    lax.fori_loop(1, count, greet, 0)

    tokens = queries_ref.shape[0]
    span = 2 * tokens
    shared_heads = QUERY_HEADS // KEY_VALUE_HEADS
    scaling = HEAD_SIZE ** (-0.5)
    contract_last = (((1,), (1,)), ((), ()))
    contract_first = (((0,), (0,)), ((), ()))

    def lanes(head):
        return slice(head * HEAD_SIZE, (head + 1) * HEAD_SIZE)

    own_keys, own_values = [], []
    for group in range(KEY_VALUE_HEADS):
        group_values = value_block[:, :, lanes(group)].reshape(span, HEAD_SIZE)
        key_grad = jnp.zeros((span, HEAD_SIZE), jnp.float32)
        value_grad = jnp.zeros((span, HEAD_SIZE), jnp.float32)
        for head in range(group * shared_heads, (group + 1) * shared_heads):
            mixed = mixed_ref[:, lanes(head)]
            probs = probs_ref[head]
            prob_grad = lax.dot_general(
                mixed, group_values, contract_last, preferred_element_type=jnp.float32
            )
            spread = jnp.sum(probs * prob_grad, axis=1, keepdims=True)
            sinks[head : head + 1] = jnp.broadcast_to(
                -jnp.sum(sink_probs_ref[head] * spread, axis=0, keepdims=True), (1, 128)
            )
            score_grad = (probs * (prob_grad - spread)).astype(jnp.bfloat16)
            score_grads[head] = score_grad
            key_grad += lax.dot_general(
                score_grad,
                queries_ref[:, lanes(head)],
                contract_first,
                preferred_element_type=jnp.float32,
            )
            value_grad += lax.dot_general(
                probs.astype(jnp.bfloat16),
                mixed,
                contract_first,
                preferred_element_type=jnp.float32,
            )
        own_keys.append(key_grad * scaling)
        own_values.append(value_grad)
    key_grad = jnp.concatenate(own_keys, axis=1)
    value_grad = jnp.concatenate(own_values, axis=1)
    outgoing[0] = key_grad[:tokens].astype(jnp.bfloat16)
    outgoing[1] = value_grad[:tokens].astype(jnp.bfloat16)

    pl.semaphore_wait(barrier, count)

    def across(source, target, at):
        return pltpu.make_async_remote_copy(
            src_ref=source,
            dst_ref=target,
            send_sem=seq_send.at[at],
            recv_sem=seq_recv.at[at],
            device_id={"seq": far},
            device_id_type=MESH,
        )

    def part_copy(step):
        return pltpu.make_async_remote_copy(
            src_ref=sinks,
            dst_ref=parts.at[me],
            send_sem=dp_send.at[step],
            recv_sem=dp_recv.at[step],
            device_id={"dp": lax.rem(me + step, count)},
            device_id_type=MESH,
        )

    def start_part(step, carry):
        part_copy(step).start()
        return carry

    def wait_part(step, carry):
        part_copy(step).wait()
        return carry

    halo = across(outgoing, came, 0)
    halo.start()
    lax.fori_loop(1, count, start_part, 0)
    parts[me] = sinks[...]

    def query_grads(group):
        group_keys = key_block[:, :, lanes(group)].reshape(span, HEAD_SIZE)
        pieces = []
        for head in range(group * shared_heads, (group + 1) * shared_heads):
            pieces.append(
                jnp.dot(score_grads[head], group_keys, preferred_element_type=jnp.float32) * scaling
            )
        start = group * shared_heads * HEAD_SIZE
        grad_queries_ref[:, start : start + shared_heads * HEAD_SIZE] = jnp.concatenate(
            pieces, axis=1
        ).astype(jnp.bfloat16)

    early = KEY_VALUE_HEADS // 2
    for group in range(early):
        query_grads(group)
    lax.fori_loop(1, count, wait_part, 0)
    half[...] = jnp.sum(parts[...], axis=0)
    swap = across(half, far_half, 1)
    swap.start()
    for group in range(early, KEY_VALUE_HEADS):
        query_grads(group)
    halo.wait()
    taken = jnp.where(side == 0, came[...].astype(jnp.float32), 0.0)
    grad_keys_ref[...] = (key_grad[tokens:] + taken[0]).astype(jnp.bfloat16)
    grad_values_ref[...] = (value_grad[tokens:] + taken[1]).astype(jnp.bfloat16)
    swap.wait()
    sums_ref[...] = half[...] + far_half[...]


def attention_backward(queries, key_block, value_block, probs, sink_probs, mixed, count):
    vmem = pl.BlockSpec(memory_space=pltpu.VMEM)
    dma = pltpu.SemaphoreType.DMA
    tile = (QUERY_HEADS, 128)
    rows = jax.ShapeDtypeStruct(key_block.shape[1:], jnp.bfloat16)
    grad_queries, grad_keys, grad_values, sums = pl.pallas_call(
        functools.partial(tail_kernel, count),
        out_shape=(
            jax.ShapeDtypeStruct(queries.shape, jnp.bfloat16),
            rows,
            rows,
            jax.ShapeDtypeStruct(tile, jnp.float32),
        ),
        in_specs=[vmem] * 6,
        out_specs=(vmem,) * 4,
        scratch_shapes=[
            pltpu.VMEM(probs.shape, jnp.bfloat16),
            pltpu.VMEM(key_block.shape, jnp.bfloat16),
            pltpu.VMEM(key_block.shape, jnp.bfloat16),
            pltpu.VMEM(tile, jnp.float32),
            pltpu.VMEM((count,) + tile, jnp.float32),
            pltpu.VMEM(tile, jnp.float32),
            pltpu.VMEM(tile, jnp.float32),
            dma((count,)),
            dma((count,)),
            dma((2,)),
            dma((2,)),
        ],
        compiler_params=pltpu.CompilerParams(
            collective_id=3, has_side_effects=True, vmem_limit_bytes=40 * MIB
        ),
        name="tail_kernel",
    )(queries, key_block, value_block, probs, sink_probs, mixed)
    return grad_queries, grad_keys, grad_values, sums[:, 0]


def shards(
    queries,
    key_rows,
    value_matrix,
    head_sink_logits,
    residual,
    out_weight,
    norm_gain,
    router,
    expert_gate,
    expert_up,
    expert_down,
    routes,
    group_ids,
    rewards,
    response_mask,
    upstream,
):
    seq_count = lax.axis_size("seq")
    dp_count = lax.axis_size("dp")
    seq_index = lax.axis_index("seq")
    query_rows = queries[0]
    own_keys = key_rows[0]
    own_values = value_matrix[0]
    tokens_here = query_rows.shape[0]
    group_count = max(dp_count // 4, 1)
    all_tokens = dp_count * seq_count * tokens_here
    group_hot = (group_ids[0] == jnp.arange(group_count, dtype=jnp.int32)).astype(jnp.float32)
    reward = rewards[0].astype(jnp.float32)
    group_terms = (
        group_hot[:, None] * jnp.stack([jnp.ones_like(reward), reward, reward * reward])[None, :]
    )
    mask_wide = response_mask[0].astype(jnp.float32)
    local_count = jnp.sum(mask_wide)
    first_device = (seq_index == 0).astype(jnp.float32)
    out_full, attended, probs, sink_probs, key_block, value_block = gather_and_attend(
        out_weight, query_rows, own_keys, own_values, head_sink_logits, dp_count
    )
    projected = jnp.dot(attended, out_full, preferred_element_type=jnp.float32)
    mid_rows = lax.optimization_barrier(
        (residual[0].astype(jnp.float32) + projected).astype(jnp.bfloat16)
    )
    mid_wide = mid_rows.astype(jnp.float32)
    inv_rms = lax.rsqrt(jnp.mean(mid_wide * mid_wide, axis=1, keepdims=True) + NORM_EPS)
    unit_rows = mid_wide * inv_rms
    normed = (unit_rows * norm_gain[None, :]).astype(jnp.bfloat16)
    logits = jnp.dot(normed, router, preferred_element_type=jnp.float32)
    route_hot = routes[0][:, :, None] == jnp.arange(EXPERTS, dtype=jnp.int32)[None, None, :]
    route_logits = jnp.sum(jnp.where(route_hot, logits[:, None, :], 0.0), axis=2)
    raised = jnp.exp(route_logits)
    route_weights = raised / jnp.sum(raised, axis=1, keepdims=True)
    member = route_hot[:, :, :EW]
    expert_share = jnp.sum(jnp.where(member, route_weights[:, :, None], 0.0), axis=1)
    chosen = jnp.any(member, axis=1)
    slot_rank = jnp.cumsum(chosen.astype(jnp.int32), axis=0) - 1
    slot_hot = chosen[:, :, None] & (
        slot_rank[:, :, None] == jnp.arange(CAP, dtype=jnp.int32)[None, None, :]
    )
    slot_low = slot_hot.astype(jnp.bfloat16)
    slot_wide = slot_hot.astype(jnp.float32)
    slot_rows = jnp.einsum(
        "tec,td->ecd", slot_low, normed, preferred_element_type=jnp.float32
    )
    share_slots = jnp.einsum("tec,te->ec", slot_wide, expert_share, precision=HIGHEST)
    upstream_slots = jnp.einsum(
        "tec,td->ecd", slot_low, upstream[0], preferred_element_type=jnp.float32
    )
    depth = expert_gate.shape[0]
    lanes = -(-depth // 128) * 128
    slots = jnp.concatenate([slot_rows, upstream_slots], axis=1)
    slots = slots.reshape(EW, 2 * CAP, dp_count, depth).transpose(0, 2, 1, 3)
    facts = jnp.concatenate([(group_terms * first_device).reshape(-1), local_count[None]])
    lanes = max(lanes, -(-(depth + facts.shape[0]) // 128) * 128)
    slots = jnp.pad(slots, ((0, 0), (0, 0), (0, 0), (0, lanes - depth)))
    facts = jnp.pad(facts, (depth, lanes - depth - facts.shape[0]))
    facts = jnp.broadcast_to(facts, (EW * CAP, lanes))
    own_part, other_part = in_place_experts(slots, facts, expert_gate, expert_up, expert_down)
    totals = jnp.sum(own_part[:dp_count, 0] + other_part[:dp_count, 0], axis=0)[depth:]
    group_totals = totals[: group_terms.size].reshape(group_terms.shape)
    token_total = totals[group_terms.size]
    group_sizes = group_totals[:, 0]
    group_means = group_totals[:, 1] / group_sizes
    group_spread = group_totals[:, 2] / group_sizes - group_means * group_means
    own_mean = jnp.sum(group_hot * group_means)
    own_spread = jnp.sum(group_hot * group_spread)
    advantage = (reward - own_mean) / jnp.sqrt(jnp.maximum(own_spread, 1.0))
    token_scale = -advantage * all_tokens / token_total
    loss_weight = token_scale * mask_wide
    weight_slots = jnp.einsum("tec,t->ec", slot_wide, loss_weight, precision=HIGHEST)
    both_parts = jnp.where(
        seq_index == 0, jnp.stack([own_part, other_part]), jnp.stack([other_part, own_part])
    )
    both_parts = lax.dynamic_slice_in_dim(both_parts, seq_index * CAP, CAP, 2)
    grad_share_slots = weight_slots * both_parts[:, dp_count, :, 0]
    grad_rows = (
        both_parts[:, :dp_count, :, :depth].transpose(0, 2, 1, 3).reshape(EW, CAP, D)
        * (weight_slots * share_slots)[:, :, None]
    )
    grad_normed_moe = jnp.einsum("tec,ecd->td", slot_wide, grad_rows, precision=HIGHEST)
    grad_share = jnp.einsum("tec,ec->te", slot_wide, grad_share_slots, precision=HIGHEST)
    grad_weights = jnp.sum(jnp.where(member, grad_share[:, None, :], 0.0), axis=2)
    grad_route = route_weights * (
        grad_weights - jnp.sum(route_weights * grad_weights, axis=1, keepdims=True)
    )
    grad_logits = jnp.sum(jnp.where(route_hot, grad_route[:, :, None], 0.0), axis=1).astype(
        jnp.bfloat16
    )
    grad_normed = (
        lax.dot_general(grad_logits, router, CONTRACT_LAST, preferred_element_type=jnp.float32)
        + grad_normed_moe
    )
    grad_unit = grad_normed * norm_gain[None, :]
    grad_mid = loss_weight[:, None] * upstream[0].astype(jnp.float32) + inv_rms * (
        grad_unit - unit_rows * jnp.mean(grad_unit * unit_rows, axis=1, keepdims=True)
    )
    grad_residual = grad_mid.astype(jnp.bfloat16)
    grad_attended = lax.dot_general(
        grad_residual, out_full, CONTRACT_LAST, preferred_element_type=jnp.float32
    ).astype(jnp.bfloat16)
    grad_queries, grad_keys, grad_values, grad_sinks = attention_backward(
        query_rows, key_block, value_block, probs, sink_probs, grad_attended, dp_count
    )
    return (
        grad_queries[None],
        grad_keys[None],
        grad_values[None],
        grad_residual[None],
        grad_sinks,
    )


def solution(mesh):
    seq_count, dp_count = mesh.shape["seq"], mesh.shape["dp"]
    in_place = seq_count == EW and dp_count >= 8 and dp_count & (dp_count - 1) == 0
    return jax.shard_map(
        shards if in_place else general_shards,
        mesh=mesh,
        in_specs=(
            P("dp", "seq", None),
            P("dp", "seq", None),
            P("dp", "seq", None),
            P(),
            P("dp", "seq", None),
            P("dp", None),
            P(),
            P(),
            P("dp", "seq"),
            P("dp", "seq"),
            P("dp", "seq"),
            P("dp", "seq", None),
            P("dp"),
            P("dp"),
            P("dp", "seq"),
            P("dp", "seq", None),
        ),
        out_specs=(
            P("dp", "seq", None),
            P("dp", "seq", None),
            P("dp", "seq", None),
            P("dp", "seq", None),
            P(),
        ),
        check_vma=False,
    )
```
